32 devices in a mesh: row: 8 (over z, y), col: 4 (over x, core).
Axes of the slice: x: 2, y: 2, z: 4, core: 2. Of those that a mesh axis runs over, the one named last changes fastest.
Arguments:
- pair: bfloat16 [2, 512, 512, 128], P(None, 'row', 'col'), may hold values from -6 to 6
- cotangent: bfloat16 [2, 512, 512, 128], P(None, 'row', 'col'), may hold values from -6 to 6
- segments: int32 [2, 512], replicated, may hold values from 0 to 3, never falling along the last dimension, each value on 1 to 256 neighbouring positions
- lengths: int32 [2], replicated, may hold values from 1 to 512, 768 in all
- weights: float32 [5, 16384], P(None, 'row')
- moment_one: float32 [5, 16384], P(None, 'row'), may hold values from -24 to 24
- moment_two: float32 [5, 16384], P(None, 'row'), may hold values from 1.31072 to 5.24288
- gain: float32 [128], replicated, may hold values from 0.5 to 1.5
- gain_m: float32 [128], replicated, may hold values from -512 to 512
- gain_v: float32 [128], replicated, may hold values from 524.288 to 2097.152
- chain_bias: float32 [4], replicated, may hold values from -1.5 to 1.5
- bias_m: float32 [4], replicated, may hold values from -48 to 48
- bias_v: float32 [4], replicated, may hold values from 5.24288 to 20.97152
Outputs:
- pair_out: bfloat16 [2, 512, 512, 128], P(None, 'row', 'col')
- pair_grad: bfloat16 [2, 512, 512, 128], P(None, 'row', 'col')
- new_weights: float32 [5, 16384], P(None, 'row')
- new_moment_one: float32 [5, 16384], P(None, 'row')
- new_moment_two: float32 [5, 16384], P(None, 'row')
- new_gain: float32 [128], replicated
- new_gain_m: float32 [128], replicated
- new_gain_v: float32 [128], replicated
- new_bias: float32 [4], replicated
- new_bias_m: float32 [4], replicated
- new_bias_v: float32 [4], replicated
The draws below stay inside these ranges and needn't reach their ends.
All inputs are finite; a program needn't handle non-finite values.
Results may differ from the reference program's by a relative error of at most 0.017.
The reference program's roundings to bfloat16 on the way count: a program that leaves them out, or rounds other values in their place, can miss the bound.
Values may be sent and summed in bfloat16 or wider, within the bound.
A program may use at most 256 MiB of HBM per device.

```python
import math
import jax
import jax.numpy as jnp
import numpy as np
from jax import lax

C = 128
H = 4
L = 512
CROPS = 2
STEP = 10


def draw_weights(key, part):
    key = jax.random.fold_in(key, 7)
    base = jax.random.normal(key, (5, C * C), jnp.float32) / math.sqrt(C)
    factor = jnp.array([1.0, 1.0, 1.0, 1.0, math.sqrt(L) / 4.0], jnp.float32)
    return base * factor[:, None]


def block_levels(stream_key, shape, split, least, top_value):
    loudness, own = 1.0, jax.random.fold_in(stream_key, 6)
    for axis_at, blocks in split:
        heights = jnp.exp(jax.random.uniform(jax.random.fold_in(own, axis_at), (blocks,), jnp.float32, least / len(split), top_value / len(split)))
        loudness = loudness * jnp.repeat(heights, shape[axis_at] // blocks).reshape([-1 if axis == axis_at else 1 for axis in range(len(shape))])
    return loudness


def length_profile(amount, total, reach, lean):
    loads = [(1 << 20) // math.isqrt(rank ** lean) + 1 for rank in range(2, amount + 1)]
    rest, holding = total - reach - (amount - 1), [1] * (amount - 1)
    while rest > 0:
        movable = [i for i in range(amount - 1) if holding[i] < reach]
        pool, left = sum([loads[i] for i in movable]), rest
        for i in movable:
            extra = min(reach - holding[i], max(1, left * loads[i] // pool), rest)
            holding[i] = holding[i] + extra
            rest = rest - extra
    return np.array([reach] + holding)


def ragged_sizes(own_key, number_of, total, reach, skew):
    if number_of == 2:
        one = jax.random.randint(own_key, (), max(1, total - reach), min(reach, total - 1) + 1)
        return jnp.stack([one, total - one])
    sizes = jnp.asarray(length_profile(number_of, total, reach, skew), jnp.int32)
    pairs = (number_of - 1) // 2
    source_of, sink = sizes[1:1 + 2 * pairs:2], sizes[2:2 + 2 * pairs:2]
    room = jnp.minimum(source_of - 1, reach - sink)
    passed = jax.random.randint(jax.random.fold_in(own_key, 1), (pairs,), 0, 1 << 20) % (room + 1)
    sizes = sizes.at[1:1 + 2 * pairs:2].set(source_of - passed).at[2:2 + 2 * pairs:2].set(sink + passed)
    return sizes[jax.random.permutation(jax.random.fold_in(own_key, 2), number_of)]


def bell_draw(key, extent, scale, bound, split=(), held_as=jnp.bfloat16):
    level = block_levels(key, extent, split, -0.22, 0.18) if split else 1.0
    entries = jax.random.normal(key, extent, jnp.float32) * scale * level
    return jnp.minimum(jnp.maximum(entries, -bound), bound).astype(held_as)


def setup_inputs(seed: int = 0) -> dict:
    seeds = jax.random.split(jax.random.key(seed), 14)
    pair = bell_draw(seeds[0], (CROPS, L, L, C), 1.0, 6.0, ((1, 8), (2, 4)))
    cotangent = bell_draw(seeds[1], (CROPS, L, L, C), 1.0, 6.0, ((1, 8), (2, 4)))
    segments = jax.vmap(lambda own: jnp.searchsorted(jnp.cumsum(ragged_sizes(own, 4, L, L // 2, 1)), jnp.arange(L), side="right"))(jax.random.split(seeds[2], CROPS)).reshape((CROPS, L)).astype(jnp.int32)
    lengths = ragged_sizes(seeds[3], CROPS, CROPS * L * 3 // 4, L, 1).astype(jnp.int32)
    weights = draw_weights(jax.random.fold_in(seeds[13], 71), 0)
    moment_one = bell_draw(seeds[5], (5, C * C), ((CROPS * L * L) ** 0.5 / 180), 24.0, ((1, 8),), jnp.float32)
    moment_two = jnp.clip(jnp.exp(math.log(5.24288) - 1.3862944 * jax.random.uniform(seeds[6], (5, C * C), jnp.float32) ** block_levels(seeds[6], (5, C * C), ((1, 8),), -0.2, 0.2)), 1.31072, 5.24288)
    gain = jnp.clip(1.0 + 0.1 * jax.random.normal(seeds[7], (C,), jnp.float32), 0.5, 1.5)
    gain_m = bell_draw(seeds[8], (C,), ((CROPS * L * L) ** 0.5 / 9), 512.0, (), jnp.float32)
    gain_v = jnp.clip(jnp.exp(jax.random.uniform(seeds[9], (C,), jnp.float32, math.log(524.288), math.log(2097.152))), 524.288, 2097.152)
    chain_bias = jnp.clip(jax.random.uniform(seeds[10], (H,), jnp.float32, -1.5, 1.5), -1.5, 1.5)
    bias_m = bell_draw(seeds[11], (H,), ((CROPS * L * L) ** 0.5 / 90), 48.0, (), jnp.float32)
    bias_v = jnp.clip(jnp.exp(jax.random.uniform(seeds[12], (H,), jnp.float32, math.log(5.24288), math.log(20.97152))), 5.24288, 20.97152)
    return {"pair": pair, "cotangent": cotangent, "segments": segments, "lengths": lengths, "weights": weights, "moment_one": moment_one, "moment_two": moment_two, "gain": gain, "gain_m": gain_m, "gain_v": gain_v, "chain_bias": chain_bias, "bias_m": bias_m, "bias_v": bias_v}


@jax.custom_vjp
def low(v):
    return lax.optimization_barrier(v.astype(jnp.bfloat16)).astype(jnp.float32)

@jax.custom_vjp
def low_back(v):
    return v

def low_keep(v):
    return (low(v), None)

def low_pass(kept, grad):
    return (grad,)

def back_keep(v):
    return (v, None)

def back_low(kept, grad):
    return (low(grad),)
low.defvjp(low_keep, low_pass)
low_back.defvjp(back_keep, back_low)
HIGH = lax.Precision.HIGHEST
beta_one = 0.9
beta_two = 0.999
epsilon = 1e-06
decay = 0.01
rate = 0.25

def column_attention(column, weights, gain, chain_bias, same, keymask):
    rows = column.shape[0]
    width = column.shape[1]
    heads = chain_bias.shape[0]
    hsize = width // heads
    feature_mean = lax.optimization_barrier(jnp.mean(column, -1, keepdims=True))
    centered_input = column - feature_mean
    var = lax.optimization_barrier(jnp.mean(centered_input * centered_input, -1, keepdims=True))
    normalized_output = low(centered_input * lax.rsqrt(var + 1e-05) * gain)
    query = low(low_back(jnp.dot(normalized_output, weights[0], precision=HIGH)))
    keys = low(low_back(jnp.dot(normalized_output, weights[1], precision=HIGH)))
    values = low(low_back(jnp.dot(normalized_output, weights[2], precision=HIGH)))
    gate = jax.nn.sigmoid(low_back(jnp.dot(normalized_output, weights[3], precision=HIGH)))
    query = query.reshape(rows, heads, hsize)
    keys = keys.reshape(rows, heads, hsize)
    values = values.reshape(rows, heads, hsize)
    scores = low_back(jnp.einsum('ihd,jhd->hij', query, keys, precision=HIGH)) * (1.0 / math.sqrt(hsize))
    scores = scores + chain_bias[:, None, None] * same[None]
    scores = jnp.where(keymask[None, None, :], scores, -1e+30)
    probs = low(low_back(jax.nn.softmax(scores, -1)))
    attended = low_back(jnp.einsum('hij,jhd->ihd', probs, values, precision=HIGH).reshape(rows, width))
    gated = low(low_back(attended * gate))
    return column + jnp.dot(gated, weights[4], precision=HIGH)

def crop_step(carry, inputs):
    weights, gain, chain_bias = (carry[3], carry[4], carry[5])
    pair_crop, cot_crop, segs, length = inputs
    same = (segs[:, None] == segs[None, :]).astype(jnp.float32)
    keymask = jnp.arange(segs.shape[0], dtype=jnp.int32) < length

    def forward(block, wts, gns, bias):
        rounded = low(wts)
        cols = jnp.swapaxes(block, 0, 1)
        single = jax.checkpoint(lambda zc: column_attention(zc, rounded, gns, bias, same, keymask))
        return jnp.swapaxes(lax.map(single, cols), 0, 1)
    result, pull = jax.vjp(forward, pair_crop.astype(jnp.float32), weights, gain, chain_bias)
    dpair, dweights, gain_gradient, dbias = pull(cot_crop.astype(jnp.float32))
    new_carry = (carry[0] + dweights, carry[1] + gain_gradient, carry[2] + dbias, weights, gain, chain_bias)
    return (new_carry, (result.astype(jnp.bfloat16), dpair.astype(jnp.bfloat16)))

def lamb(value, grad, first, second, axes):
    first_new = beta_one * first + (1.0 - beta_one) * grad
    second_new = beta_two * second + (1.0 - beta_two) * grad * grad
    step_dir = first_new / (1.0 - beta_one ** STEP) / (jnp.sqrt(second_new / (1.0 - beta_two ** STEP)) + epsilon) + decay * value
    value_norm = jnp.sqrt(lax.optimization_barrier(jnp.sum(value * value, axis=axes, keepdims=True)))
    step_norm = jnp.sqrt(lax.optimization_barrier(jnp.sum(step_dir * step_dir, axis=axes, keepdims=True)))
    return (value - rate * (value_norm / step_norm) * step_dir, first_new, second_new)

def reference(pair, cotangent, segments, lengths, weights, moment_one, moment_two, gain, gain_m, gain_v, chain_bias, bias_m, bias_v):
    width = gain.shape[0]
    square_w = weights.reshape(5, width, width)
    start = (jnp.zeros_like(square_w), jnp.zeros_like(gain), jnp.zeros_like(chain_bias), square_w, gain, chain_bias)
    final, (pair_out, pair_grad) = lax.scan(crop_step, start, (pair, cotangent, segments, lengths))
    dweights = final[0].reshape(5, width * width)
    gain_gradient, dbias = (final[1], final[2])
    new_weights, new_one, new_two = lamb(weights, dweights, moment_one, moment_two, (1,))
    new_gain, new_gm, new_gv = lamb(gain, gain_gradient, gain_m, gain_v, (0,))
    new_bias, new_bm, new_bv = lamb(chain_bias, dbias, bias_m, bias_v, (0,))
    return (pair_out, pair_grad, new_weights, new_one, new_two, new_gain, new_gm, new_gv, new_bias, new_bm, new_bv)
```

```python
import functools
import math

import jax
import jax.numpy as jnp
from jax import lax
from jax.experimental import pallas as pl
from jax.experimental.pallas import tpu as pltpu
from jax.sharding import PartitionSpec as P

STEP = 10
beta_one = 0.9
beta_two = 0.999
epsilon = 1e-06
decay = 0.01
rate = 0.25

BF = jnp.bfloat16
F32 = jnp.float32
MESH = pl.DeviceIdType.MESH
NT = ((1,), (1,))
TN = ((0,), (0,))
LOG2E = math.log2(math.e)
SEGS = 4


def dot(a, b, dims=((1,), (0,))):
    return lax.dot_general(a, b, (dims, ((), ())), preferred_element_type=F32)


def column(z, co, wallt, wkv, w4, wcat, gain, augk, augq, hot, e_ref, heads, tile):
    total, width = z.shape
    hsize = width // heads
    scale = 1.0 / math.sqrt(hsize)
    cob = co.astype(BF)
    mean = jnp.mean(z, -1, keepdims=True)
    cen = z - mean
    var = jnp.mean(cen * cen, -1, keepdims=True)
    inv = lax.rsqrt(var + 1e-05)
    xhat = cen * inv
    y = (xhat * gain).astype(BF)
    projT = dot(wallt, y, NT)
    kv = dot(y, wkv)
    k = kv[:, :width].astype(BF)
    v = kv[:, width:].astype(BF)
    qT = projT[:width].astype(BF)
    kT = projT[width : 2 * width].astype(BF)
    vT = projT[2 * width : 3 * width].astype(BF)
    gT = jax.nn.sigmoid(projT[3 * width :])
    head_of = lax.broadcasted_iota(jnp.int32, (width, 1), 0) // hsize
    kaug = jnp.concatenate([k, augk], 1)
    ones = jnp.ones((16, total), BF)
    heads_a, heads_r = [], []
    for h in range(heads):
        rows = slice(h * hsize, (h + 1) * hsize)
        qaug = jnp.concatenate([jnp.where(head_of == h, qT, jnp.zeros_like(qT)), augq[h]], 0)
        lhs = jnp.concatenate([vT[rows], ones], 0)
        tiles_a, tiles_r = [], []
        for t in range(0, total, tile):
            s = dot(kaug, qaug[:, t : t + tile]) * (scale * LOG2E)
            e = jnp.exp2(s - jnp.max(s, 0, keepdims=True)).astype(BF)
            e_ref[h, :, t : t + tile] = e
            a = dot(lhs, e)
            r = 1.0 / a[hsize : hsize + 1]
            tiles_a.append(a[:hsize] * r)
            tiles_r.append(r)
        heads_a.append(jnp.concatenate(tiles_a, 1))
        heads_r.append(jnp.broadcast_to(jnp.concatenate(tiles_r, 1), (hsize, total)))
    aT = jnp.concatenate(heads_a, 0)
    oT = (aT * gT).astype(BF)
    out = z + dot(oT, w4, TN)
    dw4 = dot(oT, cob)
    doT = dot(w4, cob, NT).astype(BF).astype(F32)
    daT = (doT * gT).astype(BF).astype(F32)
    dgT = (doT * aT * gT * (1.0 - gT)).astype(BF)
    dnT = (daT * jnp.concatenate(heads_r, 0) * scale).astype(BF)
    prod = aT * dnT.astype(F32)
    dq, dk, dv, db = [], [], [], []
    for h in range(heads):
        rows = slice(h * hsize, (h + 1) * hsize)
        shift = jnp.sum(prod[rows], 0, keepdims=True)
        masked = jnp.where(head_of == h, dnT, jnp.zeros_like(dnT))
        lhs = jnp.concatenate([kT[rows], hot], 0)
        tiles_q, dk_h, dv_h, db_h = [], 0.0, 0.0, 0.0
        for t in range(0, total, tile):
            part = slice(t, t + tile)
            e = e_ref[h, :, part]
            dp = dot(v, masked[:, part]) - shift[:, part]
            ds = (e.astype(F32) * dp).astype(BF)
            x = dot(lhs, ds)
            tiles_q.append(x[:hsize])
            db_h = db_h + x[hsize : hsize + 8] * hot[:8, part].astype(F32)
            dk_h = dk_h + dot(qT[rows, part], ds, NT)
            dv_h = dv_h + dot(dnT[rows, part], e, NT)
        dq.append(jnp.concatenate(tiles_q, 1).astype(BF))
        dk.append(dk_h.astype(BF))
        dv.append((dv_h * (1.0 / scale)).astype(BF))
        db.append(db_h)
    dprojT = jnp.concatenate(dq + dk + dv + [dgT], 0)
    dwt = dot(dprojT, y)
    dy = jnp.transpose(dot(wcat, dprojT))
    dgain = jnp.sum(dy * xhat, 0, keepdims=True)
    dx = dy * gain
    back = dx - jnp.mean(dx, -1, keepdims=True) - xhat * jnp.mean(dx * xhat, -1, keepdims=True)
    return out, co + inv * back, dwt, dw4, dgain, db


def moments(value, grad, first, second):
    first_new = beta_one * first + (1.0 - beta_one) * grad
    second_new = beta_two * second + (1.0 - beta_two) * grad * grad
    step_dir = (
        first_new
        / (1.0 - beta_one**STEP)
        / (jnp.sqrt(second_new / (1.0 - beta_two**STEP)) + epsilon)
        + decay * value
    )
    return (first_new, second_new, step_dir)


def main_kernel(
    dims,
    pair_t,
    cot_t,
    seg_ref,
    len_ref,
    w_ref,
    m1_ref,
    m2_ref,
    gain_ref,
    bias_ref,
    outc,
    gradc,
    red_ref,
    nrm_ref,
    zin,
    obuf,
    e_ref,
    wsend,
    wrecv,
    gsend,
    grecv,
    csend,
    crecv,
    nsend,
    nrecv,
    wallt_ref,
    wkv_ref,
    w4_ref,
    wcat_ref,
    augk_ref,
    augq_ref,
    hot_ref,
    dwt_acc,
    dw4_acc,
    dg_acc,
    db_acc,
    in_sem,
    send_sem,
    out_sem,
    osend_sem,
    misc_recv,
    misc_send,
    loc_sem,
):
    nrow, ncol, crops, cb, cpc, rl, width, heads, wr, tile = dims
    total = nrow * rl
    hsize = width // heads
    scale = 1.0 / math.sqrt(hsize)
    per_crop = cb // cpc
    chunks = crops * per_crop
    me = lax.axis_index("row")
    mc = lax.axis_index("col")

    def row_peer(d):
        return lax.rem(me + d, nrow)

    def col_peer(d):
        return lax.rem(mc + d, ncol)

    barrier = pltpu.get_barrier_semaphore()

    def greet_row(d, _):
        pl.semaphore_signal(barrier, inc=1, device_id=(row_peer(d), mc), device_id_type=MESH)
        return 0

    def greet_col(d, _):
        pl.semaphore_signal(barrier, inc=1, device_id=(me, col_peer(d)), device_id_type=MESH)
        return 0

    lax.fori_loop(1, nrow, greet_row, 0)
    lax.fori_loop(1, ncol, greet_col, 0)
    pl.semaphore_wait(barrier, nrow - 1 + ncol - 1)

    def exchange_row(src_of, dst, stage):
        def push(d, _):
            p = row_peer(d)
            pltpu.make_async_remote_copy(
                src_of(p),
                dst.at[me],
                misc_send.at[stage],
                misc_recv.at[stage],
                device_id=(p, mc),
                device_id_type=MESH,
            ).start()
            return 0

        lax.fori_loop(1, nrow, push, 0)
        pltpu.make_async_copy(src_of(me), dst.at[me], misc_recv.at[stage]).start()

    def exchange_wait(dst, stage):
        pltpu.make_async_copy(dst, dst, misc_recv.at[stage]).wait()

    for j in range(wr):
        wsend[j] = jnp.zeros((8, width), F32)
        wsend[j, 0:5, :] = w_ref[:, j * width : (j + 1) * width]
    exchange_row(lambda p: wsend, wrecv, 0)

    def push_chunk(i, _):
        c = i // per_crop
        j0 = lax.rem(i, per_crop) * cpc

        def push(d, _):
            p = row_peer(d)
            for a, src in enumerate((pair_t, cot_t)):
                pltpu.make_async_remote_copy(
                    src.at[c, p, pl.ds(j0, cpc)],
                    zin.at[i, a, :, me],
                    send_sem.at[a],
                    in_sem.at[i],
                    device_id=(p, mc),
                    device_id_type=MESH,
                ).start()
            return 0

        lax.fori_loop(1, nrow, push, 0)
        for a, src in enumerate((pair_t, cot_t)):
            pltpu.make_async_copy(
                src.at[c, me, pl.ds(j0, cpc)], zin.at[i, a, :, me], in_sem.at[i]
            ).start()
        return 0

    lax.fori_loop(0, chunks, push_chunk, 0)

    lane = lax.broadcasted_iota(jnp.int32, (1, total), 1)
    line = lax.broadcasted_iota(jnp.int32, (width, 1), 0)
    for c in range(crops):
        segs = seg_ref[c : c + 1, :]
        same = (lax.rem(line, SEGS) == segs).astype(F32)
        hot_ref[c] = jnp.where(line[:16] < SEGS, same[:16], 0.0).astype(BF)
        pad = jnp.where(lane >= len_ref[c], -1e30, 0.0)
        rowsk = jnp.where(line < 3 * SEGS, same, jnp.where(line == 3 * SEGS, pad, 0.0))
        augk_ref[c] = jnp.transpose(rowsk).astype(BF)
        for h in range(heads):
            full = jnp.full((width, 1), bias_ref[h] * (1.0 / scale), F32)
            high = full.astype(BF).astype(F32)
            mid = (full - high).astype(BF).astype(F32)
            low = full - high - mid
            part = jnp.where(line < SEGS, high, jnp.where(line < 2 * SEGS, mid, low))
            rowsq = jnp.where(line < 3 * SEGS, same * part, jnp.where(line == 3 * SEGS, 1.0, 0.0))
            augq_ref[c, h] = rowsq.astype(BF)

    dwt_acc[...] = jnp.zeros_like(dwt_acc)
    dw4_acc[...] = jnp.zeros_like(dw4_acc)
    dg_acc[...] = jnp.zeros_like(dg_acc)
    db_acc[...] = jnp.zeros_like(db_acc)

    exchange_wait(wrecv, 0)
    for kk in range(5):
        w = wrecv[:, :, kk, :].reshape(width, width)
        wb = w.astype(BF)
        if kk < 4:
            wallt_ref[kk * width : (kk + 1) * width, :] = jnp.transpose(w).astype(BF)
            wcat_ref[:, kk * width : (kk + 1) * width] = wb
        if kk in (1, 2):
            wkv_ref[:, (kk - 1) * width : kk * width] = wb
        if kk == 4:
            w4_ref[...] = wb

    def work(i, _):
        c = i // per_crop
        j0 = lax.rem(i, per_crop) * cpc
        pltpu.make_async_copy(zin.at[i], zin.at[i], in_sem.at[i]).wait()

        def one(j, _):
            z = zin[i, 0, j].astype(F32).reshape(total, width)
            co = zin[i, 1, j].astype(F32).reshape(total, width)
            out, grad, dwt, dw4, dgain, db = column(
                z,
                co,
                wallt_ref[...],
                wkv_ref[...],
                w4_ref[...],
                wcat_ref[...],
                gain_ref[...],
                augk_ref[c],
                [augq_ref[c, h] for h in range(heads)],
                hot_ref[c],
                e_ref,
                heads,
                tile,
            )
            obuf[i, 0, j] = out.reshape(nrow, rl, width).astype(BF)
            obuf[i, 1, j] = grad.reshape(nrow, rl, width).astype(BF)
            dwt_acc[...] += dwt
            dw4_acc[...] += dw4
            dg_acc[0:1] += dgain
            for h in range(heads):
                db_acc[h] += db[h]
            return 0

        lax.fori_loop(0, cpc, one, 0)

        def push(d, _):
            p = row_peer(d)
            for a, dst in enumerate((outc, gradc)):
                pltpu.make_async_remote_copy(
                    obuf.at[i, a, :, p],
                    dst.at[c, me, pl.ds(j0, cpc)],
                    osend_sem.at[a],
                    out_sem.at[a],
                    device_id=(p, mc),
                    device_id_type=MESH,
                ).start()
            return 0

        lax.fori_loop(1, nrow, push, 0)
        for a, dst in enumerate((outc, gradc)):
            pltpu.make_async_copy(
                obuf.at[i, a, :, me], dst.at[c, me, pl.ds(j0, cpc)], out_sem.at[a]
            ).start()
        return 0

    lax.fori_loop(0, chunks, work, 0)

    for kk in range(4):
        gsend[:, kk, :] = jnp.transpose(dwt_acc[kk * width : (kk + 1) * width, :])
    gsend[:, 4, :] = dw4_acc[...]
    gsend[:, 5, :] = jnp.broadcast_to(dg_acc[0:1], (width, width))
    spot = lax.broadcasted_iota(jnp.int32, (1, width), 1)
    dbias = jnp.zeros((1, width), F32)
    for h in range(heads):
        one_h = jnp.sum(jnp.sum(db_acc[h], 0, keepdims=True), 1, keepdims=True) * (1.0 / scale)
        dbias = jnp.where(spot == h, one_h, dbias)
    gsend[:, 6, :] = jnp.broadcast_to(dbias, (width, width))
    gsend[:, 7, :] = jnp.zeros((width, width), F32)
    exchange_row(lambda p: gsend.at[pl.ds(p * wr, wr)], grecv, 1)
    exchange_wait(grecv, 1)
    csend[...] = lax.fori_loop(1, nrow, lambda r, s: s + grecv[r], grecv[0])

    def push_col(d, _):
        pltpu.make_async_remote_copy(
            csend,
            crecv.at[mc],
            misc_send.at[2],
            misc_recv.at[2],
            device_id=(me, col_peer(d)),
            device_id_type=MESH,
        ).start()
        return 0

    lax.fori_loop(1, ncol, push_col, 0)
    pltpu.make_async_copy(csend, crecv.at[mc], misc_recv.at[2]).start()
    exchange_wait(crecv, 2)
    grads = lax.fori_loop(1, ncol, lambda r, s: s + crecv[r], crecv[0])
    red = jnp.concatenate([grads[j] for j in range(wr)], 1)
    red_ref[...] = red
    wval = w_ref[...]
    step_w = moments(wval, red[0:5], m1_ref[...], m2_ref[...])[2]
    nsend[...] = jnp.zeros_like(nsend)
    nsend[0:5, :] = jnp.where(
        spot == 0,
        jnp.sum(wval * wval, 1, keepdims=True),
        jnp.where(spot == 1, jnp.sum(step_w * step_w, 1, keepdims=True), 0.0),
    )
    exchange_row(lambda p: nsend, nrecv, 3)
    exchange_wait(nrecv, 3)
    nrm_ref[...] = lax.fori_loop(1, nrow, lambda r, s: s + nrecv[r], nrecv[0])

    for a, (src, dst) in enumerate(((pair_t, outc), (cot_t, gradc))):
        sent = src.at[:, pl.ds(0, nrow - 1)]
        pltpu.make_async_copy(sent, sent, send_sem.at[a]).wait()
        gone = dst.at[:, pl.ds(0, nrow - 1)]
        pltpu.make_async_copy(gone, gone, osend_sem.at[a]).wait()
        pltpu.make_async_copy(dst, dst, out_sem.at[a]).wait()
    for stage, dst in ((0, wrecv), (1, grecv), (3, nrecv)):
        sent = dst.at[pl.ds(0, nrow - 1)]
        pltpu.make_async_copy(sent, sent, misc_send.at[stage]).wait()
    sent = crecv.at[pl.ds(0, ncol - 1)]
    pltpu.make_async_copy(sent, sent, misc_send.at[2]).wait()


def step_kernel(
    red_ref,
    nrm_ref,
    w_ref,
    m1_ref,
    m2_ref,
    gain_ref,
    gm_ref,
    gv_ref,
    bias_ref,
    bm_ref,
    bv_ref,
    nw_ref,
    n1_ref,
    n2_ref,
    ng_ref,
    ngm_ref,
    ngv_ref,
    nb_ref,
    nbm_ref,
    nbv_ref,
):
    width = gain_ref.shape[1]
    heads = bias_ref.shape[1]
    wval = w_ref[...]
    first, second, step_w = moments(wval, red_ref[0:5], m1_ref[...], m2_ref[...])
    ratio = jnp.sqrt(nrm_ref[0:5, 0:1]) / jnp.sqrt(nrm_ref[0:5, 1:2])
    nw_ref[...] = wval - rate * ratio * step_w
    n1_ref[...] = first
    n2_ref[...] = second
    for row, n, refs in (
        (5, width, (gain_ref, gm_ref, gv_ref, ng_ref, ngm_ref, ngv_ref)),
        (6, heads, (bias_ref, bm_ref, bv_ref, nb_ref, nbm_ref, nbv_ref)),
    ):
        val = refs[0][...]
        first, second, step_v = moments(val, red_ref[row : row + 1, 0:n], refs[1][...], refs[2][...])
        ratio = jnp.sqrt(jnp.sum(val * val, 1, keepdims=True)) / jnp.sqrt(
            jnp.sum(step_v * step_v, 1, keepdims=True)
        )
        refs[3][...] = val - rate * ratio * step_v
        refs[4][...] = first
        refs[5][...] = second


def body(
    nrow,
    ncol,
    pair,
    cotangent,
    segments,
    lengths,
    weights,
    moment_one,
    moment_two,
    gain,
    gain_m,
    gain_v,
    chain_bias,
    bias_m,
    bias_v,
):
    crops, rl, cl, width = pair.shape
    heads = chain_bias.shape[0]
    cb = cl // nrow
    cpc = min(2, cb)
    wr = weights.shape[1] // width
    total = nrow * rl
    tile = min(256, total)
    chunks = crops * (cb // cpc)
    dims = (nrow, ncol, crops, cb, cpc, rl, width, heads, wr, tile)
    pair_t = jnp.swapaxes(pair, 1, 2).reshape(crops, nrow, cb, rl, width)
    cot_t = jnp.swapaxes(cotangent, 1, 2).reshape(crops, nrow, cb, rl, width)
    hbm = pl.BlockSpec(memory_space=pl.ANY)
    vmem = pl.BlockSpec(memory_space=pltpu.VMEM)
    smem = pl.BlockSpec(memory_space=pltpu.SMEM)
    dma = pltpu.SemaphoreType.DMA
    outc, gradc, red, nrm = pl.pallas_call(
        functools.partial(main_kernel, dims),
        out_shape=(
            jax.ShapeDtypeStruct((crops, nrow, cb, rl, width), BF),
            jax.ShapeDtypeStruct((crops, nrow, cb, rl, width), BF),
            jax.ShapeDtypeStruct((8, wr * width), F32),
            jax.ShapeDtypeStruct((8, width), F32),
        ),
        in_specs=[hbm, hbm, vmem, smem, vmem, vmem, vmem, vmem, smem],
        out_specs=(hbm, hbm, vmem, vmem),
        scratch_shapes=[
            pltpu.VMEM((chunks, 2, cpc, nrow, rl, width), BF),
            pltpu.VMEM((chunks, 2, cpc, nrow, rl, width), BF),
            pltpu.VMEM((heads, total, total), BF),
            pltpu.VMEM((wr, 8, width), F32),
            pltpu.VMEM((nrow, wr, 8, width), F32),
            pltpu.VMEM((nrow * wr, 8, width), F32),
            pltpu.VMEM((nrow, wr, 8, width), F32),
            pltpu.VMEM((wr, 8, width), F32),
            pltpu.VMEM((ncol, wr, 8, width), F32),
            pltpu.VMEM((8, width), F32),
            pltpu.VMEM((nrow, 8, width), F32),
            pltpu.VMEM((4 * width, width), BF),
            pltpu.VMEM((width, 2 * width), BF),
            pltpu.VMEM((width, width), BF),
            pltpu.VMEM((width, 4 * width), BF),
            pltpu.VMEM((crops, total, width), BF),
            pltpu.VMEM((crops, heads, width, total), BF),
            pltpu.VMEM((crops, 16, total), BF),
            pltpu.VMEM((4 * width, width), F32),
            pltpu.VMEM((width, width), F32),
            pltpu.VMEM((8, width), F32),
            pltpu.VMEM((heads, 8, tile), F32),
            dma((chunks,)),
            dma((2,)),
            dma((2,)),
            dma((2,)),
            dma((4,)),
            dma((4,)),
            dma((1,)),
        ],
        compiler_params=pltpu.CompilerParams(
            collective_id=0, has_side_effects=True, vmem_limit_bytes=56 << 20
        ),
        name="column_attention",
    )(
        pair_t,
        cot_t,
        segments,
        lengths,
        weights,
        moment_one,
        moment_two,
        gain.reshape(1, width),
        chain_bias,
    )
    pair_out = jnp.swapaxes(outc.reshape(crops, cl, rl, width), 1, 2)
    pair_grad = jnp.swapaxes(gradc.reshape(crops, cl, rl, width), 1, 2)
    small = (gain, gain_m, gain_v, chain_bias, bias_m, bias_v)
    ops = [red, nrm, weights, moment_one, moment_two] + [a.reshape(1, -1) for a in small]
    res = pl.pallas_call(
        step_kernel,
        out_shape=[jax.ShapeDtypeStruct(weights.shape, F32)] * 3
        + [jax.ShapeDtypeStruct((1, width), F32)] * 3
        + [jax.ShapeDtypeStruct((1, heads), F32)] * 3,
        in_specs=[vmem] * len(ops),
        out_specs=[vmem] * 9,
        name="lamb_step",
    )(*ops)
    return (pair_out, pair_grad, *res[:3], *[a.reshape(-1) for a in res[3:]])


def solution(mesh):
    big = P(None, "row", "col", None)
    shard = P(None, "row")
    return jax.shard_map(
        functools.partial(body, mesh.shape["row"], mesh.shape["col"]),
        mesh=mesh,
        in_specs=(big, big, P(), P(), shard, shard, shard) + (P(),) * 6,
        out_specs=(big, big, shard, shard, shard) + (P(),) * 6,
        check_vma=False,
    )
```

```python
import functools
import math

import jax
import jax.numpy as jnp
from jax import lax
from jax.experimental import pallas as pl
from jax.experimental.pallas import tpu as pltpu
from jax.sharding import PartitionSpec as P

STEP = 10
beta_one = 0.9
beta_two = 0.999
epsilon = 1e-06
decay = 0.01
rate = 0.25

BF = jnp.bfloat16
F32 = jnp.float32
MESH = pl.DeviceIdType.MESH
NT = ((1,), (1,))
TN = ((0,), (0,))
LOG2E = math.log2(math.e)
SEGS = 4


def dot(a, b, dims=((1,), (0,))):
    return lax.dot_general(a, b, (dims, ((), ())), preferred_element_type=F32)


def column(z, co, wallt, wkv, w4, wcat, gain, augk, augq, hot, e_ref, heads, tile):
    total, width = z.shape
    hsize = width // heads
    scale = 1.0 / math.sqrt(hsize)
    cob = co.astype(BF)
    mean = jnp.mean(z, -1, keepdims=True)
    cen = z - mean
    var = jnp.mean(cen * cen, -1, keepdims=True)
    inv = lax.rsqrt(var + 1e-05)
    xhat = cen * inv
    y = (xhat * gain).astype(BF)
    projT = dot(wallt, y, NT)
    kv = dot(y, wkv)
    k = kv[:, :width].astype(BF)
    v = kv[:, width:].astype(BF)
    qT = projT[:width].astype(BF)
    kT = projT[width : 2 * width].astype(BF)
    vT = projT[2 * width : 3 * width].astype(BF)
    gT = jax.nn.sigmoid(projT[3 * width :])
    head_of = lax.broadcasted_iota(jnp.int32, (width, 1), 0) // hsize
    kaug = jnp.concatenate([k, augk], 1)
    ones = jnp.ones((16, total), BF)
    heads_a, heads_r = [], []
    for h in range(heads):
        rows = slice(h * hsize, (h + 1) * hsize)
        qaug = jnp.concatenate([jnp.where(head_of == h, qT, jnp.zeros_like(qT)), augq[h]], 0)
        lhs = jnp.concatenate([vT[rows], ones], 0)
        tiles_a, tiles_r = [], []
        for t in range(0, total, tile):
            s = dot(kaug, qaug[:, t : t + tile]) * (scale * LOG2E)
            e = jnp.exp2(s - jnp.max(s, 0, keepdims=True)).astype(BF)
            e_ref[h, :, t : t + tile] = e
            a = dot(lhs, e)
            r = 1.0 / a[hsize : hsize + 1]
            tiles_a.append(a[:hsize] * r)
            tiles_r.append(r)
        heads_a.append(jnp.concatenate(tiles_a, 1))
        heads_r.append(jnp.broadcast_to(jnp.concatenate(tiles_r, 1), (hsize, total)))
    aT = jnp.concatenate(heads_a, 0)
    oT = (aT * gT).astype(BF)
    out = z + dot(oT, w4, TN)
    dw4 = dot(oT, cob)
    doT = dot(w4, cob, NT).astype(BF).astype(F32)
    daT = (doT * gT).astype(BF).astype(F32)
    dgT = (doT * aT * gT * (1.0 - gT)).astype(BF)
    dnT = (daT * jnp.concatenate(heads_r, 0) * scale).astype(BF)
    prod = aT * dnT.astype(F32)
    dq, dk, dv, db = [], [], [], []
    for h in range(heads):
        rows = slice(h * hsize, (h + 1) * hsize)
        shift = jnp.sum(prod[rows], 0, keepdims=True)
        masked = jnp.where(head_of == h, dnT, jnp.zeros_like(dnT))
        lhs = jnp.concatenate([kT[rows], hot], 0)
        tiles_q, dk_h, dv_h, db_h = [], 0.0, 0.0, 0.0
        for t in range(0, total, tile):
            part = slice(t, t + tile)
            e = e_ref[h, :, part]
            dp = dot(v, masked[:, part]) - shift[:, part]
            ds = (e.astype(F32) * dp).astype(BF)
            x = dot(lhs, ds)
            tiles_q.append(x[:hsize])
            db_h = db_h + x[hsize : hsize + 8] * hot[:8, part].astype(F32)
            dk_h = dk_h + dot(qT[rows, part], ds, NT)
            dv_h = dv_h + dot(dnT[rows, part], e, NT)
        dq.append(jnp.concatenate(tiles_q, 1).astype(BF))
        dk.append(dk_h.astype(BF))
        dv.append((dv_h * (1.0 / scale)).astype(BF))
        db.append(db_h)
    dprojT = jnp.concatenate(dq + dk + dv + [dgT], 0)
    dwt = dot(dprojT, y)
    dy = jnp.transpose(dot(wcat, dprojT))
    dgain = jnp.sum(dy * xhat, 0, keepdims=True)
    dx = dy * gain
    back = dx - jnp.mean(dx, -1, keepdims=True) - xhat * jnp.mean(dx * xhat, -1, keepdims=True)
    return out, co + inv * back, dwt, dw4, dgain, db


def moments(value, grad, first, second):
    first_new = beta_one * first + (1.0 - beta_one) * grad
    second_new = beta_two * second + (1.0 - beta_two) * grad * grad
    step_dir = (
        first_new
        / (1.0 - beta_one**STEP)
        / (jnp.sqrt(second_new / (1.0 - beta_two**STEP)) + epsilon)
        + decay * value
    )
    return (first_new, second_new, step_dir)


def main_kernel(dims, names, *refs):
    nrow, ncol, crops, cb, rl, width, heads, wr, tile, direct = dims
    pair_ref, cot_ref, seg_ref, len_ref, w_ref, m1_ref, m2_ref, gain_ref, bias_ref = refs[:9]
    fins, red_ref, nrm_ref = refs[9:11], refs[11], refs[12]
    s = dict(zip(names, refs[13:]))
    zin, obuf = s["zin"], s["obuf"]
    in_sem, send_sem, out_sem, osend_sem = s["in_sem"], s["send_sem"], s["out_sem"], s["osend_sem"]
    misc_recv, misc_send = s["misc_recv"], s["misc_send"]
    if direct:
        stage, sbuf, raw_sem = s["stage"], s["sbuf"], s["raw_sem"]
    srcs = (pair_ref, cot_ref)
    total = nrow * rl
    hsize = width // heads
    scale = 1.0 / math.sqrt(hsize)
    slots = s["wrow"].shape[1]
    me = lax.axis_index("row")
    mc = lax.axis_index("col")

    def row_peer(d):
        return lax.rem(me + d, nrow)

    def col_peer(d):
        return lax.rem(mc + d, ncol)

    def cols_of(p):
        return pl.ds(pl.multiple_of(p * cb, cb), cb)

    if direct:
        def load(n, _):
            c, p = n // nrow, row_peer(lax.rem(n + 1, nrow))
            for a in range(2):
                pltpu.make_async_copy(
                    srcs[a].at[c, :, cols_of(p), :], obuf.at[c, a, p], raw_sem.at[c, a, p]
                ).start()
            return 0

        lax.fori_loop(0, crops * nrow, load, 0)

    barrier = pltpu.get_barrier_semaphore()

    def greet_row(d, _):
        pl.semaphore_signal(barrier, inc=1, device_id=(row_peer(d), mc), device_id_type=MESH)
        return 0

    def greet_col(d, _):
        pl.semaphore_signal(barrier, inc=1, device_id=(me, col_peer(d)), device_id_type=MESH)
        return 0

    lax.fori_loop(1, nrow, greet_row, 0)
    lax.fori_loop(1, ncol, greet_col, 0)
    pl.semaphore_wait(barrier, nrow - 1 + ncol - 1)

    def remote(src, dst, send, recv, peer):
        pltpu.make_async_remote_copy(
            src, dst, send, recv, device_id=peer, device_id_type=MESH
        ).start()

    def exchange_row(src_of, dst, n):
        def push(d, _):
            p = row_peer(d)
            remote(src_of(p), dst.at[me], misc_send.at[n], misc_recv.at[n], (p, mc))
            return 0

        lax.fori_loop(1, nrow, push, 0)
        pltpu.make_async_copy(src_of(me), dst.at[me], misc_recv.at[n]).start()

    def exchange_col(src_of, dst, n):
        def push(d, _):
            p = col_peer(d)
            remote(src_of(p), dst.at[mc], misc_send.at[n], misc_recv.at[n], (me, p))
            return 0

        lax.fori_loop(1, ncol, push, 0)
        pltpu.make_async_copy(src_of(mc), dst.at[mc], misc_recv.at[n]).start()

    def landed(dst, n):
        pltpu.make_async_copy(dst, dst, misc_recv.at[n]).wait()

    def total_of(ref, n):
        return lax.fori_loop(1, n, lambda r, s: s + ref[r], ref[0])

    for j in range(wr):
        s["wtmp"][0:5, j, :] = w_ref[:, j * width : (j + 1) * width]
    for k in range(slots * ncol):
        s["wsend"][k] = (s["wtmp"][k] if k < 5 else jnp.zeros((wr, width), F32)).astype(s["wsend"].dtype)
    exchange_row(lambda p: s["wsend"].at[pl.ds(mc * slots, slots)], s["wrow"], 0)

    def push_column(c, j, d):
        p = row_peer(d)
        i = c * cb + j
        for a in range(2):
            src = sbuf.at[c, a, j, p] if direct else srcs[a].at[c, p, j]
            remote(src, zin.at[i, a, me], send_sem.at[a], in_sem.at[i], (p, mc))

    def keep_column(c, j):
        i = c * cb + j
        for a in range(2):
            src = sbuf.at[c, a, j, me] if direct else srcs[a].at[c, me, j]
            pltpu.make_async_copy(src, zin.at[i, a, me], in_sem.at[i]).start()

    def push_columns(c, first):
        def at_column(j, _):
            def to_peer(d, _):
                push_column(c, j, d)
                return 0

            lax.fori_loop(1, nrow, to_peer, 0)
            keep_column(c, j)
            return 0

        lax.fori_loop(first, cb, at_column, 0)

    def turn(c, d):
        p = row_peer(d)
        for a in range(2):
            here = obuf.at[c, a, p]
            pltpu.make_async_copy(here, here, raw_sem.at[c, a, p]).wait()
            stage[a] = obuf[c, a, p].astype(F32).reshape(rl * cb, width)
            for j in range(cb):
                sbuf[c, a, j, p] = stage[a, pl.ds(j, rl, stride=cb), :].astype(BF)

    if direct:

        def first_blocks(d, _):
            turn(0, d)
            push_column(0, 0, d)
            return 0

        lax.fori_loop(1, nrow, first_blocks, 0)
        turn(0, 0)
        keep_column(0, 0)
        push_columns(0, 1)
    else:
        for c in range(crops):
            push_columns(c, 0)

    landed(s["wrow"], 0)
    exchange_col(lambda p: s["wrow"], s["wall"], 1)

    if direct:

        def later_blocks(d, _):
            for c in range(1, crops):
                turn(c, d)
            return 0

        lax.fori_loop(0, nrow, later_blocks, 0)
        for c in range(1, crops):
            push_columns(c, 0)

    lane = lax.broadcasted_iota(jnp.int32, (1, total), 1)
    line = lax.broadcasted_iota(jnp.int32, (width, 1), 0)
    for c in range(crops):
        segs = seg_ref[c : c + 1, :]
        same = (lax.rem(line, SEGS) == segs).astype(F32)
        s["hot"][c] = jnp.where(line[:16] < SEGS, same[:16], 0.0).astype(BF)
        pad = jnp.where(lane >= len_ref[c], -1e30, 0.0)
        rowsk = jnp.where(line < 3 * SEGS, same, jnp.where(line == 3 * SEGS, pad, 0.0))
        s["augk"][c] = jnp.transpose(rowsk).astype(BF)
        for h in range(heads):
            full = jnp.full((width, 1), bias_ref[h] * (1.0 / scale), F32)
            high = full.astype(BF).astype(F32)
            mid = (full - high).astype(BF).astype(F32)
            low = full - high - mid
            part = jnp.where(line < SEGS, high, jnp.where(line < 2 * SEGS, mid, low))
            rowsq = jnp.where(line < 3 * SEGS, same * part, jnp.where(line == 3 * SEGS, 1.0, 0.0))
            s["augq"][c, h] = rowsq.astype(BF)

    s["dwt_acc"][...] = jnp.zeros_like(s["dwt_acc"])
    s["dw4_acc"][...] = jnp.zeros_like(s["dw4_acc"])
    s["dg_acc"][...] = jnp.zeros_like(s["dg_acc"])
    s["db_acc"][...] = jnp.zeros_like(s["db_acc"])

    landed(s["wall"], 1)
    for k in range(5):
        wb = s["wall"][k // slots, :, k % slots].astype(F32).reshape(width, width)
        if k < 4:
            s["wallt"][k * width : (k + 1) * width, :] = jnp.transpose(wb).astype(BF)
            s["wcat"][:, k * width : (k + 1) * width] = wb.astype(BF)
        if k in (1, 2):
            s["wkv"][:, (k - 1) * width : k * width] = wb.astype(BF)
        if k == 4:
            s["w4"][...] = wb.astype(BF)

    def work(c, j):
        i = c * cb + j
        pltpu.make_async_copy(zin.at[i], zin.at[i], in_sem.at[i]).wait()
        out, grad, dwt, dw4, dgain, db = column(
            zin[i, 0].astype(F32).reshape(total, width),
            zin[i, 1].astype(F32).reshape(total, width),
            s["wallt"][...],
            s["wkv"][...],
            s["w4"][...],
            s["wcat"][...],
            gain_ref[...],
            s["augk"][c],
            [s["augq"][c, h] for h in range(heads)],
            s["hot"][c],
            s["prob"],
            heads,
            tile,
        )
        s["dwt_acc"][...] += dwt
        s["dw4_acc"][...] += dw4
        s["dg_acc"][0:1] += dgain
        for h in range(heads):
            s["db_acc"][h] += db[h]
        if direct:
            zin[i, 0] = out.reshape(nrow, rl, width).astype(BF)
            zin[i, 1] = grad.reshape(nrow, rl, width).astype(BF)
        else:
            obuf[i, 0] = out.reshape(nrow, rl, width).astype(BF)
            obuf[i, 1] = grad.reshape(nrow, rl, width).astype(BF)

            def push(d, _):
                p = row_peer(d)
                for a in range(2):
                    remote(
                        obuf.at[i, a, p], fins[a].at[c, me, j], osend_sem.at[a], out_sem.at[a], (p, mc)
                    )
                return 0

            lax.fori_loop(1, nrow, push, 0)
            for a in range(2):
                pltpu.make_async_copy(obuf.at[i, a, me], fins[a].at[c, me, j], out_sem.at[a]).start()

    def work_crop(c, _):
        def work_column(j, _):
            work(c, j)
            return 0

        lax.fori_loop(0, cb, work_column, 0)
        return 0

    def give_back(c, a, first, last):
        here = fins[a].at[c, :, cols_of(me), :]

        def give(d, _):
            p = row_peer(d)
            for j in range(cb):
                stage[a, pl.ds(j, rl, stride=cb), :] = zin[c * cb + j, a, p].astype(F32)
            obuf[c, a, p] = stage[a].reshape(rl, cb, width).astype(BF)

            @pl.when(d > 0)
            def _():
                remote(obuf.at[c, a, p], here, osend_sem.at[a], out_sem.at[a], (p, mc))

            @pl.when(d == 0)
            def _():
                pltpu.make_async_copy(obuf.at[c, a, p], here, out_sem.at[a]).start()

            return 0

        lax.fori_loop(first, last, give, 0)

    if direct:

        def most(c, _):
            work_crop(c, 0)
            give_back(c, 0, 0, nrow)
            give_back(c, 1, 0, nrow)
            return 0

        lax.fori_loop(0, crops - 1, most, 0)
        work_crop(crops - 1, 0)
    else:
        lax.fori_loop(0, crops, work_crop, 0)

    gsend = s["gsend"]
    for k in range(4):
        gsend[k] = jnp.transpose(s["dwt_acc"][k * width : (k + 1) * width, :])
    gsend[4] = s["dw4_acc"][...]
    gsend[5] = jnp.broadcast_to(s["dg_acc"][0:1], (width, width))
    spot = lax.broadcasted_iota(jnp.int32, (1, width), 1)
    dbias = jnp.zeros((1, width), F32)
    for h in range(heads):
        total_h = jnp.sum(jnp.sum(s["db_acc"][h], 0, keepdims=True), 1, keepdims=True)
        dbias = jnp.where(spot == h, total_h * (1.0 / scale), dbias)
    gsend[6] = jnp.broadcast_to(dbias, (width, width))
    for k in range(7, slots * ncol):
        gsend[k] = jnp.zeros((width, width), F32)
    exchange_col(lambda p: gsend.at[pl.ds(p * slots, slots)], s["grecv"], 2)
    if direct:
        give_back(crops - 1, 0, 0, nrow)
    landed(s["grecv"], 2)
    share = total_of(s["grecv"], ncol)
    for p in range(nrow):
        s["ssend"][p] = share[:, p * wr : (p + 1) * wr, :]
    exchange_row(lambda p: s["ssend"].at[p], s["srecv"], 3)
    if direct:
        give_back(crops - 1, 1, 0, nrow)
    landed(s["srecv"], 3)
    s["csend"][...] = total_of(s["srecv"], nrow)
    exchange_col(lambda p: s["csend"], s["crecv"], 4)
    landed(s["crecv"], 4)
    for j in range(wr):
        red_ref[:, j * width : (j + 1) * width] = s["crecv"][:, :, j, :].reshape(slots * ncol, width)
    wval = w_ref[...]
    step_w = moments(wval, red_ref[0:5, :], m1_ref[...], m2_ref[...])[2]
    place = lax.broadcasted_iota(jnp.int32, (5, 1), 0)
    squares = jnp.where(spot == place, jnp.sum(wval * wval, 1, keepdims=True), 0.0)
    squares += jnp.where(spot == place + 8, jnp.sum(step_w * step_w, 1, keepdims=True), 0.0)
    s["nsend"][...] = jnp.sum(squares, 0, keepdims=True)
    exchange_row(lambda p: s["nsend"], s["nrecv"], 5)
    landed(s["nrecv"], 5)
    nrm_ref[...] = total_of(s["nrecv"], nrow)

    most_rows = pl.ds(0, nrow - 1)
    for a in range(2):
        sent = sbuf.at[:, a, :, most_rows] if direct else srcs[a].at[:, most_rows]
        pltpu.make_async_copy(sent, sent, send_sem.at[a]).wait()
        gone = obuf.at[:, a, most_rows]
        pltpu.make_async_copy(gone, gone, osend_sem.at[a]).wait()
        pltpu.make_async_copy(fins[a], fins[a], out_sem.at[a]).wait()
    for n, name in enumerate(("wrow", "wall", "grecv", "srecv", "crecv", "nrecv")):
        sent = s[name].at[pl.ds(0, s[name].shape[0] - 1)]
        pltpu.make_async_copy(sent, sent, misc_send.at[n]).wait()


def step_kernel(direct, *refs):
    if direct:
        fins, refs = refs[0:2], refs[2:]
    red_ref, nrm_ref, w_ref, m1_ref, m2_ref, gain_ref, gm_ref, gv_ref, bias_ref, bm_ref, bv_ref = refs[:11]
    refs = refs[11:]
    if direct:
        bigs, refs, sem = refs[0:2], refs[2:11], refs[11]
        copies = [pltpu.make_async_copy(fins[a], bigs[a], sem.at[a]) for a in range(2)]
        for copy in copies:
            copy.start()
    nw_ref, n1_ref, n2_ref, ng_ref, ngm_ref, ngv_ref, nb_ref, nbm_ref, nbv_ref = refs
    width = gain_ref.shape[1]
    heads = bias_ref.shape[1]
    wval = w_ref[...]
    first, second, step_w = moments(wval, red_ref[0:5, :], m1_ref[...], m2_ref[...])
    spot = lax.broadcasted_iota(jnp.int32, (1, width), 1)
    place = lax.broadcasted_iota(jnp.int32, (5, 1), 0)
    value_sq = jnp.sum(jnp.where(spot == place, nrm_ref[...], 0.0), 1, keepdims=True)
    step_sq = jnp.sum(jnp.where(spot == place + 8, nrm_ref[...], 0.0), 1, keepdims=True)
    nw_ref[...] = wval - rate * (jnp.sqrt(value_sq) / jnp.sqrt(step_sq)) * step_w
    n1_ref[...] = first
    n2_ref[...] = second
    for row, n, own in (
        (5, width, (gain_ref, gm_ref, gv_ref, ng_ref, ngm_ref, ngv_ref)),
        (6, heads, (bias_ref, bm_ref, bv_ref, nb_ref, nbm_ref, nbv_ref)),
    ):
        val = own[0][...]
        first, second, step_v = moments(val, red_ref[row : row + 1, 0:n], own[1][...], own[2][...])
        ratio = jnp.sqrt(jnp.sum(val * val, 1, keepdims=True)) / jnp.sqrt(
            jnp.sum(step_v * step_v, 1, keepdims=True)
        )
        own[3][...] = val - rate * ratio * step_v
        own[4][...] = first
        own[5][...] = second
    if direct:
        for copy in copies:
            copy.wait()


def body(
    nrow,
    ncol,
    pair,
    cotangent,
    segments,
    lengths,
    weights,
    moment_one,
    moment_two,
    gain,
    gain_m,
    gain_v,
    chain_bias,
    bias_m,
    bias_v,
):
    crops, rl, cl, width = pair.shape
    heads = chain_bias.shape[0]
    cb = cl // nrow
    wr = weights.shape[1] // width
    total = nrow * rl
    tile = min(256, total)
    slots = -(-8 // ncol)
    direct = cb % 16 == 0 and rl % 16 == 0
    dims = (nrow, ncol, crops, cb, rl, width, heads, wr, tile, direct)
    wtype = BF if wr % 16 == 0 else F32
    hbm = pl.BlockSpec(memory_space=pl.ANY)
    vmem = pl.BlockSpec(memory_space=pltpu.VMEM)
    smem = pl.BlockSpec(memory_space=pltpu.SMEM)
    dma = pltpu.SemaphoreType.DMA
    parts = (crops, nrow, cb, rl, width)
    if direct:
        sources = (pair, cotangent)
        fin = jax.ShapeDtypeStruct(pair.shape, BF)
        obuf = (crops, 2, nrow, rl, cb, width)
    else:
        sources = tuple(jnp.swapaxes(x, 1, 2).reshape(parts) for x in (pair, cotangent))
        fin = jax.ShapeDtypeStruct(parts, BF)
        obuf = (crops * cb, 2, nrow, rl, width)
    scratch = {
        "zin": pltpu.VMEM((crops * cb, 2, nrow, rl, width), BF),
        "obuf": pltpu.VMEM(obuf, BF),
        "prob": pltpu.VMEM((heads, total, total), BF),
        "wtmp": pltpu.VMEM((8, wr, width), F32),
        "wsend": pltpu.VMEM((slots * ncol, wr, width), wtype),
        "wrow": pltpu.VMEM((nrow, slots, wr, width), wtype),
        "wall": pltpu.VMEM((ncol, nrow, slots, wr, width), wtype),
        "gsend": pltpu.VMEM((slots * ncol, width, width), F32),
        "grecv": pltpu.VMEM((ncol, slots, width, width), F32),
        "ssend": pltpu.VMEM((nrow, slots, wr, width), F32),
        "srecv": pltpu.VMEM((nrow, slots, wr, width), F32),
        "csend": pltpu.VMEM((slots, wr, width), F32),
        "crecv": pltpu.VMEM((ncol, slots, wr, width), F32),
        "nsend": pltpu.VMEM((1, width), F32),
        "nrecv": pltpu.VMEM((nrow, 1, width), F32),
        "wallt": pltpu.VMEM((4 * width, width), BF),
        "wkv": pltpu.VMEM((width, 2 * width), BF),
        "w4": pltpu.VMEM((width, width), BF),
        "wcat": pltpu.VMEM((width, 4 * width), BF),
        "augk": pltpu.VMEM((crops, total, width), BF),
        "augq": pltpu.VMEM((crops, heads, width, total), BF),
        "hot": pltpu.VMEM((crops, 16, total), BF),
        "dwt_acc": pltpu.VMEM((4 * width, width), F32),
        "dw4_acc": pltpu.VMEM((width, width), F32),
        "dg_acc": pltpu.VMEM((8, width), F32),
        "db_acc": pltpu.VMEM((heads, 8, tile), F32),
        "in_sem": dma((crops * cb,)),
        "send_sem": dma((2,)),
        "out_sem": dma((2,)),
        "osend_sem": dma((2,)),
        "misc_recv": dma((6,)),
        "misc_send": dma((6,)),
    }
    if direct:
        scratch["stage"] = pltpu.VMEM((2, rl * cb, width), F32)
        scratch["sbuf"] = pltpu.VMEM((crops, 2, cb, nrow, rl, width), BF)
        scratch["raw_sem"] = dma((crops, 2, nrow))
    *fins, red, nrm = pl.pallas_call(
        functools.partial(main_kernel, dims, tuple(scratch)),
        out_shape=(
            pltpu.VMEM(fin.shape, BF) if direct else fin,
            pltpu.VMEM(fin.shape, BF) if direct else fin,
            pltpu.VMEM((slots * ncol, wr * width), F32),
            pltpu.VMEM((1, width), F32),
        ),
        in_specs=[hbm, hbm, vmem, smem, vmem, vmem, vmem, vmem, smem],
        out_specs=(hbm, hbm, vmem, vmem),
        scratch_shapes=list(scratch.values()),
        compiler_params=pltpu.CompilerParams(
            collective_id=0, has_side_effects=True, vmem_limit_bytes=44 << 20
        ),
        name="column_attention",
    )(
        *(
            pltpu.with_memory_space_constraint(x, pltpu.HBM)
            for x in (
                *sources,
                segments,
                lengths,
                weights,
                moment_one,
                moment_two,
                gain.reshape(1, width),
                chain_bias,
            )
        )
    )
    small = (gain, gain_m, gain_v, chain_bias, bias_m, bias_v)
    ops = [red, nrm, weights, moment_one, moment_two] + [a.reshape(1, -1) for a in small]
    bigs = [fin, fin] if direct else []
    res = pl.pallas_call(
        functools.partial(step_kernel, direct),
        out_shape=bigs
        + [jax.ShapeDtypeStruct(weights.shape, F32)] * 3
        + [jax.ShapeDtypeStruct((1, width), F32)] * 3
        + [jax.ShapeDtypeStruct((1, heads), F32)] * 3,
        in_specs=[vmem] * (len(bigs) + len(ops)),
        out_specs=[hbm] * len(bigs) + [vmem] * 9,
        scratch_shapes=[dma((2,))] if direct else [],
        compiler_params=pltpu.CompilerParams(vmem_limit_bytes=12 << 20),
        name="lamb_step",
    )(*(fins if direct else ()), *ops)
    if direct:
        fins, res = res[:2], res[2:]
    else:
        fins = [jnp.swapaxes(x.reshape(crops, cl, rl, width), 1, 2) for x in fins]
    return (*fins, *res[:3], *[a.reshape(-1) for a in res[3:]])


def solution(mesh):
    big = P(None, "row", "col", None)
    shard = P(None, "row")
    return jax.shard_map(
        functools.partial(body, mesh.shape["row"], mesh.shape["col"]),
        mesh=mesh,
        in_specs=(big, big, P(), P(), shard, shard, shard) + (P(),) * 6,
        out_specs=(big, big, shard, shard, shard) + (P(),) * 6,
        check_vma=False,
    )
```

```python
import functools
import math

import jax
import jax.numpy as jnp
from jax import lax
from jax.experimental import pallas as pl
from jax.experimental.pallas import tpu as pltpu
from jax.sharding import PartitionSpec as P

STEP = 10
beta_one = 0.9
beta_two = 0.999
epsilon = 1e-06
decay = 0.01
rate = 0.25

BF = jnp.bfloat16
F32 = jnp.float32
MESH = pl.DeviceIdType.MESH
NT = ((1,), (1,))
TN = ((0,), (0,))
LOG2E = math.log2(math.e)
SEGS = 4
LEAD, AHEAD, LAG = 8, 2, 2


def dot(a, b, dims=((1,), (0,))):
    return lax.dot_general(a, b, (dims, ((), ())), preferred_element_type=F32)


def normed(z, gain):
    mean = jnp.mean(z, -1, keepdims=True)
    cen = z - mean
    var = jnp.mean(cen * cen, -1, keepdims=True)
    inv = lax.rsqrt(var + 1e-05)
    xhat = cen * inv
    return xhat, inv, (xhat * gain).astype(BF)


def attend(z, co, yown, yall, wqg_t, wkv, wkv_t, w4, wqg, augk, augq, hotk, hotq, e_ref, heads):
    qn, width = z[0].shape
    hsize = width // heads
    scale = 1.0 / math.sqrt(hsize)
    kv = dot(yall, wkv).astype(BF)
    kvT = dot(wkv_t, yall, NT).astype(BF)
    head_of = lax.broadcasted_iota(jnp.int32, (width, 1), 0) // hsize
    ones = jnp.ones((16, 2 * qn), BF)
    outs, dqgT, dkA, dkP = [], [], [], None
    dw4, db = 0.0, [0.0] * heads
    for c in range(2):
        first, packed = slice(c * qn, (c + 1) * qn), slice(2 * qn, 3 * qn)
        k = jnp.concatenate([kv[first, :width], kv[packed, :width]], 0)
        v = jnp.concatenate([kv[first, width:], kv[packed, width:]], 0)
        bothT = jnp.concatenate([kvT[:, first], kvT[:, packed]], 1)
        kT, vT = bothT[:width], bothT[width:]
        projT = dot(wqg_t, yown[c], NT)
        qT = projT[:width].astype(BF)
        gT = jax.nn.sigmoid(projT[width:])
        kaug = jnp.concatenate([k, augk[c]], 1)
        heads_a, heads_r = [], []
        for h in range(heads):
            rows = slice(h * hsize, (h + 1) * hsize)
            qaug = jnp.concatenate([jnp.where(head_of == h, qT, jnp.zeros_like(qT)), augq[c][h]], 0)
            s = dot(kaug, qaug) * (scale * LOG2E)
            e = jnp.exp2(s - jnp.max(s, 0, keepdims=True)).astype(BF)
            e_ref[h] = e
            a = dot(jnp.concatenate([vT[rows], ones], 0), e)
            r = 1.0 / a[hsize : hsize + 1]
            heads_a.append(a[:hsize] * r)
            heads_r.append(jnp.broadcast_to(r, (hsize, qn)))
        aT = jnp.concatenate(heads_a, 0)
        oT = (aT * gT).astype(BF)
        outs.append(z[c] + dot(oT, w4, TN))
        dw4 = dw4 + dot(oT, co[c])
        doT = dot(w4, co[c], NT).astype(BF).astype(F32)
        daT = (doT * gT).astype(BF).astype(F32)
        dgT = (doT * aT * gT * (1.0 - gT)).astype(BF)
        dnT = (daT * jnp.concatenate(heads_r, 0) * scale).astype(BF)
        prod = aT * dnT.astype(F32)
        dq, dk, dv = [], [], []
        for h in range(heads):
            rows = slice(h * hsize, (h + 1) * hsize)
            shift = jnp.sum(prod[rows], 0, keepdims=True)
            masked = jnp.where(head_of == h, dnT, jnp.zeros_like(dnT))
            e = e_ref[h]
            ds = (e.astype(F32) * (dot(v, masked) - shift)).astype(BF)
            x = dot(jnp.concatenate([kT[rows], hotk[c]], 0), ds)
            dq.append(x[:hsize].astype(BF))
            db[h] = db[h] + x[hsize : hsize + 8] * hotq[c][:8].astype(F32)
            dk.append(dot(qT[rows], ds, NT))
            dv.append(dot(dnT[rows], e, NT) * (1.0 / scale))
        dqgT.append(jnp.concatenate(dq + [dgT], 0))
        dkv = jnp.concatenate(dk + dv, 0)
        dkA.append(dkv[:, :qn].astype(BF))
        dkP = dkv[:, qn:] if dkP is None else dkP + dkv[:, qn:]
    dqgT = jnp.concatenate(dqgT, 1)
    dkvT = jnp.concatenate(dkA + [dkP.astype(BF)], 1)
    dwqg = dot(dqgT, jnp.concatenate(yown, 0))
    dwkv = dot(dkvT, yall)
    dy_own = jnp.transpose(dot(wqg, dqgT))
    dy_all = jnp.transpose(dot(wkv, dkvT))
    return outs, dy_own, dy_all, dwqg, dwkv, dw4, db


def moments(value, grad, first, second):
    first_new = beta_one * first + (1.0 - beta_one) * grad
    second_new = beta_two * second + (1.0 - beta_two) * grad * grad
    step_dir = (
        first_new
        / (1.0 - beta_one**STEP)
        / (jnp.sqrt(second_new / (1.0 - beta_two**STEP)) + epsilon)
        + decay * value
    )
    return (first_new, second_new, step_dir)


def main_kernel(dims, names, *refs):
    nrow, ncol, crops, cpd, gc, rl, width, heads, wr, direct = dims
    pair_ref, cot_ref, seg_ref, len_ref, w_ref, m1_ref, m2_ref, gain_ref, bias_ref = refs[:9]
    srcs = (pair_ref, cot_ref)
    s = dict(zip(names, refs[9:]))
    zin, y3, d3, own, xring, iring, yring = (s[n] for n in ("zin", "y3", "d3", "own", "xring", "iring", "yring"))
    in_sem, send_sem, ret_sem, rsend_sem = s["in_sem"], s["send_sem"], s["ret_sem"], s["rsend_sem"]
    misc_recv, misc_send, y_sem, d_sem, x_send = (
        s[n] for n in ("misc_recv", "misc_send", "y_sem", "d_sem", "x_send")
    )
    red_ref, nrm_ref = s["red"], s["nrm"]
    half = nrow // 2
    qn = half * rl
    groups = cpd // gc
    ring = xring.shape[0]
    cols = [s["col%d" % g] for g in range(groups)]
    hsize = width // heads
    scale = 1.0 / math.sqrt(hsize)
    slots = s["wrow"].shape[1]
    me = lax.axis_index("row")
    mc = lax.axis_index("col")
    side = me // half
    place = lax.rem(me, half)
    partner = (lax.rem(me + half, nrow), mc)

    def row_peer(d):
        return lax.rem(me + d, nrow)

    def col_peer(d):
        return lax.rem(mc + d, ncol)

    def near(d):
        return lax.rem(place + d, half)

    def device(w):
        return (side * half + w, mc)

    def load_group(g):
        def load(w, _):
            first = pl.multiple_of(w * cpd, gc) + g * gc
            for c in range(crops):
                for a in range(2):
                    pltpu.make_async_copy(
                        srcs[a].at[c, :, pl.ds(pl.multiple_of(first, gc), gc), :],
                        s["raw"].at[w, c, a],
                        s["raw_sem"].at[w, c, a],
                    ).start()
            return 0

        lax.fori_loop(0, half, load, 0)

    if direct:
        load_group(0)

    barrier = pltpu.get_barrier_semaphore()

    def greet_row(d, _):
        pl.semaphore_signal(barrier, inc=1, device_id=(row_peer(d), mc), device_id_type=MESH)
        return 0

    def greet_col(d, _):
        pl.semaphore_signal(barrier, inc=1, device_id=(me, col_peer(d)), device_id_type=MESH)
        return 0

    lax.fori_loop(1, nrow, greet_row, 0)
    lax.fori_loop(1, ncol, greet_col, 0)
    for j in range(wr):
        s["wtmp"][0:5, j, :] = w_ref[:, j * width : (j + 1) * width]
    for k in range(slots * ncol):
        s["wsend"][k] = (s["wtmp"][k] if k < 5 else jnp.zeros((wr, width), F32)).astype(s["wsend"].dtype)
    pl.semaphore_wait(barrier, nrow - 1 + ncol - 1)

    def remote(src, dst, send, recv, peer):
        pltpu.make_async_remote_copy(
            src, dst, send, recv, device_id=peer, device_id_type=MESH
        ).start()

    def exchange_row(src_of, dst, n):
        def push(d, _):
            p = row_peer(d)
            remote(src_of(p), dst.at[me], misc_send.at[n], misc_recv.at[n], (p, mc))
            return 0

        lax.fori_loop(1, nrow, push, 0)
        pltpu.make_async_copy(src_of(me), dst.at[me], misc_recv.at[n]).start()

    def exchange_col(src_of, dst, n):
        def push(d, _):
            p = col_peer(d)
            remote(src_of(p), dst.at[mc], misc_send.at[n], misc_recv.at[n], (me, p))
            return 0

        lax.fori_loop(1, ncol, push, 0)
        pltpu.make_async_copy(src_of(mc), dst.at[mc], misc_recv.at[n]).start()

    def landed(dst, n):
        pltpu.make_async_copy(dst, dst, misc_recv.at[n]).wait()

    def total_of(ref, n):
        return lax.fori_loop(1, n, lambda r, t: t + ref[r], ref[0])

    exchange_row(lambda p: s["wsend"].at[pl.ds(mc * slots, slots)], s["wrow"], 0)

    def column_of(u, w):
        return s["sbuf"].at[lax.rem(u, gc), :, :, w] if direct else pair_ref.at[u, :, :, w]

    def push_to(u, d):
        w = near(d)
        remote(column_of(u, w), zin.at[u, :, :, place], send_sem.at[u // gc], in_sem.at[u], device(w))

    def push_column(u):
        def to_peer(d, _):
            push_to(u, d)
            return 0

        lax.fori_loop(1, half, to_peer, 0)
        if not direct:
            pltpu.make_async_copy(column_of(u, place), zin.at[u, :, :, place], in_sem.at[u]).start()

    def push_columns(first, last):
        def at_column(u, _):
            push_column(u)
            return 0

        lax.fori_loop(first, last, at_column, 0)

    def turn(g, w, mine):
        for c in range(crops):
            for a in range(2):
                here = s["raw"].at[w, c, a]
                pltpu.make_async_copy(here, here, s["raw_sem"].at[w, c, a]).wait()
                s["stage"][a] = s["raw"][w, c, a].astype(F32).reshape(rl * gc, width)
                for j in range(gc):
                    turned = s["stage"][a, pl.ds(j, rl, stride=gc), :].astype(BF)
                    if mine:
                        zin[g * gc + j, c, a, w] = turned
                    else:
                        s["sbuf"][j, c, a, w] = turned

    if direct:

        def first_blocks(d, _):
            turn(0, near(d), False)
            push_to(0, d)
            return 0

        lax.fori_loop(1, half, first_blocks, 0)
        turn(0, place, True)
        push_columns(1, LEAD - AHEAD)
        if groups > 1:
            load_group(1)
    else:
        push_columns(0, min(LEAD - AHEAD, cpd))

    landed(s["wrow"], 0)
    exchange_col(lambda p: s["wrow"], s["wall"], 1)

    back = lax.broadcasted_iota(jnp.int32, (qn, qn), 0) + lax.broadcasted_iota(jnp.int32, (qn, qn), 1)
    s["rev"][...] = jnp.where(back == qn - 1, 1.0, 0.0).astype(BF)
    lane = lax.broadcasted_iota(jnp.int32, (1, qn), 1)
    line = lax.broadcasted_iota(jnp.int32, (width, 1), 0)
    for c in range(crops):
        low_seg, high_seg = seg_ref[c : c + 1, :qn], seg_ref[c : c + 1, qn:]
        own_seg = jnp.where(side == 0, low_seg, high_seg)
        same_low = (lax.rem(line, SEGS) == low_seg).astype(F32)
        same_high = (lax.rem(line, SEGS) == high_seg).astype(F32)
        pad = jnp.where(lane + qn >= len_ref[c], -1e30, 0.0)
        if c == 1:
            same_high = dot(same_high.astype(BF), s["rev"][...])
            pad = jnp.where(2 * qn - 1 - lane >= len_ref[c], -1e30, 0.0)
        same = jnp.concatenate([same_low, same_high], 1)
        pad = jnp.concatenate([jnp.zeros((1, qn), F32), pad], 1)
        s["hotk"][c] = jnp.where(line[:16] < SEGS, same[:16], 0.0).astype(BF)
        rowsk = jnp.where(line < 3 * SEGS, same, jnp.where(line == 3 * SEGS, pad, 0.0))
        s["augk"][c] = jnp.transpose(rowsk).astype(BF)
        same = (lax.rem(line, SEGS) == own_seg).astype(F32)
        s["hotq"][c] = jnp.where(line[:16] < SEGS, same[:16], 0.0).astype(BF)
        for h in range(heads):
            full = jnp.full((width, 1), bias_ref[h] * (1.0 / scale), F32)
            high = full.astype(BF).astype(F32)
            mid = (full - high).astype(BF).astype(F32)
            low = full - high - mid
            part = jnp.where(line < SEGS, high, jnp.where(line < 2 * SEGS, mid, low))
            rowsq = jnp.where(line < 3 * SEGS, same * part, jnp.where(line == 3 * SEGS, 1.0, 0.0))
            s["augq"][c, h] = rowsq.astype(BF)

    for name in ("dwqg_acc", "dwkv_acc", "dw4_acc", "dg_acc", "db_acc"):
        s[name][...] = jnp.zeros_like(s[name])

    landed(s["wall"], 1)
    for k in range(5):
        w = s["wall"][k // slots, :, k % slots].astype(F32).reshape(width, width)
        if k == 4:
            s["w4"][...] = w.astype(BF)
        else:
            name, at = {0: ("wqg", 0), 3: ("wqg", 1), 1: ("wkv", 0), 2: ("wkv", 1)}[k]
            s[name][:, at * width : (at + 1) * width] = w.astype(BF)
            s[name + "_t"][at * width : (at + 1) * width, :] = jnp.transpose(w).astype(BF)

    where_t = lax.broadcasted_iota(jnp.int32, (qn, 1), 0)

    def prepare(u):
        new = zin.at[u, :, :, pl.ds(0, half - 1)] if direct else zin.at[u]
        pltpu.make_async_copy(new, new, in_sem.at[u]).wait()
        at = lax.rem(u, ring)
        for c in range(crops):
            rows = slice(c * qn, (c + 1) * qn)
            xhat, inv, y = normed(zin[u, c, 0].astype(F32).reshape(qn, width), gain_ref[...])
            xring[at, rows, :] = xhat
            iring[at, rows, :] = jnp.broadcast_to(inv, (qn, width))
            yring[at, rows, :] = y

        @pl.when(side == 0)
        def _():
            y3[u, 0 : 2 * qn, :] = yring[at]
            part = y3.at[u, pl.ds(0, 2 * qn)]
            remote(part, part, x_send.at[0], y_sem.at[u], partner)

        @pl.when(side == 1)
        def _():
            y1 = dot(s["rev"][...], yring[at, qn : 2 * qn, :])
            y0 = yring[at, 0:qn, :].astype(F32)
            y3[u, 2 * qn : 3 * qn, :] = jnp.where(where_t < len_ref[0] - qn, y0, y1).astype(BF)
            part = y3.at[u, pl.ds(2 * qn, qn)]
            remote(part, part, x_send.at[0], y_sem.at[u], partner)

    def give(u, a):
        g = u // gc
        for n in range(groups):

            @pl.when(g == n)
            def _():
                here = cols[n].at[a, :, place, u - n * gc]

                def to_peer(d, _):
                    w = near(d)
                    remote(zin.at[u, :, a, w], here, rsend_sem.at[n], ret_sem.at[n], device(w))
                    return 0

                lax.fori_loop(1, half, to_peer, 0)
                pltpu.make_async_copy(zin.at[u, :, a, place], here, ret_sem.at[n]).start()

    def work(u):
        @pl.when(side == 0)
        def _():
            part = y3.at[u, pl.ds(2 * qn, qn)]
            pltpu.make_async_copy(part, part, y_sem.at[u]).wait()

        @pl.when(side == 1)
        def _():
            part = y3.at[u, pl.ds(0, 2 * qn)]
            pltpu.make_async_copy(part, part, y_sem.at[u]).wait()

        at = lax.rem(u, ring)
        outs, dy_own, dy_all, dwqg, dwkv, dw4, db = attend(
            [zin[u, c, 0].astype(F32).reshape(qn, width) for c in range(crops)],
            [zin[u, c, 1].astype(F32).reshape(qn, width).astype(BF) for c in range(crops)],
            [yring[at, c * qn : (c + 1) * qn, :] for c in range(crops)],
            y3[u],
            s["wqg_t"][...],
            s["wkv"][...],
            s["wkv_t"][...],
            s["w4"][...],
            s["wqg"][...],
            [s["augk"][c] for c in range(crops)],
            [[s["augq"][c, h] for h in range(heads)] for c in range(crops)],
            [s["hotk"][c] for c in range(crops)],
            [s["hotq"][c] for c in range(crops)],
            s["prob"],
            heads,
        )
        s["dwqg_acc"][...] += dwqg
        s["dwkv_acc"][...] += dwkv
        s["dw4_acc"][...] += dw4
        for h in range(heads):
            s["db_acc"][h] += db[h]
        for c in range(crops):
            zin[u, c, 0] = outs[c].reshape(half, rl, width).astype(BF)
        give(u, 0)

        @pl.when(side == 0)
        def _():
            own[at, 0 : 2 * qn, :] = dy_own + dy_all[0 : 2 * qn]
            d3[u, 2 * qn : 3 * qn, :] = dy_all[2 * qn :].astype(BF)
            part = d3.at[u, pl.ds(2 * qn, qn)]
            remote(part, part, x_send.at[1], d_sem.at[u], partner)

        @pl.when(side == 1)
        def _():
            own[at, 0 : 2 * qn, :] = dy_own
            own[at, 2 * qn : 3 * qn, :] = dy_all[2 * qn :]
            d3[u, 0 : 2 * qn, :] = dy_all[0 : 2 * qn].astype(BF)
            part = d3.at[u, pl.ds(0, 2 * qn)]
            remote(part, part, x_send.at[1], d_sem.at[u], partner)

    def finish(u):
        at = lax.rem(u, ring)

        @pl.when(side == 0)
        def _():
            part = d3.at[u, pl.ds(0, 2 * qn)]
            pltpu.make_async_copy(part, part, d_sem.at[u]).wait()
            own[at, 0 : 2 * qn, :] += d3[u, 0 : 2 * qn, :].astype(F32)

        @pl.when(side == 1)
        def _():
            part = d3.at[u, pl.ds(2 * qn, qn)]
            pltpu.make_async_copy(part, part, d_sem.at[u]).wait()
            both = own[at, 2 * qn : 3 * qn, :] + d3[u, 2 * qn : 3 * qn, :].astype(F32)
            mine = where_t < len_ref[0] - qn
            own[at, 0:qn, :] += jnp.where(mine, both, 0.0)
            own[at, qn : 2 * qn, :] += dot(s["rev"][...], jnp.where(mine, 0.0, both).astype(BF))

        for c in range(crops):
            rows = slice(c * qn, (c + 1) * qn)
            dy, xhat = own[at, rows, :], xring[at, rows, :]
            s["dg_acc"][0:1] += jnp.sum(dy * xhat, 0, keepdims=True)
            dx = dy * gain_ref[...]
            rest = dx - jnp.mean(dx, -1, keepdims=True) - xhat * jnp.mean(dx * xhat, -1, keepdims=True)
            grad = zin[u, c, 1].astype(F32).reshape(qn, width) + iring[at, rows, :] * rest
            zin[u, c, 1] = grad.reshape(half, rl, width).astype(BF)
        give(u, 1)

    def refill():
        sent = s["sbuf"].at[:, :, :, pl.ds(0, half - 1)]
        pltpu.make_async_copy(sent, sent, send_sem.at[0]).wait()

        def block(d, _):
            turn(1, near(d), False)
            return 0

        lax.fori_loop(1, half, block, 0)
        turn(1, place, True)

    def turn_back():
        pltpu.make_async_copy(cols[0], cols[0], ret_sem.at[0]).wait()

        def block(w, _):
            for c in range(crops):
                for a in range(2):
                    for j in range(gc):
                        s["stage"][a, pl.ds(j, rl, stride=gc), :] = cols[0][a, c, w, j].astype(F32)
                    s["fin0"][a, c, w] = s["stage"][a].reshape(rl, gc, width).astype(BF)
            return 0

        lax.fori_loop(0, half, block, 0)

    turn_at = gc + LAG + 5
    refill_at = gc - 5

    def step(n, _):
        it = n - AHEAD
        nxt = it + LEAD
        limit = gc if direct else cpd

        @pl.when(nxt < limit)
        def _():
            push_column(nxt)

        if direct and groups > 1:

            @pl.when(it == refill_at)
            def _():
                refill()
                push_columns(gc, refill_at + LEAD + 1)

            @pl.when((it > refill_at) & (nxt < cpd))
            def _():
                push_column(nxt)

        @pl.when(it + AHEAD < cpd)
        def _():
            prepare(it + AHEAD)

        @pl.when((it >= 0) & (it < cpd))
        def _():
            work(it)

        @pl.when(it >= LAG)
        def _():
            finish(it - LAG)

        if direct and groups > 1:

            @pl.when(it == turn_at)
            def _():
                turn_back()

        return 0

    lax.fori_loop(0, cpd + AHEAD + LAG, step, 0)

    gsend = s["gsend"]
    for k, (name, at) in enumerate((("dwqg_acc", 0), ("dwkv_acc", 0), ("dwkv_acc", 1), ("dwqg_acc", 1))):
        gsend[k] = jnp.transpose(s[name][at * width : (at + 1) * width, :])
    gsend[4] = s["dw4_acc"][...]
    gsend[5] = jnp.broadcast_to(s["dg_acc"][0:1], (width, width))
    spot = lax.broadcasted_iota(jnp.int32, (1, width), 1)
    dbias = jnp.zeros((1, width), F32)
    for h in range(heads):
        total_h = jnp.sum(jnp.sum(s["db_acc"][h], 0, keepdims=True), 1, keepdims=True)
        dbias = jnp.where(spot == h, total_h * (1.0 / scale), dbias)
    gsend[6] = jnp.broadcast_to(dbias, (width, width))
    for k in range(7, slots * ncol):
        gsend[k] = jnp.zeros((width, width), F32)
    exchange_col(lambda p: gsend.at[pl.ds(p * slots, slots)], s["grecv"], 2)
    landed(s["grecv"], 2)
    share = total_of(s["grecv"], ncol)
    for p in range(nrow):
        s["ssend"][p] = share[:, p * wr : (p + 1) * wr, :]
    exchange_row(lambda p: s["ssend"].at[p], s["srecv"], 3)
    landed(s["srecv"], 3)
    s["csend"][...] = total_of(s["srecv"], nrow)
    exchange_col(lambda p: s["csend"], s["crecv"], 4)
    landed(s["crecv"], 4)
    for j in range(wr):
        red_ref[:, j * width : (j + 1) * width] = s["crecv"][:, :, j, :].reshape(slots * ncol, width)
    wval = w_ref[...]
    step_w = moments(wval, red_ref[0:5, :], m1_ref[...], m2_ref[...])[2]
    row5 = lax.broadcasted_iota(jnp.int32, (5, 1), 0)
    squares = jnp.where(spot == row5, jnp.sum(wval * wval, 1, keepdims=True), 0.0)
    squares += jnp.where(spot == row5 + 8, jnp.sum(step_w * step_w, 1, keepdims=True), 0.0)
    s["nsend"][...] = jnp.sum(squares, 0, keepdims=True)
    exchange_row(lambda p: s["nsend"], s["nrecv"], 5)
    landed(s["nrecv"], 5)
    nrm_ref[...] = total_of(s["nrecv"], nrow)

    most = pl.ds(0, half - 1)
    for g in range(groups):
        if not direct or g == groups - 1:
            sent = s["sbuf"].at[:, :, :, most] if direct else pair_ref.at[:, :, :, most]
            pltpu.make_async_copy(sent, sent, send_sem.at[g]).wait()
        gone = cols[g].at[:, :, most]
        pltpu.make_async_copy(gone, gone, rsend_sem.at[g]).wait()
        if not direct or groups == 1 or g > 0:
            pltpu.make_async_copy(cols[g], cols[g], ret_sem.at[g]).wait()

    @pl.when(side == 0)
    def _():
        part = y3.at[:, pl.ds(0, 2 * qn)]
        pltpu.make_async_copy(part, part, x_send.at[0]).wait()
        part = d3.at[:, pl.ds(2 * qn, qn)]
        pltpu.make_async_copy(part, part, x_send.at[1]).wait()

    @pl.when(side == 1)
    def _():
        part = y3.at[:, pl.ds(2 * qn, qn)]
        pltpu.make_async_copy(part, part, x_send.at[0]).wait()
        part = d3.at[:, pl.ds(0, 2 * qn)]
        pltpu.make_async_copy(part, part, x_send.at[1]).wait()

    for n, name in enumerate(("wrow", "wall", "grecv", "srecv", "crecv", "nrecv")):
        sent = s[name].at[pl.ds(0, s[name].shape[0] - 1)]
        pltpu.make_async_copy(sent, sent, misc_send.at[n]).wait()


def step_kernel(direct, *refs):
    if direct:
        fins, refs = refs[0:2], refs[2:]
    red_ref, nrm_ref, w_ref, m1_ref, m2_ref, gain_ref, gm_ref, gv_ref, bias_ref, bm_ref, bv_ref = refs[:11]
    refs = refs[11:]
    if direct:
        bigs, refs = refs[0:2], refs[2:11] + refs[11:]
        refs, (slot, stage, sem) = refs[:9], refs[9:]
        _, crops, half, rl, gc, width = fins[0].shape
        cpd = 2 * gc
        copies = []

        def put(n, src, a, c, w, g):
            there = bigs[a].at[c, :, pl.ds(w * cpd + g * gc, gc), :]
            copy = pltpu.make_async_copy(src, there, sem.at[n])
            copy.start()
            copies.append(copy)

        blocks = [(a, c, w) for w in range(half) for c in range(crops) for a in range(2)]
        for n, (a, c, w) in enumerate(blocks):
            put(n, fins[0].at[a, c, w], a, c, w, 0)
        for n, (a, c, w) in enumerate(blocks):
            for j in range(gc):
                stage[n % 2, pl.ds(j, rl, stride=gc), :] = fins[1][a, c, w, j].astype(F32)
            slot[n] = stage[n % 2].reshape(rl, gc, width).astype(BF)
            put(len(blocks) + n, slot.at[n], a, c, w, 1)
    nw_ref, n1_ref, n2_ref, ng_ref, ngm_ref, ngv_ref, nb_ref, nbm_ref, nbv_ref = refs
    width = gain_ref.shape[1]
    heads = bias_ref.shape[1]
    wval = w_ref[...]
    first, second, step_w = moments(wval, red_ref[0:5, :], m1_ref[...], m2_ref[...])
    spot = lax.broadcasted_iota(jnp.int32, (1, width), 1)
    place = lax.broadcasted_iota(jnp.int32, (5, 1), 0)
    value_sq = jnp.sum(jnp.where(spot == place, nrm_ref[...], 0.0), 1, keepdims=True)
    step_sq = jnp.sum(jnp.where(spot == place + 8, nrm_ref[...], 0.0), 1, keepdims=True)
    nw_ref[...] = wval - rate * (jnp.sqrt(value_sq) / jnp.sqrt(step_sq)) * step_w
    n1_ref[...] = first
    n2_ref[...] = second
    for row, n, own in (
        (5, width, (gain_ref, gm_ref, gv_ref, ng_ref, ngm_ref, ngv_ref)),
        (6, heads, (bias_ref, bm_ref, bv_ref, nb_ref, nbm_ref, nbv_ref)),
    ):
        val = own[0][...]
        first, second, step_v = moments(val, red_ref[row : row + 1, 0:n], own[1][...], own[2][...])
        ratio = jnp.sqrt(jnp.sum(val * val, 1, keepdims=True)) / jnp.sqrt(
            jnp.sum(step_v * step_v, 1, keepdims=True)
        )
        own[3][...] = val - rate * ratio * step_v
        own[4][...] = first
        own[5][...] = second
    if direct:
        for copy in copies:
            copy.wait()


def body(
    nrow,
    ncol,
    pair,
    cotangent,
    segments,
    lengths,
    weights,
    moment_one,
    moment_two,
    gain,
    gain_m,
    gain_v,
    chain_bias,
    bias_m,
    bias_v,
):
    crops, rl, cl, width = pair.shape
    heads = chain_bias.shape[0]
    half = nrow // 2
    qn = half * rl
    cpd = cl // half
    wr = weights.shape[1] // width
    slots = -(-8 // ncol)
    direct = cpd == 32 and rl % 16 == 0
    gc = 16 if direct else cpd
    groups = cpd // gc
    dims = (nrow, ncol, crops, cpd, gc, rl, width, heads, wr, direct)
    wtype = BF if wr % 16 == 0 else F32
    ring = AHEAD + LAG + 1
    hbm = pl.BlockSpec(memory_space=pl.ANY)
    vmem = pl.BlockSpec(memory_space=pltpu.VMEM)
    smem = pl.BlockSpec(memory_space=pltpu.SMEM)
    dma = pltpu.SemaphoreType.DMA
    held = (2, crops, half, gc, rl, width)
    outs = {"red": pltpu.VMEM((slots * ncol, wr * width), F32), "nrm": pltpu.VMEM((1, width), F32)}
    scratch = {
        "zin": pltpu.VMEM((cpd, crops, 2, half, rl, width), BF),
        "y3": pltpu.VMEM((cpd, 3 * qn, width), BF),
        "d3": pltpu.VMEM((cpd, 3 * qn, width), BF),
        "own": pltpu.VMEM((ring, 3 * qn, width), F32),
        "xring": pltpu.VMEM((ring, 2 * qn, width), F32),
        "iring": pltpu.VMEM((ring, 2 * qn, width), F32),
        "yring": pltpu.VMEM((ring, 2 * qn, width), BF),
        "prob": pltpu.VMEM((heads, 2 * qn, qn), BF),
        "rev": pltpu.VMEM((qn, qn), BF),
        "wtmp": pltpu.VMEM((8, wr, width), F32),
        "wsend": pltpu.VMEM((slots * ncol, wr, width), wtype),
        "wrow": pltpu.VMEM((nrow, slots, wr, width), wtype),
        "wall": pltpu.VMEM((ncol, nrow, slots, wr, width), wtype),
        "gsend": pltpu.VMEM((slots * ncol, width, width), F32),
        "grecv": pltpu.VMEM((ncol, slots, width, width), F32),
        "ssend": pltpu.VMEM((nrow, slots, wr, width), F32),
        "srecv": pltpu.VMEM((nrow, slots, wr, width), F32),
        "csend": pltpu.VMEM((slots, wr, width), F32),
        "crecv": pltpu.VMEM((ncol, slots, wr, width), F32),
        "nsend": pltpu.VMEM((1, width), F32),
        "nrecv": pltpu.VMEM((nrow, 1, width), F32),
        "wqg": pltpu.VMEM((width, 2 * width), BF),
        "wkv": pltpu.VMEM((width, 2 * width), BF),
        "wqg_t": pltpu.VMEM((2 * width, width), BF),
        "wkv_t": pltpu.VMEM((2 * width, width), BF),
        "w4": pltpu.VMEM((width, width), BF),
        "augk": pltpu.VMEM((crops, 2 * qn, width), BF),
        "augq": pltpu.VMEM((crops, heads, width, qn), BF),
        "hotk": pltpu.VMEM((crops, 16, 2 * qn), BF),
        "hotq": pltpu.VMEM((crops, 16, qn), BF),
        "dwqg_acc": pltpu.VMEM((2 * width, width), F32),
        "dwkv_acc": pltpu.VMEM((2 * width, width), F32),
        "dw4_acc": pltpu.VMEM((width, width), F32),
        "dg_acc": pltpu.VMEM((8, width), F32),
        "db_acc": pltpu.VMEM((heads, 8, qn), F32),
        "in_sem": dma((cpd,)),
        "y_sem": dma((cpd,)),
        "d_sem": dma((cpd,)),
        "send_sem": dma((groups,)),
        "ret_sem": dma((groups,)),
        "rsend_sem": dma((groups,)),
        "x_send": dma((2,)),
        "misc_recv": dma((6,)),
        "misc_send": dma((6,)),
    }
    if direct:
        sources = (pair, cotangent)
        outs["fin0"] = pltpu.VMEM((2, crops, half, rl, gc, width), BF)
        outs["col1"] = pltpu.VMEM(held, BF)
        scratch["col0"] = pltpu.VMEM(held, BF)
        scratch["raw"] = pltpu.VMEM((half, crops, 2, rl, gc, width), BF)
        scratch["sbuf"] = pltpu.VMEM((gc, crops, 2, half, rl, width), BF)
        scratch["stage"] = pltpu.VMEM((2, rl * gc, width), F32)
        scratch["raw_sem"] = dma((half, crops, 2))
    else:
        both = jnp.stack([pair, cotangent], 1).reshape(crops, 2, rl, half, cpd, width)
        sources = (jnp.transpose(both, (4, 0, 1, 3, 2, 5)), cotangent)
        outs["col0"] = pltpu.VMEM(held, BF)
    names = tuple(outs) + tuple(scratch)
    res1 = pl.pallas_call(
        functools.partial(main_kernel, dims, names),
        out_shape=tuple(outs.values()),
        in_specs=[hbm, hbm, vmem, smem, vmem, vmem, vmem, vmem, smem],
        out_specs=(vmem,) * len(outs),
        scratch_shapes=list(scratch.values()),
        compiler_params=pltpu.CompilerParams(
            collective_id=0, has_side_effects=True, vmem_limit_bytes=50 << 20
        ),
        name="column_attention",
    )(
        *(
            pltpu.with_memory_space_constraint(x, pltpu.HBM)
            for x in (
                *sources,
                segments,
                lengths,
                weights,
                moment_one,
                moment_two,
                gain.reshape(1, width),
                chain_bias,
            )
        )
    )
    res1 = dict(zip(outs, res1))
    small = (gain, gain_m, gain_v, chain_bias, bias_m, bias_v)
    ops = [res1["red"], res1["nrm"], weights, moment_one, moment_two] + [a.reshape(1, -1) for a in small]
    fin = jax.ShapeDtypeStruct(pair.shape, BF)
    bigs = [fin, fin] if direct else []
    count = 2 * crops * half
    res = pl.pallas_call(
        functools.partial(step_kernel, direct),
        out_shape=bigs
        + [jax.ShapeDtypeStruct(weights.shape, F32)] * 3
        + [jax.ShapeDtypeStruct((1, width), F32)] * 3
        + [jax.ShapeDtypeStruct((1, heads), F32)] * 3,
        in_specs=[vmem] * (len(bigs) + len(ops)),
        out_specs=[hbm] * len(bigs) + [vmem] * 9,
        scratch_shapes=[
            pltpu.VMEM((count, rl, gc, width), BF),
            pltpu.VMEM((2, rl * gc, width), F32),
            dma((2 * count,)),
        ]
        if direct
        else [],
        compiler_params=pltpu.CompilerParams(vmem_limit_bytes=16 << 20),
        name="lamb_step",
    )(*((res1["fin0"], res1["col1"]) if direct else ()), *ops)
    if direct:
        fins, res = res[:2], res[2:]
    else:
        back = res1["col0"].reshape(2, crops, cl, rl, width)
        fins = [jnp.swapaxes(back[a], 1, 2) for a in range(2)]
    return (*fins, *res[:3], *[a.reshape(-1) for a in res[3:]])


def solution(mesh):
    big = P(None, "row", "col", None)
    shard = P(None, "row")
    return jax.shard_map(
        functools.partial(body, mesh.shape["row"], mesh.shape["col"]),
        mesh=mesh,
        in_specs=(big, big, P(), P(), shard, shard, shard) + (P(),) * 6,
        out_specs=(big, big, shard, shard, shard) + (P(),) * 6,
        check_vma=False,
    )
```

```python
import functools
import math

import jax
import jax.numpy as jnp
from jax import lax
from jax.experimental import pallas as pl
from jax.experimental.pallas import tpu as pltpu
from jax.sharding import PartitionSpec as P

STEP = 10
beta_one = 0.9
beta_two = 0.999
epsilon = 1e-06
decay = 0.01
rate = 0.25

BF = jnp.bfloat16
F32 = jnp.float32
MESH = pl.DeviceIdType.MESH
NT = ((1,), (1,))
TN = ((0,), (0,))
LOG2E = math.log2(math.e)
SEGS = 4
LEAD, AHEAD, LAG = 8, 2, 2
LIGHT = 24


def dot(a, b, dims=((1,), (0,))):
    return lax.dot_general(a, b, (dims, ((), ())), preferred_element_type=F32)


def normed(z, gain):
    mean = jnp.mean(z, -1, keepdims=True)
    cen = z - mean
    var = jnp.mean(cen * cen, -1, keepdims=True)
    inv = lax.rsqrt(var + 1e-05)
    xhat = cen * inv
    return xhat, inv, (xhat * gain).astype(BF)


def attend(z, co, yown, yall, wqg_t, wkv, wkv_t, w4, wqg, augk, augq, hotk, hotq, heads):
    qn, width = z[0].shape
    hsize = width // heads
    scale = 1.0 / math.sqrt(hsize)
    kv = dot(yall, wkv).astype(BF)
    kvT = dot(wkv_t, yall, NT).astype(BF)
    head_of = lax.broadcasted_iota(jnp.int32, (width, 1), 0) // hsize
    ones = jnp.ones((16, 2 * qn), BF)
    outs, dqgT, dkA, dkP = [], [], [], None
    dw4, db = 0.0, [0.0] * heads
    for c in range(2):
        first, packed = slice(c * qn, (c + 1) * qn), slice(2 * qn, 3 * qn)
        k = jnp.concatenate([kv[first, :width], kv[packed, :width]], 0)
        v = jnp.concatenate([kv[first, width:], kv[packed, width:]], 0)
        bothT = jnp.concatenate([kvT[:, first], kvT[:, packed]], 1)
        kT, vT = bothT[:width], bothT[width:]
        projT = dot(wqg_t, yown[c], NT)
        qT = projT[:width].astype(BF)
        gT = jax.nn.sigmoid(projT[width:])
        kaug = jnp.concatenate([k, augk[c]], 1)
        row16 = lax.broadcasted_iota(jnp.int32, (16, 1), 0)
        tile_k = jnp.concatenate([hotk[c][:4].astype(F32)] * 4, 0)
        tile_q = jnp.concatenate([hotq[c][:4].astype(F32)] * 4, 0)
        hk = [jnp.where(row16 // 4 == h, tile_k, 0.0).astype(BF) for h in range(heads)]
        hq = [jnp.where(row16 // 4 == h, tile_q, 0.0) for h in range(heads)]
        es = []
        for h in range(heads):
            qaug = jnp.concatenate([jnp.where(head_of == h, qT, jnp.zeros_like(qT)), augq[c][h]], 0)
            s = dot(kaug, qaug) * (scale * LOG2E)
            e = jnp.exp2(s - jnp.max(s, 0, keepdims=True)).astype(BF)
            es.append(e)
        e_all = jnp.concatenate(es, 0)
        one_row = lax.broadcasted_iota(jnp.int32, (16, 1), 0)
        lhs = [
            jnp.concatenate(
                [
                    jnp.where(head_of == h, vT, jnp.zeros_like(vT)),
                    jnp.broadcast_to(jnp.where(one_row == h, 1.0, 0.0).astype(BF), (16, 2 * qn)),
                ],
                0,
            )
            for h in range(heads)
        ]
        a = dot(jnp.concatenate(lhs, 1), e_all)
        r = 1.0 / a[width : width + heads]
        rb = jnp.concatenate([jnp.broadcast_to(r[h : h + 1], (hsize, qn)) for h in range(heads)], 0)
        aT = a[:width] * rb
        oT = (aT * gT).astype(BF)
        outs.append(z[c] + dot(oT, w4, TN))
        dw4 = dw4 + dot(oT, co[c])
        doT = dot(w4, co[c], NT).astype(BF).astype(F32)
        daT = (doT * gT).astype(BF).astype(F32)
        dgT = (doT * aT * gT * (1.0 - gT)).astype(BF)
        dnT = (daT * rb * scale).astype(BF)
        prod = aT * dnT.astype(F32)
        dss, dk, dv, lhs = [], [], [], []
        dps = dot(v, jnp.concatenate([jnp.where(head_of == h, dnT, jnp.zeros_like(dnT)) for h in range(heads)], 1))
        for h in range(heads):
            rows = slice(h * hsize, (h + 1) * hsize)
            shift = jnp.sum(prod[rows], 0, keepdims=True)
            e = es[h]
            ds = (e.astype(F32) * (dps[:, h * qn : (h + 1) * qn] - shift)).astype(BF)
            dss.append(ds)
            dk.append(dot(qT[rows], ds, NT))
            dv.append(dot(dnT[rows], e, NT) * (1.0 / scale))
            lhs.append(
                jnp.concatenate(
                    [jnp.where(head_of == h, kT, jnp.zeros_like(kT)), hk[h]], 0
                )
            )
        x = dot(jnp.concatenate(lhs, 1), jnp.concatenate(dss, 0))
        for h in range(heads):
            db[h] = db[h] + (x[width : width + 16] * hq[h])[:8] + (x[width : width + 16] * hq[h])[8:]
        dqgT.append(jnp.concatenate([x[:width].astype(BF), dgT], 0))
        dkv = jnp.concatenate(dk + dv, 0)
        dkA.append(dkv[:, :qn].astype(BF))
        dkP = dkv[:, qn:] if dkP is None else dkP + dkv[:, qn:]
    dqgT = jnp.concatenate(dqgT, 1)
    dkvT = jnp.concatenate(dkA + [dkP.astype(BF)], 1)
    dwqg = dot(dqgT, jnp.concatenate(yown, 0))
    dwkv = dot(dkvT, yall)
    dy_own = jnp.transpose(dot(wqg, dqgT))
    dy_all = jnp.transpose(dot(wkv, dkvT))
    return outs, dy_own, dy_all, dwqg, dwkv, dw4, db


def moments(value, grad, first, second):
    first_new = beta_one * first + (1.0 - beta_one) * grad
    second_new = beta_two * second + (1.0 - beta_two) * grad * grad
    step_dir = (
        first_new
        / (1.0 - beta_one**STEP)
        / (jnp.sqrt(second_new / (1.0 - beta_two**STEP)) + epsilon)
        + decay * value
    )
    return (first_new, second_new, step_dir)


def main_kernel(dims, names, *refs):
    nrow, ncol, crops, light, heavy, rl, width, heads, wr, direct = dims
    pair_ref, cot_ref, seg_ref, len_ref, w_ref, m1_ref, m2_ref, gain_ref, bias_ref = refs[:9]
    srcs = (pair_ref, cot_ref)
    s = dict(zip(names, refs[9:]))
    zin, y3, d3, own, xring, iring, yring = (s[n] for n in ("zin", "y3", "d3", "own", "xring", "iring", "yring"))
    in_sem, send_sem, ret_sem, rsend_sem = s["in_sem"], s["send_sem"], s["ret_sem"], s["rsend_sem"]
    misc_recv, misc_send, y_sem, d_sem, x_send = (
        s[n] for n in ("misc_recv", "misc_send", "y_sem", "d_sem", "x_send")
    )
    red_ref, nrm_ref = s["red"], s["nrm"]
    half = nrow // 2
    qn = half * rl
    gc = 16
    ring = xring.shape[0]
    cols = s["cols"]
    hsize = width // heads
    scale = 1.0 / math.sqrt(hsize)
    slots = s["wrow"].shape[1]
    me = lax.axis_index("row")
    mc = lax.axis_index("col")
    side = me // half
    place = lax.rem(me, half)

    def rank_of(at_side, w):
        return lax.rem(w + at_side * (half // 2), half)

    def first_of(rank):
        near_rank = rank - half // 2
        return jnp.where(near_rank < 0, rank * light, (half // 2) * light + near_rank * heavy)

    rank = rank_of(side, place)
    is_heavy = rank >= half // 2
    base = first_of(rank)
    partner = ((1 - side) * half + rank_of(1 - side, rank), mc)

    def active(heavy_one, n):
        return heavy_one | (((n + 1) * light) // heavy > (n * light) // heavy)

    def unit_of(heavy_one, n):
        return jnp.where(heavy_one, n, (n * light) // heavy)

    def row_peer(d):
        return lax.rem(me + d, nrow)

    def col_peer(d):
        return lax.rem(mc + d, ncol)

    def near(d):
        return lax.rem(place + d, half)

    def device(w):
        return (side * half + w, mc)

    def load_block(b, slot):
        for c in range(crops):
            for a in range(2):
                pltpu.make_async_copy(
                    srcs[a].at[c, :, pl.ds(b * gc, gc), :],
                    s["raw"].at[slot, c, a],
                    s["raw_sem"].at[slot, c, a],
                ).start()

    if direct:
        starts = [r * light for r in range(half // 2)]
        starts += [(half // 2) * light + r * heavy for r in range(half // 2)]
        early = sorted({(x + n) // gc for x in starts for n in range(LEAD)})
        order = early + [b for b in range(cols.shape[2] // gc) if b not in early]
        nslot = s["raw"].shape[0]
        for n in range(nslot):
            load_block(order[n], n)

    barrier = pltpu.get_barrier_semaphore()

    def greet_row(d, _):
        pl.semaphore_signal(barrier, inc=1, device_id=(row_peer(d), mc), device_id_type=MESH)
        return 0

    def greet_col(d, _):
        pl.semaphore_signal(barrier, inc=1, device_id=(me, col_peer(d)), device_id_type=MESH)
        return 0

    lax.fori_loop(1, nrow, greet_row, 0)
    lax.fori_loop(1, ncol, greet_col, 0)
    for j in range(wr):
        s["wtmp"][0:5, j, :] = w_ref[:, j * width : (j + 1) * width]
    for k in range(slots * ncol):
        s["wsend"][k] = (s["wtmp"][k] if k < 5 else jnp.zeros((wr, width), F32)).astype(s["wsend"].dtype)
    pl.semaphore_wait(barrier, nrow - 1 + ncol - 1)

    def remote(src, dst, send, recv, peer):
        pltpu.make_async_remote_copy(
            src, dst, send, recv, device_id=peer, device_id_type=MESH
        ).start()

    def exchange_row(src_of, dst, n):
        def push(d, _):
            p = row_peer(d)
            remote(src_of(p), dst.at[me], misc_send.at[n], misc_recv.at[n], (p, mc))
            return 0

        lax.fori_loop(1, nrow, push, 0)
        pltpu.make_async_copy(src_of(me), dst.at[me], misc_recv.at[n]).start()

    def exchange_col(src_of, dst, n):
        def push(d, _):
            p = col_peer(d)
            remote(src_of(p), dst.at[mc], misc_send.at[n], misc_recv.at[n], (me, p))
            return 0

        lax.fori_loop(1, ncol, push, 0)
        pltpu.make_async_copy(src_of(mc), dst.at[mc], misc_recv.at[n]).start()

    def landed(dst, n):
        pltpu.make_async_copy(dst, dst, misc_recv.at[n]).wait()

    def total_of(ref, n):
        return lax.fori_loop(1, n, lambda r, t: t + ref[r], ref[0])

    exchange_row(lambda p: s["wsend"].at[pl.ds(mc * slots, slots)], s["wrow"], 0)

    def column_of(col):
        return s["sbuf"].at[col] if direct else pair_ref.at[col]

    def push_turn(n):
        def to_peer(d, _):
            w = near(d)
            there = rank_of(side, w)
            to_heavy = there >= half // 2
            u = unit_of(to_heavy, n)

            @pl.when(active(to_heavy, n))
            def _():
                src = column_of(first_of(there) + u)
                remote(src, zin.at[u, :, :, place], send_sem.at[0], in_sem.at[u], device(w))

            return 0

        lax.fori_loop(1, half, to_peer, 0)
        mine = unit_of(is_heavy, n)

        @pl.when(active(is_heavy, n))
        def _():
            src = column_of(base + mine)
            pltpu.make_async_copy(src, zin.at[mine, :, :, place], in_sem.at[mine]).start()

    def push_turns(first, last):
        def at_turn(n, _):
            push_turn(n)
            return 0

        lax.fori_loop(first, last, at_turn, 0)

    def turn_block(n):
        b, slot = order[n], n % nslot
        for c in range(crops):
            for a in range(2):
                here = s["raw"].at[slot, c, a]
                pltpu.make_async_copy(here, here, s["raw_sem"].at[slot, c, a]).wait()
                s["stage"][a] = s["raw"][slot, c, a].astype(F32).reshape(rl * gc, width)
                for j in range(gc):
                    s["sbuf"][b * gc + j, c, a] = s["stage"][a, pl.ds(j, rl, stride=gc), :].astype(BF)
        if n + nslot < len(order):
            load_block(order[n + nslot], slot)

    if direct:
        for n in range(len(early)):
            turn_block(n)
    push_turns(0, LEAD - AHEAD)
    if direct:
        for n in range(len(early), len(order)):
            turn_block(n)

    landed(s["wrow"], 0)
    exchange_col(lambda p: s["wrow"], s["wall"], 1)

    back = lax.broadcasted_iota(jnp.int32, (qn, qn), 0) + lax.broadcasted_iota(jnp.int32, (qn, qn), 1)
    s["rev"][...] = jnp.where(back == qn - 1, 1.0, 0.0).astype(BF)
    lane = lax.broadcasted_iota(jnp.int32, (1, qn), 1)
    line = lax.broadcasted_iota(jnp.int32, (width, 1), 0)
    for c in range(crops):
        low_seg, high_seg = seg_ref[c : c + 1, :qn], seg_ref[c : c + 1, qn:]
        own_seg = jnp.where(side == 0, low_seg, high_seg)
        same_low = (lax.rem(line, SEGS) == low_seg).astype(F32)
        same_high = (lax.rem(line, SEGS) == high_seg).astype(F32)
        pad = jnp.where(lane + qn >= len_ref[c], -1e30, 0.0)
        if c == 1:
            same_high = dot(same_high.astype(BF), s["rev"][...])
            pad = jnp.where(2 * qn - 1 - lane >= len_ref[c], -1e30, 0.0)
        same = jnp.concatenate([same_low, same_high], 1)
        pad = jnp.concatenate([jnp.zeros((1, qn), F32), pad], 1)
        s["hotk"][c] = jnp.where(line[:16] < SEGS, same[:16], 0.0).astype(BF)
        rowsk = jnp.where(line < 3 * SEGS, same, jnp.where(line == 3 * SEGS, pad, 0.0))
        s["augk"][c] = jnp.transpose(rowsk).astype(BF)
        same = (lax.rem(line, SEGS) == own_seg).astype(F32)
        s["hotq"][c] = jnp.where(line[:16] < SEGS, same[:16], 0.0).astype(BF)
        for h in range(heads):
            full = jnp.full((width, 1), bias_ref[h] * (1.0 / scale), F32)
            high = full.astype(BF).astype(F32)
            mid = (full - high).astype(BF).astype(F32)
            low = full - high - mid
            part = jnp.where(line < SEGS, high, jnp.where(line < 2 * SEGS, mid, low))
            rowsq = jnp.where(line < 3 * SEGS, same * part, jnp.where(line == 3 * SEGS, 1.0, 0.0))
            s["augq"][c, h] = rowsq.astype(BF)

    for name in ("dwqg_acc", "dwkv_acc", "dw4_acc", "dg_acc", "db_acc"):
        s[name][...] = jnp.zeros_like(s[name])

    landed(s["wall"], 1)
    for k in range(5):
        w = s["wall"][k // slots, :, k % slots].astype(F32).reshape(width, width)
        if k == 4:
            s["w4"][...] = w.astype(BF)
        else:
            name, at = {0: ("wqg", 0), 3: ("wqg", 1), 1: ("wkv", 0), 2: ("wkv", 1)}[k]
            s[name][:, at * width : (at + 1) * width] = w.astype(BF)
            s[name + "_t"][at * width : (at + 1) * width, :] = jnp.transpose(w).astype(BF)

    where_t = lax.broadcasted_iota(jnp.int32, (qn, 1), 0)

    def prepare(u, at):
        pltpu.make_async_copy(zin.at[u], zin.at[u], in_sem.at[u]).wait()
        for c in range(crops):
            rows = slice(c * qn, (c + 1) * qn)
            xhat, inv, y = normed(zin[u, c, 0].astype(F32).reshape(qn, width), gain_ref[...])
            xring[at, rows, :] = xhat
            iring[at, rows, :] = jnp.broadcast_to(inv, (qn, width))
            yring[at, rows, :] = y

        @pl.when(side == 0)
        def _():
            y3[u, 0 : 2 * qn, :] = yring[at]
            part = y3.at[u, pl.ds(0, 2 * qn)]
            remote(part, part, x_send.at[0], y_sem.at[u], partner)

        @pl.when(side == 1)
        def _():
            y1 = dot(s["rev"][...], yring[at, qn : 2 * qn, :])
            y0 = yring[at, 0:qn, :].astype(F32)
            y3[u, 2 * qn : 3 * qn, :] = jnp.where(where_t < len_ref[0] - qn, y0, y1).astype(BF)
            part = y3.at[u, pl.ds(2 * qn, qn)]
            remote(part, part, x_send.at[0], y_sem.at[u], partner)

    def give(u, a):
        here = cols.at[a, :, base + u]

        def to_peer(d, _):
            w = near(d)
            remote(zin.at[u, :, a, w], here, rsend_sem.at[0], ret_sem.at[0], device(w))
            return 0

        lax.fori_loop(1, half, to_peer, 0)
        pltpu.make_async_copy(zin.at[u, :, a, place], here, ret_sem.at[0]).start()

    def work(u, at):
        @pl.when(side == 0)
        def _():
            part = y3.at[u, pl.ds(2 * qn, qn)]
            pltpu.make_async_copy(part, part, y_sem.at[u]).wait()

        @pl.when(side == 1)
        def _():
            part = y3.at[u, pl.ds(0, 2 * qn)]
            pltpu.make_async_copy(part, part, y_sem.at[u]).wait()

        outs, dy_own, dy_all, dwqg, dwkv, dw4, db = attend(
            [zin[u, c, 0].astype(F32).reshape(qn, width) for c in range(crops)],
            [zin[u, c, 1].astype(F32).reshape(qn, width).astype(BF) for c in range(crops)],
            [yring[at, c * qn : (c + 1) * qn, :] for c in range(crops)],
            y3[u],
            s["wqg_t"][...],
            s["wkv"][...],
            s["wkv_t"][...],
            s["w4"][...],
            s["wqg"][...],
            [s["augk"][c] for c in range(crops)],
            [[s["augq"][c, h] for h in range(heads)] for c in range(crops)],
            [s["hotk"][c] for c in range(crops)],
            [s["hotq"][c] for c in range(crops)],
            heads,
        )
        s["dwqg_acc"][...] += dwqg
        s["dwkv_acc"][...] += dwkv
        s["dw4_acc"][...] += dw4
        for h in range(heads):
            s["db_acc"][h] += db[h]
        for c in range(crops):
            zin[u, c, 0] = outs[c].reshape(half, rl, width).astype(BF)
        give(u, 0)

        @pl.when(side == 0)
        def _():
            own[at, 0 : 2 * qn, :] = dy_own + dy_all[0 : 2 * qn]
            d3[u, 2 * qn : 3 * qn, :] = dy_all[2 * qn :].astype(BF)
            part = d3.at[u, pl.ds(2 * qn, qn)]
            remote(part, part, x_send.at[1], d_sem.at[u], partner)

        @pl.when(side == 1)
        def _():
            own[at, 0 : 2 * qn, :] = dy_own
            own[at, 2 * qn : 3 * qn, :] = dy_all[2 * qn :]
            d3[u, 0 : 2 * qn, :] = dy_all[0 : 2 * qn].astype(BF)
            part = d3.at[u, pl.ds(0, 2 * qn)]
            remote(part, part, x_send.at[1], d_sem.at[u], partner)

    def finish(u, at):

        @pl.when(side == 0)
        def _():
            part = d3.at[u, pl.ds(0, 2 * qn)]
            pltpu.make_async_copy(part, part, d_sem.at[u]).wait()
            own[at, 0 : 2 * qn, :] += d3[u, 0 : 2 * qn, :].astype(F32)

        @pl.when(side == 1)
        def _():
            part = d3.at[u, pl.ds(2 * qn, qn)]
            pltpu.make_async_copy(part, part, d_sem.at[u]).wait()
            both = own[at, 2 * qn : 3 * qn, :] + d3[u, 2 * qn : 3 * qn, :].astype(F32)
            mine = where_t < len_ref[0] - qn
            own[at, 0:qn, :] += jnp.where(mine, both, 0.0)
            own[at, qn : 2 * qn, :] += dot(s["rev"][...], jnp.where(mine, 0.0, both).astype(BF))

        for c in range(crops):
            rows = slice(c * qn, (c + 1) * qn)
            dy, xhat = own[at, rows, :], xring[at, rows, :]
            s["dg_acc"][0:1] += jnp.sum(dy * xhat, 0, keepdims=True)
            dx = dy * gain_ref[...]
            rest = dx - jnp.mean(dx, -1, keepdims=True) - xhat * jnp.mean(dx * xhat, -1, keepdims=True)
            grad = zin[u, c, 1].astype(F32).reshape(qn, width) + iring[at, rows, :] * rest
            zin[u, c, 1] = grad.reshape(half, rl, width).astype(BF)
        give(u, 1)

    def step(n, _):
        def at_turn(t, act):
            @pl.when((t >= 0) & (t < heavy) & active(is_heavy, t))
            def _():
                act(unit_of(is_heavy, t), lax.rem(t, ring))

        @pl.when(n - AHEAD + LEAD < heavy)
        def _():
            push_turn(n - AHEAD + LEAD)

        at_turn(n, prepare)
        at_turn(n - AHEAD, work)
        at_turn(n - AHEAD - LAG, finish)
        return 0

    lax.fori_loop(0, heavy + AHEAD + LAG, step, 0)

    gsend = s["gsend"]
    for k, (name, at) in enumerate((("dwqg_acc", 0), ("dwkv_acc", 0), ("dwkv_acc", 1), ("dwqg_acc", 1))):
        gsend[k] = jnp.transpose(s[name][at * width : (at + 1) * width, :])
    gsend[4] = s["dw4_acc"][...]
    gsend[5] = jnp.broadcast_to(s["dg_acc"][0:1], (width, width))
    spot = lax.broadcasted_iota(jnp.int32, (1, width), 1)
    dbias = jnp.zeros((1, width), F32)
    for h in range(heads):
        total_h = jnp.sum(jnp.sum(s["db_acc"][h], 0, keepdims=True), 1, keepdims=True)
        dbias = jnp.where(spot == h, total_h * (1.0 / scale), dbias)
    gsend[6] = jnp.broadcast_to(dbias, (width, width))
    for k in range(7, slots * ncol):
        gsend[k] = jnp.zeros((width, width), F32)
    exchange_col(lambda p: gsend.at[pl.ds(p * slots, slots)], s["grecv"], 2)
    landed(s["grecv"], 2)
    share = total_of(s["grecv"], ncol)
    for p in range(nrow):
        s["ssend"][p] = share[:, p * wr : (p + 1) * wr, :]
    exchange_row(lambda p: s["ssend"].at[p], s["srecv"], 3)
    landed(s["srecv"], 3)
    s["csend"][...] = total_of(s["srecv"], nrow)
    exchange_col(lambda p: s["csend"], s["crecv"], 4)
    landed(s["crecv"], 4)
    for j in range(wr):
        red_ref[:, j * width : (j + 1) * width] = s["crecv"][:, :, j, :].reshape(slots * ncol, width)
    wval = w_ref[...]
    step_w = moments(wval, red_ref[0:5, :], m1_ref[...], m2_ref[...])[2]
    row5 = lax.broadcasted_iota(jnp.int32, (5, 1), 0)
    squares = jnp.where(spot == row5, jnp.sum(wval * wval, 1, keepdims=True), 0.0)
    squares += jnp.where(spot == row5 + 8, jnp.sum(step_w * step_w, 1, keepdims=True), 0.0)
    s["nsend"][...] = jnp.sum(squares, 0, keepdims=True)
    exchange_row(lambda p: s["nsend"], s["nrecv"], 5)
    landed(s["nrecv"], 5)
    nrm_ref[...] = total_of(s["nrecv"], nrow)

    pltpu.make_async_copy(cols, cols, ret_sem.at[0]).wait()

    def ended(count):
        sent = s["sbuf"] if direct else pair_ref
        sent = sent.at[pl.ds(0, cols.shape[2] - count)]
        pltpu.make_async_copy(sent, sent, send_sem.at[0]).wait()
        gone = zin.at[pl.ds(0, count), :, :, pl.ds(0, half - 1)]
        pltpu.make_async_copy(gone, gone, rsend_sem.at[0]).wait()
        for at_side, rows_y, rows_d in ((0, 2 * qn, qn), (1, qn, 2 * qn)):

            @pl.when(side == at_side)
            def _():
                part = y3.at[pl.ds(0, count), pl.ds(0, rows_y)]
                pltpu.make_async_copy(part, part, x_send.at[0]).wait()
                part = d3.at[pl.ds(0, count), pl.ds(0, rows_d)]
                pltpu.make_async_copy(part, part, x_send.at[1]).wait()

    for kind, count in ((False, light), (True, heavy)):

        @pl.when(is_heavy == kind)
        def _():
            ended(count)

    for n, name in enumerate(("wrow", "wall", "grecv", "srecv", "crecv", "nrecv")):
        sent = s[name].at[pl.ds(0, s[name].shape[0] - 1)]
        pltpu.make_async_copy(sent, sent, misc_send.at[n]).wait()


def step_kernel(direct, *refs):
    if direct:
        cols, refs = refs[0], refs[1:]
    red_ref, nrm_ref, w_ref, m1_ref, m2_ref, gain_ref, gm_ref, gv_ref, bias_ref, bm_ref, bv_ref = refs[:11]
    refs = refs[11:]
    if direct:
        bigs, refs = refs[0:2], refs[2:11] + refs[11:]
        refs, (slot, stage, sem) = refs[:9], refs[9:]
        _, crops, cl, rl, width = cols.shape
        gc = 16
        copies = []
        for b in range(cl // gc):
            for c in range(crops):
                for a in range(2):
                    n = len(copies)
                    for j in range(gc):
                        stage[n % 2, pl.ds(j, rl, stride=gc), :] = cols[a, c, b * gc + j].astype(F32)
                    slot[n] = stage[n % 2].reshape(rl, gc, width).astype(BF)
                    there = bigs[a].at[c, :, pl.ds(b * gc, gc), :]
                    copy = pltpu.make_async_copy(slot.at[n], there, sem.at[n])
                    copy.start()
                    copies.append(copy)
    nw_ref, n1_ref, n2_ref, ng_ref, ngm_ref, ngv_ref, nb_ref, nbm_ref, nbv_ref = refs
    width = gain_ref.shape[1]
    heads = bias_ref.shape[1]
    wval = w_ref[...]
    first, second, step_w = moments(wval, red_ref[0:5, :], m1_ref[...], m2_ref[...])
    spot = lax.broadcasted_iota(jnp.int32, (1, width), 1)
    place = lax.broadcasted_iota(jnp.int32, (5, 1), 0)
    value_sq = jnp.sum(jnp.where(spot == place, nrm_ref[...], 0.0), 1, keepdims=True)
    step_sq = jnp.sum(jnp.where(spot == place + 8, nrm_ref[...], 0.0), 1, keepdims=True)
    nw_ref[...] = wval - rate * (jnp.sqrt(value_sq) / jnp.sqrt(step_sq)) * step_w
    n1_ref[...] = first
    n2_ref[...] = second
    for row, n, own in (
        (5, width, (gain_ref, gm_ref, gv_ref, ng_ref, ngm_ref, ngv_ref)),
        (6, heads, (bias_ref, bm_ref, bv_ref, nb_ref, nbm_ref, nbv_ref)),
    ):
        val = own[0][...]
        first, second, step_v = moments(val, red_ref[row : row + 1, 0:n], own[1][...], own[2][...])
        ratio = jnp.sqrt(jnp.sum(val * val, 1, keepdims=True)) / jnp.sqrt(
            jnp.sum(step_v * step_v, 1, keepdims=True)
        )
        own[3][...] = val - rate * ratio * step_v
        own[4][...] = first
        own[5][...] = second
    if direct:
        for copy in copies:
            copy.wait()


def body(
    nrow,
    ncol,
    pair,
    cotangent,
    segments,
    lengths,
    weights,
    moment_one,
    moment_two,
    gain,
    gain_m,
    gain_v,
    chain_bias,
    bias_m,
    bias_v,
):
    crops, rl, cl, width = pair.shape
    heads = chain_bias.shape[0]
    half = nrow // 2
    qn = half * rl
    wr = weights.shape[1] // width
    slots = -(-8 // ncol)
    direct = cl % 16 == 0 and rl % 16 == 0
    pairs = cl // (half // 2)
    light = LIGHT if direct and pairs == 64 else pairs // 2
    heavy = pairs - light
    dims = (nrow, ncol, crops, light, heavy, rl, width, heads, wr, direct)
    wtype = BF if wr % 16 == 0 else F32
    ring = AHEAD + LAG + 1
    hbm = pl.BlockSpec(memory_space=pl.ANY)
    vmem = pl.BlockSpec(memory_space=pltpu.VMEM)
    smem = pl.BlockSpec(memory_space=pltpu.SMEM)
    dma = pltpu.SemaphoreType.DMA
    outs = {
        "red": pltpu.VMEM((slots * ncol, wr * width), F32),
        "nrm": pltpu.VMEM((1, width), F32),
        "cols": pltpu.VMEM((2, crops, cl, rl, width), BF),
    }
    scratch = {
        "zin": pltpu.VMEM((heavy, crops, 2, half, rl, width), BF),
        "y3": pltpu.VMEM((heavy, 3 * qn, width), BF),
        "d3": pltpu.VMEM((heavy, 3 * qn, width), BF),
        "own": pltpu.VMEM((ring, 3 * qn, width), F32),
        "xring": pltpu.VMEM((ring, 2 * qn, width), F32),
        "iring": pltpu.VMEM((ring, 2 * qn, width), F32),
        "yring": pltpu.VMEM((ring, 2 * qn, width), BF),
        "rev": pltpu.VMEM((qn, qn), BF),
        "wtmp": pltpu.VMEM((8, wr, width), F32),
        "wsend": pltpu.VMEM((slots * ncol, wr, width), wtype),
        "wrow": pltpu.VMEM((nrow, slots, wr, width), wtype),
        "wall": pltpu.VMEM((ncol, nrow, slots, wr, width), wtype),
        "gsend": pltpu.VMEM((slots * ncol, width, width), F32),
        "grecv": pltpu.VMEM((ncol, slots, width, width), F32),
        "ssend": pltpu.VMEM((nrow, slots, wr, width), F32),
        "srecv": pltpu.VMEM((nrow, slots, wr, width), F32),
        "csend": pltpu.VMEM((slots, wr, width), F32),
        "crecv": pltpu.VMEM((ncol, slots, wr, width), F32),
        "nsend": pltpu.VMEM((1, width), F32),
        "nrecv": pltpu.VMEM((nrow, 1, width), F32),
        "wqg": pltpu.VMEM((width, 2 * width), BF),
        "wkv": pltpu.VMEM((width, 2 * width), BF),
        "wqg_t": pltpu.VMEM((2 * width, width), BF),
        "wkv_t": pltpu.VMEM((2 * width, width), BF),
        "w4": pltpu.VMEM((width, width), BF),
        "augk": pltpu.VMEM((crops, 2 * qn, width), BF),
        "augq": pltpu.VMEM((crops, heads, width, qn), BF),
        "hotk": pltpu.VMEM((crops, 16, 2 * qn), BF),
        "hotq": pltpu.VMEM((crops, 16, qn), BF),
        "dwqg_acc": pltpu.VMEM((2 * width, width), F32),
        "dwkv_acc": pltpu.VMEM((2 * width, width), F32),
        "dw4_acc": pltpu.VMEM((width, width), F32),
        "dg_acc": pltpu.VMEM((8, width), F32),
        "db_acc": pltpu.VMEM((heads, 8, qn), F32),
        "in_sem": dma((heavy,)),
        "y_sem": dma((heavy,)),
        "d_sem": dma((heavy,)),
        "send_sem": dma((1,)),
        "ret_sem": dma((1,)),
        "rsend_sem": dma((1,)),
        "x_send": dma((2,)),
        "misc_recv": dma((6,)),
        "misc_send": dma((6,)),
    }
    if direct:
        sources = (pair, cotangent)
        scratch["raw"] = pltpu.VMEM((4, crops, 2, rl, 16, width), BF)
        scratch["sbuf"] = pltpu.VMEM((cl, crops, 2, rl, width), BF)
        scratch["stage"] = pltpu.VMEM((2, rl * 16, width), F32)
        scratch["raw_sem"] = dma((4, crops, 2))
    else:
        sources = (jnp.transpose(jnp.stack([pair, cotangent], 1), (3, 0, 1, 2, 4)), cotangent)
    names = tuple(outs) + tuple(scratch)
    res1 = pl.pallas_call(
        functools.partial(main_kernel, dims, names),
        out_shape=tuple(outs.values()),
        in_specs=[hbm, hbm, vmem, smem, vmem, vmem, vmem, vmem, smem],
        out_specs=(vmem,) * len(outs),
        scratch_shapes=list(scratch.values()),
        compiler_params=pltpu.CompilerParams(
            collective_id=0, has_side_effects=True, vmem_limit_bytes=54 << 20
        ),
        name="column_attention",
    )(
        *(
            pltpu.with_memory_space_constraint(x, pltpu.HBM)
            for x in (
                *sources,
                segments,
                lengths,
                weights,
                moment_one,
                moment_two,
                gain.reshape(1, width),
                chain_bias,
            )
        )
    )
    res1 = dict(zip(outs, res1))
    small = (gain, gain_m, gain_v, chain_bias, bias_m, bias_v)
    ops = [res1["red"], res1["nrm"], weights, moment_one, moment_two] + [a.reshape(1, -1) for a in small]
    fin = jax.ShapeDtypeStruct(pair.shape, BF)
    bigs = [fin, fin] if direct else []
    count = 2 * crops * (cl // 16)
    res = pl.pallas_call(
        functools.partial(step_kernel, direct),
        out_shape=bigs
        + [jax.ShapeDtypeStruct(weights.shape, F32)] * 3
        + [jax.ShapeDtypeStruct((1, width), F32)] * 3
        + [jax.ShapeDtypeStruct((1, heads), F32)] * 3,
        in_specs=[vmem] * (len(ops) + direct),
        out_specs=[hbm] * len(bigs) + [vmem] * 9,
        scratch_shapes=[
            pltpu.VMEM((count, rl, 16, width), BF),
            pltpu.VMEM((2, rl * 16, width), F32),
            dma((count,)),
        ]
        if direct
        else [],
        compiler_params=pltpu.CompilerParams(vmem_limit_bytes=18 << 20),
        name="lamb_step",
    )(*((res1["cols"],) if direct else ()), *ops)
    if direct:
        fins, res = res[:2], res[2:]
    else:
        fins = [jnp.swapaxes(res1["cols"][a], 1, 2) for a in range(2)]
    return (*fins, *res[:3], *[a.reshape(-1) for a in res[3:]])


def solution(mesh):
    big = P(None, "row", "col", None)
    shard = P(None, "row")
    return jax.shard_map(
        functools.partial(body, mesh.shape["row"], mesh.shape["col"]),
        mesh=mesh,
        in_specs=(big, big, P(), P(), shard, shard, shard) + (P(),) * 6,
        out_specs=(big, big, shard, shard, shard) + (P(),) * 6,
        check_vma=False,
    )
```

```python
import functools
import math

import jax
import jax.numpy as jnp
from jax import lax
from jax.experimental import pallas as pl
from jax.experimental.pallas import tpu as pltpu
from jax.sharding import PartitionSpec as P

STEP = 10
beta_one = 0.9
beta_two = 0.999
epsilon = 1e-06
decay = 0.01
rate = 0.25

BF = jnp.bfloat16
F32 = jnp.float32
MESH = pl.DeviceIdType.MESH
NT = ((1,), (1,))
TN = ((0,), (0,))
LOG2E = math.log2(math.e)
SEGS = 4
LEAD, AHEAD, LAG = 6, 3, 3
LIGHT = 24


def dot(a, b, dims=((1,), (0,))):
    return lax.dot_general(a, b, (dims, ((), ())), preferred_element_type=F32)


def normed(z, gain):
    mean = jnp.mean(z, -1, keepdims=True)
    cen = z - mean
    var = jnp.mean(cen * cen, -1, keepdims=True)
    inv = lax.rsqrt(var + 1e-05)
    xhat = cen * inv
    return xhat, inv, (xhat * gain).astype(BF)


def attend(z, co, yown, yall, wqg_t, wkv, wkv_t, w4, wqg, augk, augq, hotk, hotq, heads):
    qn, width = z[0].shape
    hsize = width // heads
    scale = 1.0 / math.sqrt(hsize)
    kv = dot(yall, wkv).astype(BF)
    kvT = dot(wkv_t, yall, NT).astype(BF)
    head_of = lax.broadcasted_iota(jnp.int32, (width, 1), 0) // hsize
    ones = jnp.ones((16, 2 * qn), BF)
    outs, dqgT, dkA, dkP = [], [], [], None
    dw4, db = 0.0, [0.0] * heads
    for c in range(2):
        first, packed = slice(c * qn, (c + 1) * qn), slice(2 * qn, 3 * qn)
        k = jnp.concatenate([kv[first, :width], kv[packed, :width]], 0)
        v = jnp.concatenate([kv[first, width:], kv[packed, width:]], 0)
        bothT = jnp.concatenate([kvT[:, first], kvT[:, packed]], 1)
        kT, vT = bothT[:width], bothT[width:]
        projT = dot(wqg_t, yown[c], NT)
        qT = projT[:width].astype(BF)
        gT = jax.nn.sigmoid(projT[width:])
        kaug = jnp.concatenate([k, augk[c]], 1)
        row16 = lax.broadcasted_iota(jnp.int32, (16, 1), 0)
        tile_k = jnp.concatenate([hotk[c][:4].astype(F32)] * 4, 0)
        tile_q = jnp.concatenate([hotq[c][:4].astype(F32)] * 4, 0)
        hk = [jnp.where(row16 // 4 == h, tile_k, 0.0).astype(BF) for h in range(heads)]
        hq = [jnp.where(row16 // 4 == h, tile_q, 0.0) for h in range(heads)]
        es = []
        for h in range(heads):
            qaug = jnp.concatenate([jnp.where(head_of == h, qT, jnp.zeros_like(qT)), augq[c][h]], 0)
            s = dot(kaug, qaug) * (scale * LOG2E)
            e = jnp.exp2(s - jnp.max(s, 0, keepdims=True)).astype(BF)
            es.append(e)
        e_all = jnp.concatenate(es, 0)
        one_row = lax.broadcasted_iota(jnp.int32, (16, 1), 0)
        lhs = [
            jnp.concatenate(
                [
                    jnp.where(head_of == h, vT, jnp.zeros_like(vT)),
                    jnp.broadcast_to(jnp.where(one_row == h, 1.0, 0.0).astype(BF), (16, 2 * qn)),
                ],
                0,
            )
            for h in range(heads)
        ]
        a = dot(jnp.concatenate(lhs, 1), e_all)
        r = 1.0 / a[width : width + heads]
        rb = jnp.concatenate([jnp.broadcast_to(r[h : h + 1], (hsize, qn)) for h in range(heads)], 0)
        aT = a[:width] * rb
        oT = (aT * gT).astype(BF)
        outs.append(z[c] + dot(oT, w4, TN))
        dw4 = dw4 + dot(oT, co[c])
        doT = dot(w4, co[c], NT).astype(BF).astype(F32)
        daT = (doT * gT).astype(BF).astype(F32)
        dgT = (doT * aT * gT * (1.0 - gT)).astype(BF)
        dnT = (daT * rb * scale).astype(BF)
        prod = aT * dnT.astype(F32)
        dss, dk, dv, lhs = [], [], [], []
        dps = dot(v, jnp.concatenate([jnp.where(head_of == h, dnT, jnp.zeros_like(dnT)) for h in range(heads)], 1))
        for h in range(heads):
            rows = slice(h * hsize, (h + 1) * hsize)
            shift = jnp.sum(prod[rows], 0, keepdims=True)
            e = es[h]
            ds = (e.astype(F32) * (dps[:, h * qn : (h + 1) * qn] - shift)).astype(BF)
            dss.append(ds)
            dk.append(dot(qT[rows], ds, NT))
            dv.append(dot(dnT[rows], e, NT) * (1.0 / scale))
            lhs.append(
                jnp.concatenate(
                    [jnp.where(head_of == h, kT, jnp.zeros_like(kT)), hk[h]], 0
                )
            )
        x = dot(jnp.concatenate(lhs, 1), jnp.concatenate(dss, 0))
        for h in range(heads):
            db[h] = db[h] + (x[width : width + 16] * hq[h])[:8] + (x[width : width + 16] * hq[h])[8:]
        dqgT.append(jnp.concatenate([x[:width].astype(BF), dgT], 0))
        dkv = jnp.concatenate(dk + dv, 0)
        dkA.append(dkv[:, :qn].astype(BF))
        dkP = dkv[:, qn:] if dkP is None else dkP + dkv[:, qn:]
    dqgT = jnp.concatenate(dqgT, 1)
    dkvT = jnp.concatenate(dkA + [dkP.astype(BF)], 1)
    dwqg = dot(dqgT, jnp.concatenate(yown, 0))
    dwkv = dot(dkvT, yall)
    dy_own = jnp.transpose(dot(wqg, dqgT))
    dy_all = jnp.transpose(dot(wkv, dkvT))
    return outs, dy_own, dy_all, dwqg, dwkv, dw4, db


def moments(value, grad, first, second):
    first_new = beta_one * first + (1.0 - beta_one) * grad
    second_new = beta_two * second + (1.0 - beta_two) * grad * grad
    step_dir = (
        first_new
        / (1.0 - beta_one**STEP)
        / (jnp.sqrt(second_new / (1.0 - beta_two**STEP)) + epsilon)
        + decay * value
    )
    return (first_new, second_new, step_dir)


def early_blocks(light, heavy, half, gc):
    late = set()
    for r in range(half):
        first = r * light if r < half // 2 else half // 2 * light + (r - half // 2) * heavy
        count = light if r < half // 2 else heavy
        for u in range(count):
            turn = -(-((u + 1) * heavy) // count)
            if turn > heavy - 8:
                late.add((first + u) // gc)
    return [b for b in range(half // 2 * (light + heavy) // gc) if b not in late]


def main_kernel(dims, names, *refs):
    nrow, ncol, crops, light, heavy, rl, width, heads, wr, direct = dims
    pair_ref, cot_ref, seg_ref, len_ref, w_ref, m1_ref, m2_ref, gain_ref, bias_ref = refs[:9]
    srcs = (pair_ref, cot_ref)
    s = dict(zip(names, refs[9:]))
    zin, y3, d3, own, xring, iring, yring = (s[n] for n in ("zin", "y3", "d3", "own", "xring", "iring", "yring"))
    in_sem, send_sem, ret_sem, rsend_sem = s["in_sem"], s["send_sem"], s["ret_sem"], s["rsend_sem"]
    misc_recv, misc_send, y_sem, d_sem, x_send = (
        s[n] for n in ("misc_recv", "misc_send", "y_sem", "d_sem", "x_send")
    )
    red_ref, nrm_ref = s["red"], s["nrm"]
    half = nrow // 2
    qn = half * rl
    gc = 16 if direct else half // 2 * (light + heavy)
    ring = xring.shape[0]
    cols = s["cols"]
    nblocks = (half // 2 * (light + heavy)) // gc
    hsize = width // heads
    scale = 1.0 / math.sqrt(hsize)
    slots = s["wrow"].shape[1]
    me = lax.axis_index("row")
    mc = lax.axis_index("col")
    side = me // half
    place = lax.rem(me, half)

    def rank_of(at_side, w):
        return lax.rem(w + at_side * (half // 2), half)

    def first_of(rank):
        near_rank = rank - half // 2
        return jnp.where(near_rank < 0, rank * light, (half // 2) * light + near_rank * heavy)

    rank = rank_of(side, place)
    is_heavy = rank >= half // 2
    base = first_of(rank)
    partner = ((1 - side) * half + rank_of(1 - side, rank), mc)

    def active(heavy_one, n):
        return heavy_one | (((n + 1) * light) // heavy > (n * light) // heavy)

    def unit_of(heavy_one, n):
        return jnp.where(heavy_one, n, (n * light) // heavy)

    def row_peer(d):
        return lax.rem(me + d, nrow)

    def col_peer(d):
        return lax.rem(mc + d, ncol)

    def near(d):
        return lax.rem(place + d, half)

    def device(w):
        return (side * half + w, mc)

    def load_block(b, slot):
        for c in range(crops):
            for a in range(2):
                pltpu.make_async_copy(
                    srcs[a].at[c, :, pl.ds(b * gc, gc), :],
                    s["raw"].at[slot, c, a],
                    s["raw_sem"].at[slot, c, a],
                ).start()

    if direct:
        starts = [r * light for r in range(half // 2)]
        starts += [(half // 2) * light + r * heavy for r in range(half // 2)]
        order = []
        for x in starts[half // 2 :] + starts[: half // 2]:
            order += [b for b in sorted({(x + n) // gc for n in range(LEAD)}) if b not in order]
        order += [b for b in range(nblocks) if b not in order]
        done_blocks = 0
        nslot = s["raw"].shape[0]
        for n in range(nslot):
            load_block(order[n], n)

    barrier = pltpu.get_barrier_semaphore()

    def greet_row(d, _):
        pl.semaphore_signal(barrier, inc=1, device_id=(row_peer(d), mc), device_id_type=MESH)
        return 0

    def greet_col(d, _):
        pl.semaphore_signal(barrier, inc=1, device_id=(me, col_peer(d)), device_id_type=MESH)
        return 0

    lax.fori_loop(1, nrow, greet_row, 0)
    lax.fori_loop(1, ncol, greet_col, 0)
    for j in range(wr):
        s["wtmp"][0:5, j, :] = w_ref[:, j * width : (j + 1) * width]
    for k in range(slots * ncol):
        s["wsend"][k] = (s["wtmp"][k] if k < 5 else jnp.zeros((wr, width), F32)).astype(s["wsend"].dtype)
    pl.semaphore_wait(barrier, nrow - 1 + ncol - 1)

    def remote(src, dst, send, recv, peer):
        pltpu.make_async_remote_copy(
            src, dst, send, recv, device_id=peer, device_id_type=MESH
        ).start()

    def exchange_row(src_of, dst, n):
        def push(d, _):
            p = row_peer(d)
            remote(src_of(p), dst.at[me], misc_send.at[n], misc_recv.at[n], (p, mc))
            return 0

        lax.fori_loop(1, nrow, push, 0)
        pltpu.make_async_copy(src_of(me), dst.at[me], misc_recv.at[n]).start()

    def exchange_col(src_of, dst, n):
        def push(d, _):
            p = col_peer(d)
            remote(src_of(p), dst.at[mc], misc_send.at[n], misc_recv.at[n], (me, p))
            return 0

        lax.fori_loop(1, ncol, push, 0)
        pltpu.make_async_copy(src_of(mc), dst.at[mc], misc_recv.at[n]).start()

    def landed(dst, n):
        pltpu.make_async_copy(dst, dst, misc_recv.at[n]).wait()

    def total_of(ref, n):
        return lax.fori_loop(1, n, lambda r, t: t + ref[r], ref[0])

    exchange_row(lambda p: s["wsend"].at[pl.ds(mc * slots, slots)], s["wrow"], 0)

    def column_of(col):
        return s["sbuf"].at[col] if direct else pair_ref.at[col]

    def push_turn(n):
        def to_peer(d, _):
            w = near(d)
            there = rank_of(side, w)
            to_heavy = there >= half // 2
            u = unit_of(to_heavy, n)

            @pl.when(active(to_heavy, n))
            def _():
                src = column_of(first_of(there) + u)
                remote(src, zin.at[u, :, :, place], send_sem.at[0], in_sem.at[u], device(w))

            return 0

        lax.fori_loop(1, half, to_peer, 0)
        mine = unit_of(is_heavy, n)

        @pl.when(active(is_heavy, n))
        def _():
            src = column_of(base + mine)
            pltpu.make_async_copy(src, zin.at[mine, :, :, place], in_sem.at[mine]).start()

    def push_turns(first, last):
        def at_turn(n, _):
            push_turn(n)
            return 0

        lax.fori_loop(first, last, at_turn, 0)

    def turn_block(n):
        b, slot = order[n], n % nslot
        for c in range(crops):
            for a in range(2):
                here = s["raw"].at[slot, c, a]
                pltpu.make_async_copy(here, here, s["raw_sem"].at[slot, c, a]).wait()
                s["stage"][a] = s["raw"][slot, c, a].astype(F32).reshape(rl * gc, width)
                for j in range(gc):
                    s["sbuf"][b * gc + j, c, a] = s["stage"][a, pl.ds(j, rl, stride=gc), :].astype(BF)
        if n + nslot < len(order):
            load_block(order[n + nslot], slot)

    def push_one(there, n):
        to_heavy = there >= half // 2
        u = unit_of(to_heavy, n)

        @pl.when(active(to_heavy, n) & (there == rank))
        def _():
            src = column_of(base + u)
            pltpu.make_async_copy(src, zin.at[u, :, :, place], in_sem.at[u]).start()

        @pl.when(active(to_heavy, n) & (there != rank))
        def _():
            src = column_of(first_of(there) + u)
            remote(src, zin.at[u, :, :, place], send_sem.at[0], in_sem.at[u], device(rank_of(side, there)))

    if direct:
        for there in list(range(half // 2, half)) + list(range(half // 2)):
            for b in sorted({(starts[there] + n) // gc for n in range(LEAD)}):
                if b in order[:done_blocks]:
                    continue
                turn_block(order.index(b))
                done_blocks += 1
            push_one(there, 0)
        push_turns(1, LEAD)
    else:
        push_turns(0, LEAD)

    back = lax.broadcasted_iota(jnp.int32, (qn, qn), 0) + lax.broadcasted_iota(jnp.int32, (qn, qn), 1)
    s["rev"][...] = jnp.where(back == qn - 1, 1.0, 0.0).astype(BF)

    where_t = lax.broadcasted_iota(jnp.int32, (qn, 1), 0)

    def prepare(u, at):
        pltpu.make_async_copy(zin.at[u], zin.at[u], in_sem.at[u]).wait()
        for c in range(crops):
            rows = slice(c * qn, (c + 1) * qn)
            xhat, inv, y = normed(zin[u, c, 0].astype(F32).reshape(qn, width), gain_ref[...])
            xring[at, rows, :] = xhat
            iring[at, rows, :] = jnp.broadcast_to(inv, (qn, width))
            yring[at, rows, :] = y

        @pl.when(side == 0)
        def _():
            y3[u, 0 : 2 * qn, :] = yring[at]
            part = y3.at[u, pl.ds(0, 2 * qn)]
            remote(part, part, x_send.at[0], y_sem.at[u], partner)

        @pl.when(side == 1)
        def _():
            y1 = dot(s["rev"][...], yring[at, qn : 2 * qn, :])
            y0 = yring[at, 0:qn, :].astype(F32)
            y3[u, 2 * qn : 3 * qn, :] = jnp.where(where_t < len_ref[0] - qn, y0, y1).astype(BF)
            part = y3.at[u, pl.ds(2 * qn, qn)]
            remote(part, part, x_send.at[0], y_sem.at[u], partner)

    def at_turn(t, act):
        @pl.when((t >= 0) & (t < heavy) & active(is_heavy, t))
        def _():
            act(unit_of(is_heavy, t), lax.rem(t, ring))

    def early_turn(n, _):
        at_turn(n, prepare)
        return 0

    lax.fori_loop(0, 1, early_turn, 0)
    if direct:
        for n in range(done_blocks, nblocks):
            turn_block(n)
    lax.fori_loop(1, AHEAD, early_turn, 0)

    landed(s["wrow"], 0)
    exchange_col(lambda p: s["wrow"], s["wall"], 1)

    lane = lax.broadcasted_iota(jnp.int32, (1, qn), 1)
    line = lax.broadcasted_iota(jnp.int32, (width, 1), 0)
    for c in range(crops):
        low_seg, high_seg = seg_ref[c : c + 1, :qn], seg_ref[c : c + 1, qn:]
        own_seg = jnp.where(side == 0, low_seg, high_seg)
        same_low = (lax.rem(line, SEGS) == low_seg).astype(F32)
        same_high = (lax.rem(line, SEGS) == high_seg).astype(F32)
        pad = jnp.where(lane + qn >= len_ref[c], -1e30, 0.0)
        if c == 1:
            same_high = dot(same_high.astype(BF), s["rev"][...])
            pad = jnp.where(2 * qn - 1 - lane >= len_ref[c], -1e30, 0.0)
        same = jnp.concatenate([same_low, same_high], 1)
        pad = jnp.concatenate([jnp.zeros((1, qn), F32), pad], 1)
        s["hotk"][c] = jnp.where(line[:16] < SEGS, same[:16], 0.0).astype(BF)
        rowsk = jnp.where(line < 3 * SEGS, same, jnp.where(line == 3 * SEGS, pad, 0.0))
        s["augk"][c] = jnp.transpose(rowsk).astype(BF)
        same = (lax.rem(line, SEGS) == own_seg).astype(F32)
        s["hotq"][c] = jnp.where(line[:16] < SEGS, same[:16], 0.0).astype(BF)
        for h in range(heads):
            full = jnp.full((width, 1), bias_ref[h] * (1.0 / scale), F32)
            high = full.astype(BF).astype(F32)
            mid = (full - high).astype(BF).astype(F32)
            low = full - high - mid
            part = jnp.where(line < SEGS, high, jnp.where(line < 2 * SEGS, mid, low))
            rowsq = jnp.where(line < 3 * SEGS, same * part, jnp.where(line == 3 * SEGS, 1.0, 0.0))
            s["augq"][c, h] = rowsq.astype(BF)

    for name in ("dwqg_acc", "dwkv_acc", "dw4_acc", "dg_acc", "db_acc"):
        s[name][...] = jnp.zeros_like(s[name])

    landed(s["wall"], 1)
    for k in range(5):
        w = s["wall"][k // slots, :, k % slots].astype(F32).reshape(width, width)
        if k == 4:
            s["w4"][...] = w.astype(BF)
        else:
            name, at = {0: ("wqg", 0), 3: ("wqg", 1), 1: ("wkv", 0), 2: ("wkv", 1)}[k]
            s[name][:, at * width : (at + 1) * width] = w.astype(BF)
            s[name + "_t"][at * width : (at + 1) * width, :] = jnp.transpose(w).astype(BF)

    def give(u, a):
        here = cols.at[a, :, pl.ds((base + u) * rl, rl)]
        landing = ret_sem.at[(base + u) // gc]

        def to_peer(d, _):
            w = near(d)
            remote(zin.at[u, :, a, w], here, rsend_sem.at[0], landing, device(w))
            return 0

        lax.fori_loop(1, half, to_peer, 0)
        pltpu.make_async_copy(zin.at[u, :, a, place], here, landing).start()

    def work(u, at):
        @pl.when(side == 0)
        def _():
            part = y3.at[u, pl.ds(2 * qn, qn)]
            pltpu.make_async_copy(part, part, y_sem.at[u]).wait()

        @pl.when(side == 1)
        def _():
            part = y3.at[u, pl.ds(0, 2 * qn)]
            pltpu.make_async_copy(part, part, y_sem.at[u]).wait()

        outs, dy_own, dy_all, dwqg, dwkv, dw4, db = attend(
            [zin[u, c, 0].astype(F32).reshape(qn, width) for c in range(crops)],
            [zin[u, c, 1].astype(F32).reshape(qn, width).astype(BF) for c in range(crops)],
            [yring[at, c * qn : (c + 1) * qn, :] for c in range(crops)],
            y3[u],
            s["wqg_t"][...],
            s["wkv"][...],
            s["wkv_t"][...],
            s["w4"][...],
            s["wqg"][...],
            [s["augk"][c] for c in range(crops)],
            [[s["augq"][c, h] for h in range(heads)] for c in range(crops)],
            [s["hotk"][c] for c in range(crops)],
            [s["hotq"][c] for c in range(crops)],
            heads,
        )
        s["dwqg_acc"][...] += dwqg
        s["dwkv_acc"][...] += dwkv
        s["dw4_acc"][...] += dw4
        for h in range(heads):
            s["db_acc"][h] += db[h]
        for c in range(crops):
            zin[u, c, 0] = outs[c].reshape(half, rl, width).astype(BF)
        give(u, 0)

        @pl.when(side == 0)
        def _():
            own[at, 0 : 2 * qn, :] = dy_own + dy_all[0 : 2 * qn]
            d3[u, 2 * qn : 3 * qn, :] = dy_all[2 * qn :].astype(BF)
            part = d3.at[u, pl.ds(2 * qn, qn)]
            remote(part, part, x_send.at[1], d_sem.at[u], partner)

        @pl.when(side == 1)
        def _():
            own[at, 0 : 2 * qn, :] = dy_own
            own[at, 2 * qn : 3 * qn, :] = dy_all[2 * qn :]
            d3[u, 0 : 2 * qn, :] = dy_all[0 : 2 * qn].astype(BF)
            part = d3.at[u, pl.ds(0, 2 * qn)]
            remote(part, part, x_send.at[1], d_sem.at[u], partner)

    def finish(u, at):

        @pl.when(side == 0)
        def _():
            part = d3.at[u, pl.ds(0, 2 * qn)]
            pltpu.make_async_copy(part, part, d_sem.at[u]).wait()
            own[at, 0 : 2 * qn, :] += d3[u, 0 : 2 * qn, :].astype(F32)

        @pl.when(side == 1)
        def _():
            part = d3.at[u, pl.ds(2 * qn, qn)]
            pltpu.make_async_copy(part, part, d_sem.at[u]).wait()
            both = own[at, 2 * qn : 3 * qn, :] + d3[u, 2 * qn : 3 * qn, :].astype(F32)
            mine = where_t < len_ref[0] - qn
            own[at, 0:qn, :] += jnp.where(mine, both, 0.0)
            own[at, qn : 2 * qn, :] += dot(s["rev"][...], jnp.where(mine, 0.0, both).astype(BF))

        for c in range(crops):
            rows = slice(c * qn, (c + 1) * qn)
            dy, xhat = own[at, rows, :], xring[at, rows, :]
            s["dg_acc"][0:1] += jnp.sum(dy * xhat, 0, keepdims=True)
            dx = dy * gain_ref[...]
            rest = dx - jnp.mean(dx, -1, keepdims=True) - xhat * jnp.mean(dx * xhat, -1, keepdims=True)
            grad = zin[u, c, 1].astype(F32).reshape(qn, width) + iring[at, rows, :] * rest
            zin[u, c, 1] = grad.reshape(half, rl, width).astype(BF)
        give(u, 1)

    def step(it, _):
        @pl.when(it + LEAD < heavy)
        def _():
            push_turn(it + LEAD)

        at_turn(it + AHEAD, prepare)
        at_turn(it, work)
        at_turn(it - LAG, finish)
        return 0

    lax.fori_loop(0, heavy, step, 0)

    def turn_back(b):
        block = cols.at[:, :, pl.ds(b * gc * rl, gc * rl)]
        pltpu.make_async_copy(block, block, ret_sem.at[b]).wait()
        rows = slice(b * gc * rl, (b + 1) * gc * rl)
        for c in range(crops):
            for a in range(2):
                for j in range(gc):
                    at = (b * gc + j) * rl
                    s["stage"][a, pl.ds(j, rl, stride=gc), :] = cols[a, c, at : at + rl, :].astype(F32)
                cols[a, c, rows, :] = s["stage"][a].astype(BF)

    soon = early_blocks(light, heavy, half, gc) if direct else []

    gsend = s["gsend"]
    for k, (name, at) in enumerate((("dwqg_acc", 0), ("dwkv_acc", 0), ("dwkv_acc", 1), ("dwqg_acc", 1))):
        gsend[k] = jnp.transpose(s[name][at * width : (at + 1) * width, :])
    gsend[4] = s["dw4_acc"][...]
    spot = lax.broadcasted_iota(jnp.int32, (1, width), 1)
    dbias = jnp.zeros((1, width), F32)
    for h in range(heads):
        total_h = jnp.sum(jnp.sum(s["db_acc"][h], 0, keepdims=True), 1, keepdims=True)
        dbias = jnp.where(spot == h, total_h * (1.0 / scale), dbias)
    gsend[6] = jnp.broadcast_to(dbias, (width, width))
    for k in [5] + list(range(7, slots * ncol)):
        gsend[k] = jnp.zeros((width, width), F32)
    exchange_col(lambda p: gsend.at[pl.ds(p * slots, slots)], s["grecv"], 2)

    def last_turn(t, _):
        at_turn(t, finish)
        return 0

    lax.fori_loop(heavy - LAG, heavy, last_turn, 0)
    s["vsend"][0] = s["dg_acc"][0:1]
    exchange_row(lambda p: s["vsend"].at[0], s["vrow"], 6)
    landed(s["grecv"], 2)
    share = total_of(s["grecv"], ncol)
    for p in range(nrow):
        s["ssend"][p] = share[:, p * wr : (p + 1) * wr, :]
    exchange_row(lambda p: s["ssend"].at[p], s["srecv"], 3)
    for b in soon[0::3]:
        turn_back(b)
    landed(s["vrow"], 6)
    s["vsend"][1] = total_of(s["vrow"], nrow)
    exchange_col(lambda p: s["vsend"].at[1], s["vcol"], 7)
    landed(s["srecv"], 3)
    s["csend"][...] = total_of(s["srecv"], nrow)
    exchange_col(lambda p: s["csend"], s["crecv"], 4)
    for b in soon[1::3]:
        turn_back(b)
    landed(s["crecv"], 4)
    landed(s["vcol"], 7)
    for j in range(wr):
        red_ref[:, j * width : (j + 1) * width] = s["crecv"][:, :, j, :].reshape(slots * ncol, width)
    red_ref[5:6, 0:width] = total_of(s["vcol"], ncol)
    wval = w_ref[...]
    step_w = moments(wval, red_ref[0:5, :], m1_ref[...], m2_ref[...])[2]
    row5 = lax.broadcasted_iota(jnp.int32, (5, 1), 0)
    squares = jnp.where(spot == row5, jnp.sum(wval * wval, 1, keepdims=True), 0.0)
    squares += jnp.where(spot == row5 + 8, jnp.sum(step_w * step_w, 1, keepdims=True), 0.0)
    s["nsend"][...] = jnp.sum(squares, 0, keepdims=True)
    exchange_row(lambda p: s["nsend"], s["nrecv"], 5)
    for b in soon[2::3]:
        turn_back(b)
    landed(s["nrecv"], 5)
    nrm_ref[...] = total_of(s["nrecv"], nrow)

    for b in range(nblocks):
        if b not in soon:
            block = cols.at[:, :, pl.ds(b * gc * rl, gc * rl)]
            pltpu.make_async_copy(block, block, ret_sem.at[b]).wait()

    def ended(count):
        sent = s["sbuf"] if direct else pair_ref
        sent = sent.at[pl.ds(0, half // 2 * (light + heavy) - count)]
        pltpu.make_async_copy(sent, sent, send_sem.at[0]).wait()
        gone = zin.at[pl.ds(0, count), :, :, pl.ds(0, half - 1)]
        pltpu.make_async_copy(gone, gone, rsend_sem.at[0]).wait()
        for at_side, rows_y, rows_d in ((0, 2 * qn, qn), (1, qn, 2 * qn)):

            @pl.when(side == at_side)
            def _():
                part = y3.at[pl.ds(0, count), pl.ds(0, rows_y)]
                pltpu.make_async_copy(part, part, x_send.at[0]).wait()
                part = d3.at[pl.ds(0, count), pl.ds(0, rows_d)]
                pltpu.make_async_copy(part, part, x_send.at[1]).wait()

    for kind, count in ((False, light), (True, heavy)):

        @pl.when(is_heavy == kind)
        def _():
            ended(count)

    for n, name in enumerate(
        ("wrow", "wall", "grecv", "srecv", "crecv", "nrecv", "vrow", "vcol")
    ):
        sent = s[name].at[pl.ds(0, s[name].shape[0] - 1)]
        pltpu.make_async_copy(sent, sent, misc_send.at[n]).wait()


def step_kernel(direct, soon, *refs):
    if direct:
        cols, blocks, refs = refs[0], refs[1], refs[2:]
    red_ref, nrm_ref, w_ref, m1_ref, m2_ref, gain_ref, gm_ref, gv_ref, bias_ref, bm_ref, bv_ref = refs[:11]
    refs = refs[11:]
    if direct:
        bigs, refs = refs[0:2], refs[2:11] + refs[11:]
        refs, (slot, stage, sem) = refs[:9], refs[9:]
        _, crops, _, width = cols.shape
        _, rl, cl, _ = bigs[0].shape
        gc = 16
        copies = []

        def put(src, a, c, b):
            n = len(copies)
            copy = pltpu.make_async_copy(src, bigs[a].at[c, :, pl.ds(b * gc, gc), :], sem.at[n])
            copy.start()
            copies.append(copy)

        for b in soon:
            for c in range(crops):
                for a in range(2):
                    put(blocks.at[a, c, b], a, c, b)
        late = [b for b in range(cl // gc) if b not in soon]
        for n, b in enumerate(late):
            for c in range(crops):
                for a in range(2):
                    for j in range(gc):
                        at = (b * gc + j) * rl
                        stage[a, pl.ds(j, rl, stride=gc), :] = cols[a, c, at : at + rl, :].astype(F32)
                    slot[n, c, a] = stage[a].reshape(rl, gc, width).astype(BF)
                    put(slot.at[n, c, a], a, c, b)
    nw_ref, n1_ref, n2_ref, ng_ref, ngm_ref, ngv_ref, nb_ref, nbm_ref, nbv_ref = refs
    width = gain_ref.shape[1]
    heads = bias_ref.shape[1]
    wval = w_ref[...]
    first, second, step_w = moments(wval, red_ref[0:5, :], m1_ref[...], m2_ref[...])
    spot = lax.broadcasted_iota(jnp.int32, (1, width), 1)
    place = lax.broadcasted_iota(jnp.int32, (5, 1), 0)
    value_sq = jnp.sum(jnp.where(spot == place, nrm_ref[...], 0.0), 1, keepdims=True)
    step_sq = jnp.sum(jnp.where(spot == place + 8, nrm_ref[...], 0.0), 1, keepdims=True)
    nw_ref[...] = wval - rate * (jnp.sqrt(value_sq) / jnp.sqrt(step_sq)) * step_w
    n1_ref[...] = first
    n2_ref[...] = second
    for row, n, own in (
        (5, width, (gain_ref, gm_ref, gv_ref, ng_ref, ngm_ref, ngv_ref)),
        (6, heads, (bias_ref, bm_ref, bv_ref, nb_ref, nbm_ref, nbv_ref)),
    ):
        val = own[0][...]
        first, second, step_v = moments(val, red_ref[row : row + 1, 0:n], own[1][...], own[2][...])
        ratio = jnp.sqrt(jnp.sum(val * val, 1, keepdims=True)) / jnp.sqrt(
            jnp.sum(step_v * step_v, 1, keepdims=True)
        )
        own[3][...] = val - rate * ratio * step_v
        own[4][...] = first
        own[5][...] = second
    if direct:
        for copy in copies:
            copy.wait()


def body(
    nrow,
    ncol,
    pair,
    cotangent,
    segments,
    lengths,
    weights,
    moment_one,
    moment_two,
    gain,
    gain_m,
    gain_v,
    chain_bias,
    bias_m,
    bias_v,
):
    crops, rl, cl, width = pair.shape
    heads = chain_bias.shape[0]
    half = nrow // 2
    qn = half * rl
    wr = weights.shape[1] // width
    slots = -(-8 // ncol)
    direct = cl % 16 == 0 and rl % 16 == 0
    pairs = cl // (half // 2)
    light = LIGHT if direct and pairs == 64 else pairs // 2
    heavy = pairs - light
    dims = (nrow, ncol, crops, light, heavy, rl, width, heads, wr, direct)
    wtype = BF if wr % 16 == 0 else F32
    ring = AHEAD + LAG + 1
    hbm = pl.BlockSpec(memory_space=pl.ANY)
    vmem = pl.BlockSpec(memory_space=pltpu.VMEM)
    smem = pl.BlockSpec(memory_space=pltpu.SMEM)
    dma = pltpu.SemaphoreType.DMA
    outs = {
        "red": pltpu.VMEM((slots * ncol, wr * width), F32),
        "nrm": pltpu.VMEM((1, width), F32),
        "cols": pltpu.VMEM((2, crops, cl * rl, width), BF),
    }
    scratch = {
        "zin": pltpu.VMEM((heavy, crops, 2, half, rl, width), BF),
        "y3": pltpu.VMEM((heavy, 3 * qn, width), BF),
        "d3": pltpu.VMEM((heavy, 3 * qn, width), BF),
        "own": pltpu.VMEM((ring, 3 * qn, width), F32),
        "xring": pltpu.VMEM((ring, 2 * qn, width), F32),
        "iring": pltpu.VMEM((ring, 2 * qn, width), F32),
        "yring": pltpu.VMEM((ring, 2 * qn, width), BF),
        "rev": pltpu.VMEM((qn, qn), BF),
        "wtmp": pltpu.VMEM((8, wr, width), F32),
        "wsend": pltpu.VMEM((slots * ncol, wr, width), wtype),
        "wrow": pltpu.VMEM((nrow, slots, wr, width), wtype),
        "wall": pltpu.VMEM((ncol, nrow, slots, wr, width), wtype),
        "gsend": pltpu.VMEM((slots * ncol, width, width), F32),
        "grecv": pltpu.VMEM((ncol, slots, width, width), F32),
        "ssend": pltpu.VMEM((nrow, slots, wr, width), F32),
        "srecv": pltpu.VMEM((nrow, slots, wr, width), F32),
        "csend": pltpu.VMEM((slots, wr, width), F32),
        "crecv": pltpu.VMEM((ncol, slots, wr, width), F32),
        "vsend": pltpu.VMEM((2, 1, width), F32),
        "vrow": pltpu.VMEM((nrow, 1, width), F32),
        "vcol": pltpu.VMEM((ncol, 1, width), F32),
        "nsend": pltpu.VMEM((1, width), F32),
        "nrecv": pltpu.VMEM((nrow, 1, width), F32),
        "wqg": pltpu.VMEM((width, 2 * width), BF),
        "wkv": pltpu.VMEM((width, 2 * width), BF),
        "wqg_t": pltpu.VMEM((2 * width, width), BF),
        "wkv_t": pltpu.VMEM((2 * width, width), BF),
        "w4": pltpu.VMEM((width, width), BF),
        "augk": pltpu.VMEM((crops, 2 * qn, width), BF),
        "augq": pltpu.VMEM((crops, heads, width, qn), BF),
        "hotk": pltpu.VMEM((crops, 16, 2 * qn), BF),
        "hotq": pltpu.VMEM((crops, 16, qn), BF),
        "dwqg_acc": pltpu.VMEM((2 * width, width), F32),
        "dwkv_acc": pltpu.VMEM((2 * width, width), F32),
        "dw4_acc": pltpu.VMEM((width, width), F32),
        "dg_acc": pltpu.VMEM((8, width), F32),
        "db_acc": pltpu.VMEM((heads, 8, qn), F32),
        "in_sem": dma((heavy,)),
        "y_sem": dma((heavy,)),
        "d_sem": dma((heavy,)),
        "send_sem": dma((1,)),
        "ret_sem": dma((cl // 16 if direct else 1,)),
        "rsend_sem": dma((1,)),
        "x_send": dma((2,)),
        "misc_recv": dma((8,)),
        "misc_send": dma((8,)),
    }
    if direct:
        sources = (pair, cotangent)
        scratch["raw"] = pltpu.VMEM((4, crops, 2, rl, 16, width), BF)
        scratch["sbuf"] = pltpu.VMEM((cl, crops, 2, rl, width), BF)
        scratch["stage"] = pltpu.VMEM((2, rl * 16, width), F32)
        scratch["raw_sem"] = dma((4, crops, 2))
    else:
        sources = (jnp.transpose(jnp.stack([pair, cotangent], 1), (3, 0, 1, 2, 4)), cotangent)
    names = tuple(outs) + tuple(scratch)
    res1 = pl.pallas_call(
        functools.partial(main_kernel, dims, names),
        out_shape=tuple(outs.values()),
        in_specs=[hbm, hbm, vmem, smem, vmem, vmem, vmem, vmem, smem],
        out_specs=(vmem,) * len(outs),
        scratch_shapes=list(scratch.values()),
        compiler_params=pltpu.CompilerParams(
            collective_id=0, has_side_effects=True, vmem_limit_bytes=54 << 20
        ),
        name="column_attention",
    )(
        *(
            pltpu.with_memory_space_constraint(x, pltpu.HBM)
            for x in (
                *sources,
                segments,
                lengths,
                weights,
                moment_one,
                moment_two,
                gain.reshape(1, width),
                chain_bias,
            )
        )
    )
    res1 = dict(zip(outs, res1))
    small = (gain, gain_m, gain_v, chain_bias, bias_m, bias_v)
    ops = [res1["red"], res1["nrm"], weights, moment_one, moment_two] + [a.reshape(1, -1) for a in small]
    fin = jax.ShapeDtypeStruct(pair.shape, BF)
    bigs = [fin, fin] if direct else []
    count = 2 * crops * (cl // 16)
    soon = early_blocks(light, heavy, half, 16) if direct else []
    turned = ()
    if direct:
        turned = (res1["cols"], res1["cols"].reshape(2, crops, cl // 16, rl, 16, width))
    res = pl.pallas_call(
        functools.partial(step_kernel, direct, soon),
        out_shape=bigs
        + [jax.ShapeDtypeStruct(weights.shape, F32)] * 3
        + [jax.ShapeDtypeStruct((1, width), F32)] * 3
        + [jax.ShapeDtypeStruct((1, heads), F32)] * 3,
        in_specs=[vmem] * (len(ops) + len(turned)),
        out_specs=[hbm] * len(bigs) + [vmem] * 9,
        scratch_shapes=[
            pltpu.VMEM((cl // 16 - len(soon), crops, 2, rl, 16, width), BF),
            pltpu.VMEM((2, rl * 16, width), F32),
            dma((count,)),
        ]
        if direct
        else [],
        compiler_params=pltpu.CompilerParams(vmem_limit_bytes=18 << 20),
        name="lamb_step",
    )(*turned, *ops)
    if direct:
        fins, res = res[:2], res[2:]
    else:
        fins = [jnp.swapaxes(res1["cols"][a].reshape(crops, cl, rl, width), 1, 2) for a in range(2)]
    return (*fins, *res[:3], *[a.reshape(-1) for a in res[3:]])


def solution(mesh):
    big = P(None, "row", "col", None)
    shard = P(None, "row")
    return jax.shard_map(
        functools.partial(body, mesh.shape["row"], mesh.shape["col"]),
        mesh=mesh,
        in_specs=(big, big, P(), P(), shard, shard, shard) + (P(),) * 6,
        out_specs=(big, big, shard, shard, shard) + (P(),) * 6,
        check_vma=False,
    )
```

```python
import functools
import math

import jax
import jax.numpy as jnp
from jax import lax
from jax.experimental import pallas as pl
from jax.experimental.pallas import tpu as pltpu
from jax.sharding import PartitionSpec as P

STEP = 10
beta_one = 0.9
beta_two = 0.999
epsilon = 1e-06
decay = 0.01
rate = 0.25

BF = jnp.bfloat16
F32 = jnp.float32
MESH = pl.DeviceIdType.MESH
NT = ((1,), (1,))
TN = ((0,), (0,))
LOG2E = math.log2(math.e)
SEGS = 4
EARLY, LEAD, AHEAD, LAG = 2, 4, 2, 3
LIGHT = 22


def dot(a, b, dims=((1,), (0,))):
    return lax.dot_general(a, b, (dims, ((), ())), preferred_element_type=F32)


def normed(z, gain):
    mean = jnp.mean(z, -1, keepdims=True)
    cen = z - mean
    var = jnp.mean(cen * cen, -1, keepdims=True)
    inv = lax.rsqrt(var + 1e-05)
    xhat = cen * inv
    return xhat, inv, (xhat * gain).astype(BF)


def attend(z, co, yown, yall, wqg_t, wkv, wkv_t, w4, wqg, augk, augq, hotk, hotq, heads):
    qn, width = z[0].shape
    hsize = width // heads
    scale = 1.0 / math.sqrt(hsize)
    head_of = lax.broadcasted_iota(jnp.int32, (width, 1), 0) // hsize
    row16 = lax.broadcasted_iota(jnp.int32, (16, 1), 0)
    packed = slice(2 * qn, 3 * qn)

    def spread(xT, last):
        parts = [jnp.where(head_of == h, xT, jnp.zeros_like(xT)) for h in range(heads)]
        if last is not None:
            parts = [jnp.concatenate([p, x], 0) for p, x in zip(parts, last)]
        return jnp.concatenate(parts, 1)

    kv = dot(yall, wkv).astype(BF)
    kvT = dot(wkv_t, yall, NT).astype(BF)
    ones = [jnp.broadcast_to(jnp.where(row16 == h, 1.0, 0.0).astype(BF), (16, 2 * qn)) for h in range(heads)]
    crops = range(2)
    st = [{} for c in crops]
    for c in crops:
        t = st[c]
        first = slice(c * qn, (c + 1) * qn)
        t["k"] = jnp.concatenate([kv[first, :width], kv[packed, :width]], 0)
        t["v"] = jnp.concatenate([kv[first, width:], kv[packed, width:]], 0)
        bothT = jnp.concatenate([kvT[:, first], kvT[:, packed]], 1)
        t["kT"], t["vT"] = bothT[:width], bothT[width:]
        projT = dot(wqg_t, yown[c], NT)
        t["qT"] = projT[:width].astype(BF)
        t["gT"] = jax.nn.sigmoid(projT[width:])
        t["doT"] = dot(w4, co[c], NT).astype(BF).astype(F32)
    outs, dqgT, dkA, dkP = [], [], [], None
    dw4, db = 0.0, [0.0] * heads
    for c in crops:
        t = st[c]
        kaug = jnp.concatenate([t["k"], augk[c]], 1)
        es = []
        for h in range(heads):
            qaug = jnp.concatenate([jnp.where(head_of == h, t["qT"], jnp.zeros_like(t["qT"])), augq[c][h]], 0)
            s = dot(kaug, qaug) * (scale * LOG2E)
            es.append(jnp.exp2(s - jnp.max(s, 0, keepdims=True)).astype(BF))
        t["es"] = es
        t = st[c]
        a = dot(spread(t["vT"], ones), jnp.concatenate(t["es"], 0))
        r = 1.0 / a[width : width + heads]
        t["rb"] = jnp.concatenate([jnp.broadcast_to(r[h : h + 1], (hsize, qn)) for h in range(heads)], 0)
        t["aT"] = a[:width] * t["rb"]
        t = st[c]
        aT, gT, doT = t["aT"], t["gT"], t["doT"]
        daT = (doT * gT).astype(BF).astype(F32)
        t["dgT"] = (doT * aT * gT * (1.0 - gT)).astype(BF)
        t["dnT"] = (daT * t["rb"] * scale).astype(BF)
        prod = aT * t["dnT"].astype(F32)
        t["shift"] = [jnp.sum(prod[h * hsize : (h + 1) * hsize], 0, keepdims=True) for h in range(heads)]
    for c in crops:
        t = st[c]
        dps = dot(t["v"], spread(t["dnT"], None))
        t["ds"] = [
            (t["es"][h].astype(F32) * (dps[:, h * qn : (h + 1) * qn] - t["shift"][h])).astype(BF) for h in range(heads)
        ]
        t = st[c]
        oT = (t["aT"] * t["gT"]).astype(BF)
        outs.append(z[c] + dot(oT, w4, TN))
        dw4 = dw4 + dot(oT, co[c])
        t = st[c]
        dk, dv = [], []
        for h in range(heads):
            rows = slice(h * hsize, (h + 1) * hsize)
            dk.append(dot(t["qT"][rows], t["ds"][h], NT))
            dv.append(dot(t["dnT"][rows], t["es"][h], NT) * (1.0 / scale))
        t["dkv"] = jnp.concatenate(dk + dv, 0)
    for c in crops:
        t = st[c]
        tile_k = jnp.concatenate([hotk[c][:4].astype(F32)] * 4, 0)
        tile_q = jnp.concatenate([hotq[c][:4].astype(F32)] * 4, 0)
        x = dot(
            spread(t["kT"], [jnp.where(row16 // 4 == h, tile_k, 0.0).astype(BF) for h in range(heads)]),
            jnp.concatenate(t["ds"], 0),
        )
        for h in range(heads):
            part = jnp.where(row16 // 4 == h, x[width : width + 16] * tile_q, 0.0)
            db[h] = db[h] + part[:8] + part[8:]
        dqgT.append(jnp.concatenate([x[:width].astype(BF), t["dgT"]], 0))
        dkv = t["dkv"]
        dkA.append(dkv[:, :qn].astype(BF))
        dkP = dkv[:, qn:] if dkP is None else dkP + dkv[:, qn:]
    dqgT = jnp.concatenate(dqgT, 1)
    dkvT = jnp.concatenate(dkA + [dkP.astype(BF)], 1)
    dwqg = dot(dqgT, jnp.concatenate(yown, 0))
    dwkv = dot(dkvT, yall)
    dy_own = jnp.transpose(dot(wqg, dqgT))
    dy_all = jnp.transpose(dot(wkv, dkvT))
    return outs, dy_own, dy_all, dwqg, dwkv, dw4, db


def moments(value, grad, first, second):
    first_new = beta_one * first + (1.0 - beta_one) * grad
    second_new = beta_two * second + (1.0 - beta_two) * grad * grad
    step_dir = (
        first_new
        / (1.0 - beta_one**STEP)
        / (jnp.sqrt(second_new / (1.0 - beta_two**STEP)) + epsilon)
        + decay * value
    )
    return (first_new, second_new, step_dir)


def blocks_of(rank, units, light, heavy, half, gc):
    far = rank < half // 2
    first = rank * light if far else half // 2 * light + (rank - half // 2) * heavy
    count = light if far else heavy
    return sorted({(first + (count - 1 - u if rank % 2 else u)) // gc for u in units if u < count})


def early_blocks(light, heavy, half, gc):
    late = set()
    for r in range(half):
        count = light if r < half // 2 else heavy
        units = [u for u in range(count) if -(-((u + 1) * heavy) // count) > heavy - 8]
        late |= set(blocks_of(r, units, light, heavy, half, gc))
    return [b for b in range(half // 2 * (light + heavy) // gc) if b not in late]


def main_kernel(dims, names, *refs):
    nrow, ncol, crops, light, heavy, rl, width, heads, wr, direct = dims
    pair_ref, cot_ref, seg_ref, len_ref, w_ref, m1_ref, m2_ref, gain_ref, bias_ref = refs[:9]
    srcs = (pair_ref, cot_ref)
    s = dict(zip(names, refs[9:]))
    zin, y3, d3, own, xring, iring, yring = (s[n] for n in ("zin", "y3", "d3", "own", "xring", "iring", "yring"))
    in_sem, send_sem, ret_sem, rsend_sem = s["in_sem"], s["send_sem"], s["ret_sem"], s["rsend_sem"]
    misc_recv, misc_send, y_sem, d_sem, x_send = (
        s[n] for n in ("misc_recv", "misc_send", "y_sem", "d_sem", "x_send")
    )
    red_ref, nrm_ref = s["red"], s["nrm"]
    half = nrow // 2
    qn = half * rl
    gc = 16 if direct else half // 2 * (light + heavy)
    ring = xring.shape[0]
    cols = s["cols"]
    nblocks = (half // 2 * (light + heavy)) // gc
    hsize = width // heads
    scale = 1.0 / math.sqrt(hsize)
    slots = s["wrow"].shape[1]
    me = lax.axis_index("row")
    mc = lax.axis_index("col")
    side = me // half
    place = lax.rem(me, half)

    def rank_of(at_side, w):
        return lax.rem(w + at_side * (half // 2), half)

    def first_of(rank):
        near_rank = rank - half // 2
        return jnp.where(near_rank < 0, rank * light, (half // 2) * light + near_rank * heavy)

    def column_at(there, u):
        count = jnp.where(there < half // 2, light, heavy)
        return first_of(there) + jnp.where(lax.rem(there, 2) == 1, count - 1 - u, u)

    rank = rank_of(side, place)
    is_heavy = rank >= half // 2
    partner = ((1 - side) * half + rank_of(1 - side, rank), mc)

    def active(heavy_one, n):
        return heavy_one | (((n + 1) * light) // heavy > (n * light) // heavy)

    def unit_of(heavy_one, n):
        return jnp.where(heavy_one, n, (n * light) // heavy)

    def row_peer(d):
        return lax.rem(me + d, nrow)

    def col_peer(d):
        return lax.rem(mc + d, ncol)

    def near(d):
        return lax.rem(place + d, half)

    def device(w):
        return (side * half + w, mc)

    def load_block(b, slot):
        for c in range(crops):
            for a in range(2):
                pltpu.make_async_copy(
                    srcs[a].at[c, :, pl.ds(b * gc, gc), :],
                    s["raw"].at[slot, c, a],
                    s["raw_sem"].at[slot, c, a],
                ).start()

    if direct:
        needs = [blocks_of(r, range(LEAD), light, heavy, half, gc) for r in range(half)]
        order = []
        for need in needs[half // 2 :] + needs[: half // 2]:
            order += [b for b in need if b not in order]
        order += [b for b in range(nblocks) if b not in order]
        done_blocks = 0
        nslot = s["raw"].shape[0]
        for n in range(nslot):
            load_block(order[n], n)

    barrier = pltpu.get_barrier_semaphore()

    def greet_row(d, _):
        pl.semaphore_signal(barrier, inc=1, device_id=(row_peer(d), mc), device_id_type=MESH)
        return 0

    def greet_col(d, _):
        pl.semaphore_signal(barrier, inc=1, device_id=(me, col_peer(d)), device_id_type=MESH)
        return 0

    lax.fori_loop(1, nrow, greet_row, 0)
    lax.fori_loop(1, ncol, greet_col, 0)
    for j in range(wr):
        s["wtmp"][0:5, j, :] = w_ref[:, j * width : (j + 1) * width]
    for k in range(slots * ncol):
        s["wsend"][k] = (s["wtmp"][k] if k < 5 else jnp.zeros((wr, width), F32)).astype(s["wsend"].dtype)
    pl.semaphore_wait(barrier, nrow - 1 + ncol - 1)

    def remote(src, dst, send, recv, peer):
        pltpu.make_async_remote_copy(
            src, dst, send, recv, device_id=peer, device_id_type=MESH
        ).start()

    def exchange_row(src_of, dst, n):
        def push(d, _):
            p = row_peer(d)
            remote(src_of(p), dst.at[me], misc_send.at[n], misc_recv.at[n], (p, mc))
            return 0

        lax.fori_loop(1, nrow, push, 0)
        pltpu.make_async_copy(src_of(me), dst.at[me], misc_recv.at[n]).start()

    def exchange_col(src_of, dst, n):
        def push(d, _):
            p = col_peer(d)
            remote(src_of(p), dst.at[mc], misc_send.at[n], misc_recv.at[n], (me, p))
            return 0

        lax.fori_loop(1, ncol, push, 0)
        pltpu.make_async_copy(src_of(mc), dst.at[mc], misc_recv.at[n]).start()

    def landed(dst, n):
        pltpu.make_async_copy(dst, dst, misc_recv.at[n]).wait()

    def total_of(ref, n):
        return lax.fori_loop(1, n, lambda r, t: t + ref[r].astype(F32), ref[0].astype(F32))

    exchange_row(lambda p: s["wsend"].at[pl.ds(mc * slots, slots)], s["wrow"], 0)

    def column_of(col):
        return s["sbuf"].at[col] if direct else pair_ref.at[col]

    def push_turn(n):
        def to_peer(d, _):
            w = near(d)
            there = rank_of(side, w)
            to_heavy = there >= half // 2
            u = unit_of(to_heavy, n)

            @pl.when(active(to_heavy, n))
            def _():
                src = column_of(column_at(there, u))
                remote(src, zin.at[u, :, :, place], send_sem.at[0], in_sem.at[u], device(w))

            return 0

        lax.fori_loop(1, half, to_peer, 0)
        mine = unit_of(is_heavy, n)

        @pl.when(active(is_heavy, n))
        def _():
            src = column_of(column_at(rank, mine))
            pltpu.make_async_copy(src, zin.at[mine, :, :, place], in_sem.at[mine]).start()

    def push_turns(first, last):
        def at_turn(n, _):
            push_turn(n)
            return 0

        lax.fori_loop(first, last, at_turn, 0)

    def turn_block(n):
        b, slot = order[n], n % nslot
        for c in range(crops):
            for a in range(2):
                here = s["raw"].at[slot, c, a]
                pltpu.make_async_copy(here, here, s["raw_sem"].at[slot, c, a]).wait()
                s["stage"][a] = s["raw"][slot, c, a].astype(F32).reshape(rl * gc, width)
                for j in range(gc):
                    s["sbuf"][b * gc + j, c, a] = s["stage"][a, pl.ds(j, rl, stride=gc), :].astype(BF)
        if n + nslot < len(order):
            load_block(order[n + nslot], slot)

    def push_one(there, n):
        to_heavy = there >= half // 2
        u = unit_of(to_heavy, n)

        @pl.when(active(to_heavy, n) & (there == rank))
        def _():
            src = column_of(column_at(rank, u))
            pltpu.make_async_copy(src, zin.at[u, :, :, place], in_sem.at[u]).start()

        @pl.when(active(to_heavy, n) & (there != rank))
        def _():
            src = column_of(column_at(there, u))
            remote(src, zin.at[u, :, :, place], send_sem.at[0], in_sem.at[u], device(rank_of(side, there)))

    if direct:
        for there in list(range(half // 2, half)) + list(range(half // 2)):
            for b in needs[there]:
                if b in order[:done_blocks]:
                    continue
                turn_block(order.index(b))
                done_blocks += 1
            for n in range(EARLY):
                push_one(there, n)
        push_turns(EARLY, LEAD)
    else:
        push_turns(0, LEAD)

    back = lax.broadcasted_iota(jnp.int32, (qn, qn), 0) + lax.broadcasted_iota(jnp.int32, (qn, qn), 1)
    s["rev"][...] = jnp.where(back == qn - 1, 1.0, 0.0).astype(BF)

    where_t = lax.broadcasted_iota(jnp.int32, (qn, 1), 0)

    def prepare(u, at):
        pltpu.make_async_copy(zin.at[u], zin.at[u], in_sem.at[u]).wait()
        for c in range(crops):
            rows = slice(c * qn, (c + 1) * qn)
            xhat, inv, y = normed(zin[u, c, 0].astype(F32).reshape(qn, width), gain_ref[...])
            xring[at, rows, :] = xhat
            iring[at, rows, :] = jnp.broadcast_to(inv, (qn, width))
            yring[at, rows, :] = y

        @pl.when(side == 0)
        def _():
            y3[u, 0 : 2 * qn, :] = yring[at]
            part = y3.at[u, pl.ds(0, 2 * qn)]
            remote(part, part, x_send.at[0], y_sem.at[u], partner)

        @pl.when(side == 1)
        def _():
            y1 = dot(s["rev"][...], yring[at, qn : 2 * qn, :])
            y0 = yring[at, 0:qn, :].astype(F32)
            y3[u, 2 * qn : 3 * qn, :] = jnp.where(where_t < len_ref[0] - qn, y0, y1).astype(BF)
            part = y3.at[u, pl.ds(2 * qn, qn)]
            remote(part, part, x_send.at[0], y_sem.at[u], partner)

    def at_turn(t, act):
        @pl.when((t >= 0) & (t < heavy) & active(is_heavy, t))
        def _():
            act(unit_of(is_heavy, t), lax.rem(t, ring))

    def early_turn(n, _):
        at_turn(n, prepare)
        return 0

    lax.fori_loop(0, 1, early_turn, 0)
    if direct:
        for n in range(done_blocks, nblocks):
            turn_block(n)
    lax.fori_loop(1, AHEAD, early_turn, 0)

    landed(s["wrow"], 0)
    exchange_col(lambda p: s["wrow"], s["wall"], 1)

    lane = lax.broadcasted_iota(jnp.int32, (1, qn), 1)
    line = lax.broadcasted_iota(jnp.int32, (width, 1), 0)
    for c in range(crops):
        low_seg, high_seg = seg_ref[c : c + 1, :qn], seg_ref[c : c + 1, qn:]
        own_seg = jnp.where(side == 0, low_seg, high_seg)
        same_low = (lax.rem(line, SEGS) == low_seg).astype(F32)
        same_high = (lax.rem(line, SEGS) == high_seg).astype(F32)
        pad = jnp.where(lane + qn >= len_ref[c], -1e30, 0.0)
        if c == 1:
            same_high = dot(same_high.astype(BF), s["rev"][...])
            pad = jnp.where(2 * qn - 1 - lane >= len_ref[c], -1e30, 0.0)
        same = jnp.concatenate([same_low, same_high], 1)
        pad = jnp.concatenate([jnp.zeros((1, qn), F32), pad], 1)
        s["hotk"][c] = jnp.where(line[:16] < SEGS, same[:16], 0.0).astype(BF)
        rowsk = jnp.where(line < 3 * SEGS, same, jnp.where(line == 3 * SEGS, pad, 0.0))
        s["augk"][c] = jnp.transpose(rowsk).astype(BF)
        same = (lax.rem(line, SEGS) == own_seg).astype(F32)
        s["hotq"][c] = jnp.where(line[:16] < SEGS, same[:16], 0.0).astype(BF)
        for h in range(heads):
            full = jnp.full((width, 1), bias_ref[h] * (1.0 / scale), F32)
            high = full.astype(BF).astype(F32)
            mid = (full - high).astype(BF).astype(F32)
            low = full - high - mid
            part = jnp.where(line < SEGS, high, jnp.where(line < 2 * SEGS, mid, low))
            rowsq = jnp.where(line < 3 * SEGS, same * part, jnp.where(line == 3 * SEGS, 1.0, 0.0))
            s["augq"][c, h] = rowsq.astype(BF)

    for name in ("dwqg_acc", "dwkv_acc", "dw4_acc", "dg_acc", "db_acc"):
        s[name][...] = jnp.zeros_like(s[name])

    landed(s["wall"], 1)
    for k in range(5):
        w = s["wall"][k // slots, :, k % slots].astype(F32).reshape(width, width)
        if k == 4:
            s["w4"][...] = w.astype(BF)
        else:
            name, at = {0: ("wqg", 0), 3: ("wqg", 1), 1: ("wkv", 0), 2: ("wkv", 1)}[k]
            s[name][:, at * width : (at + 1) * width] = w.astype(BF)
            s[name + "_t"][at * width : (at + 1) * width, :] = jnp.transpose(w).astype(BF)

    def give(u, a):
        col = column_at(rank, u)
        here = cols.at[a, :, pl.ds(col * rl, rl)]
        landing = ret_sem.at[col // gc]

        def to_peer(d, _):
            w = near(d)
            remote(zin.at[u, :, a, w], here, rsend_sem.at[0], landing, device(w))
            return 0

        lax.fori_loop(1, half, to_peer, 0)
        pltpu.make_async_copy(zin.at[u, :, a, place], here, landing).start()

    def work(u, at):
        @pl.when(side == 0)
        def _():
            part = y3.at[u, pl.ds(2 * qn, qn)]
            pltpu.make_async_copy(part, part, y_sem.at[u]).wait()

        @pl.when(side == 1)
        def _():
            part = y3.at[u, pl.ds(0, 2 * qn)]
            pltpu.make_async_copy(part, part, y_sem.at[u]).wait()

        outs, dy_own, dy_all, dwqg, dwkv, dw4, db = attend(
            [zin[u, c, 0].astype(F32).reshape(qn, width) for c in range(crops)],
            [zin[u, c, 1].astype(F32).reshape(qn, width).astype(BF) for c in range(crops)],
            [yring[at, c * qn : (c + 1) * qn, :] for c in range(crops)],
            y3[u],
            s["wqg_t"][...],
            s["wkv"][...],
            s["wkv_t"][...],
            s["w4"][...],
            s["wqg"][...],
            [s["augk"][c] for c in range(crops)],
            [[s["augq"][c, h] for h in range(heads)] for c in range(crops)],
            [s["hotk"][c] for c in range(crops)],
            [s["hotq"][c] for c in range(crops)],
            heads,
        )
        s["dwqg_acc"][...] += dwqg
        s["dwkv_acc"][...] += dwkv
        s["dw4_acc"][...] += dw4
        for h in range(heads):
            s["db_acc"][h] += db[h]
        @pl.when(side == 0)
        def _():
            own[at, 0 : 2 * qn, :] = dy_own + dy_all[0 : 2 * qn]
            d3[u, 2 * qn : 3 * qn, :] = dy_all[2 * qn :].astype(BF)
            part = d3.at[u, pl.ds(2 * qn, qn)]
            remote(part, part, x_send.at[1], d_sem.at[u], partner)

        @pl.when(side == 1)
        def _():
            own[at, 0 : 2 * qn, :] = dy_own
            own[at, 2 * qn : 3 * qn, :] = dy_all[2 * qn :]
            d3[u, 0 : 2 * qn, :] = dy_all[0 : 2 * qn].astype(BF)
            part = d3.at[u, pl.ds(0, 2 * qn)]
            remote(part, part, x_send.at[1], d_sem.at[u], partner)

        for c in range(crops):
            zin[u, c, 0] = outs[c].reshape(half, rl, width).astype(BF)
        give(u, 0)

    def finish(u, at):

        @pl.when(side == 0)
        def _():
            part = d3.at[u, pl.ds(0, 2 * qn)]
            pltpu.make_async_copy(part, part, d_sem.at[u]).wait()
            own[at, 0 : 2 * qn, :] += d3[u, 0 : 2 * qn, :].astype(F32)

        @pl.when(side == 1)
        def _():
            part = d3.at[u, pl.ds(2 * qn, qn)]
            pltpu.make_async_copy(part, part, d_sem.at[u]).wait()
            both = own[at, 2 * qn : 3 * qn, :] + d3[u, 2 * qn : 3 * qn, :].astype(F32)
            mine = where_t < len_ref[0] - qn
            own[at, 0:qn, :] += jnp.where(mine, both, 0.0)
            own[at, qn : 2 * qn, :] += dot(s["rev"][...], jnp.where(mine, 0.0, both).astype(BF))

        for c in range(crops):
            rows = slice(c * qn, (c + 1) * qn)
            dy, xhat = own[at, rows, :], xring[at, rows, :]
            s["dg_acc"][0:1] += jnp.sum(dy * xhat, 0, keepdims=True)
            dx = dy * gain_ref[...]
            rest = dx - jnp.mean(dx, -1, keepdims=True) - xhat * jnp.mean(dx * xhat, -1, keepdims=True)
            grad = zin[u, c, 1].astype(F32).reshape(qn, width) + iring[at, rows, :] * rest
            zin[u, c, 1] = grad.reshape(half, rl, width).astype(BF)
        give(u, 1)

    def step(it, _):
        at_turn(it + AHEAD, prepare)

        @pl.when(it + LEAD < heavy)
        def _():
            push_turn(it + LEAD)

        at_turn(it, work)
        at_turn(it - LAG, finish)
        return 0

    lax.fori_loop(0, heavy, step, 0)

    def turn_back(b):
        block = cols.at[:, :, pl.ds(b * gc * rl, gc * rl)]
        pltpu.make_async_copy(block, block, ret_sem.at[b]).wait()
        rows = slice(b * gc * rl, (b + 1) * gc * rl)
        for c in range(crops):
            for a in range(2):
                for j in range(gc):
                    at = (b * gc + j) * rl
                    s["stage"][a, pl.ds(j, rl, stride=gc), :] = cols[a, c, at : at + rl, :].astype(F32)
                cols[a, c, rows, :] = s["stage"][a].astype(BF)

    soon = early_blocks(light, heavy, half, gc) if direct else []

    gsend = s["gsend"]
    for k, (name, at) in enumerate((("dwqg_acc", 0), ("dwkv_acc", 0), ("dwkv_acc", 1), ("dwqg_acc", 1))):
        gsend[k] = jnp.transpose(s[name][at * width : (at + 1) * width, :]).astype(gsend.dtype)
    gsend[4] = s["dw4_acc"][...].astype(gsend.dtype)
    spot = lax.broadcasted_iota(jnp.int32, (1, width), 1)
    dbias = jnp.zeros((1, width), F32)
    for h in range(heads):
        total_h = jnp.sum(jnp.sum(s["db_acc"][h], 0, keepdims=True), 1, keepdims=True)
        dbias = jnp.where(spot == h, total_h * (1.0 / scale), dbias)
    for k in range(5, slots * ncol):
        gsend[k] = jnp.zeros((width, width), gsend.dtype)
    exchange_col(lambda p: gsend.at[pl.ds(p * slots, slots)], s["grecv"], 2)

    def last_turn(t, _):
        at_turn(t, finish)
        return 0

    lax.fori_loop(heavy - LAG, heavy, last_turn, 0)
    s["vsend"][0, 0:1, :] = s["dg_acc"][0:1]
    s["vsend"][0, 1:2, :] = dbias
    exchange_row(lambda p: s["vsend"].at[0], s["vrow"], 6)
    landed(s["grecv"], 2)
    share = total_of(s["grecv"], ncol)
    for p in range(nrow):
        s["ssend"][p] = share[:, p * wr : (p + 1) * wr, :].astype(s["ssend"].dtype)
    exchange_row(lambda p: s["ssend"].at[p], s["srecv"], 3)
    for b in soon[0::3]:
        turn_back(b)
    landed(s["vrow"], 6)
    s["vsend"][1] = total_of(s["vrow"], nrow)
    exchange_col(lambda p: s["vsend"].at[1], s["vcol"], 7)
    landed(s["srecv"], 3)
    s["csend"][...] = total_of(s["srecv"], nrow)
    exchange_col(lambda p: s["csend"], s["crecv"], 4)
    for b in soon[1::3]:
        turn_back(b)
    landed(s["crecv"], 4)
    landed(s["vcol"], 7)
    for j in range(wr):
        red_ref[:, j * width : (j + 1) * width] = s["crecv"][:, :, j, :].reshape(slots * ncol, width)
    red_ref[5:7, 0:width] = total_of(s["vcol"], ncol)
    wval = w_ref[...]
    step_w = moments(wval, red_ref[0:5, :], m1_ref[...], m2_ref[...])[2]
    row5 = lax.broadcasted_iota(jnp.int32, (5, 1), 0)
    squares = jnp.where(spot == row5, jnp.sum(wval * wval, 1, keepdims=True), 0.0)
    squares += jnp.where(spot == row5 + 8, jnp.sum(step_w * step_w, 1, keepdims=True), 0.0)
    s["nsend"][...] = jnp.sum(squares, 0, keepdims=True)
    exchange_row(lambda p: s["nsend"], s["nrecv"], 5)
    for b in soon[2::3]:
        turn_back(b)
    landed(s["nrecv"], 5)
    nrm_ref[...] = total_of(s["nrecv"], nrow)

    for b in range(nblocks):
        if b not in soon:
            block = cols.at[:, :, pl.ds(b * gc * rl, gc * rl)]
            pltpu.make_async_copy(block, block, ret_sem.at[b]).wait()

    def ended(count):
        sent = s["sbuf"] if direct else pair_ref
        sent = sent.at[pl.ds(0, half // 2 * (light + heavy) - count)]
        pltpu.make_async_copy(sent, sent, send_sem.at[0]).wait()
        gone = zin.at[pl.ds(0, count), :, :, pl.ds(0, half - 1)]
        pltpu.make_async_copy(gone, gone, rsend_sem.at[0]).wait()
        for at_side, rows_y, rows_d in ((0, 2 * qn, qn), (1, qn, 2 * qn)):

            @pl.when(side == at_side)
            def _():
                part = y3.at[pl.ds(0, count), pl.ds(0, rows_y)]
                pltpu.make_async_copy(part, part, x_send.at[0]).wait()
                part = d3.at[pl.ds(0, count), pl.ds(0, rows_d)]
                pltpu.make_async_copy(part, part, x_send.at[1]).wait()

    for kind, count in ((False, light), (True, heavy)):

        @pl.when(is_heavy == kind)
        def _():
            ended(count)

    for n, name in enumerate(
        ("wrow", "wall", "grecv", "srecv", "crecv", "nrecv", "vrow", "vcol")
    ):
        sent = s[name].at[pl.ds(0, s[name].shape[0] - 1)]
        pltpu.make_async_copy(sent, sent, misc_send.at[n]).wait()


def step_kernel(direct, soon, *refs):
    if direct:
        cols, blocks, refs = refs[0], refs[1], refs[2:]
    red_ref, nrm_ref, w_ref, m1_ref, m2_ref, gain_ref, gm_ref, gv_ref, bias_ref, bm_ref, bv_ref = refs[:11]
    refs = refs[11:]
    if direct:
        bigs, refs = refs[0:2], refs[2:11] + refs[11:]
        refs, (slot, stage, sem) = refs[:9], refs[9:]
        _, crops, _, width = cols.shape
        _, rl, cl, _ = bigs[0].shape
        gc = 16
        copies = []

        def put(src, a, c, b):
            n = len(copies)
            copy = pltpu.make_async_copy(src, bigs[a].at[c, :, pl.ds(b * gc, gc), :], sem.at[n])
            copy.start()
            copies.append(copy)

        for b in soon:
            for c in range(crops):
                for a in range(2):
                    put(blocks.at[a, c, b], a, c, b)
        late = [b for b in range(cl // gc) if b not in soon]
        for n, b in enumerate(late):
            for c in range(crops):
                for a in range(2):
                    for j in range(gc):
                        at = (b * gc + j) * rl
                        stage[a, pl.ds(j, rl, stride=gc), :] = cols[a, c, at : at + rl, :].astype(F32)
                    slot[n, c, a] = stage[a].reshape(rl, gc, width).astype(BF)
                    put(slot.at[n, c, a], a, c, b)
    nw_ref, n1_ref, n2_ref, ng_ref, ngm_ref, ngv_ref, nb_ref, nbm_ref, nbv_ref = refs
    width = gain_ref.shape[1]
    heads = bias_ref.shape[1]
    wval = w_ref[...]
    first, second, step_w = moments(wval, red_ref[0:5, :], m1_ref[...], m2_ref[...])
    spot = lax.broadcasted_iota(jnp.int32, (1, width), 1)
    place = lax.broadcasted_iota(jnp.int32, (5, 1), 0)
    value_sq = jnp.sum(jnp.where(spot == place, nrm_ref[...], 0.0), 1, keepdims=True)
    step_sq = jnp.sum(jnp.where(spot == place + 8, nrm_ref[...], 0.0), 1, keepdims=True)
    nw_ref[...] = wval - rate * (jnp.sqrt(value_sq) / jnp.sqrt(step_sq)) * step_w
    n1_ref[...] = first
    n2_ref[...] = second
    for row, n, own in (
        (5, width, (gain_ref, gm_ref, gv_ref, ng_ref, ngm_ref, ngv_ref)),
        (6, heads, (bias_ref, bm_ref, bv_ref, nb_ref, nbm_ref, nbv_ref)),
    ):
        val = own[0][...]
        first, second, step_v = moments(val, red_ref[row : row + 1, 0:n], own[1][...], own[2][...])
        ratio = jnp.sqrt(jnp.sum(val * val, 1, keepdims=True)) / jnp.sqrt(
            jnp.sum(step_v * step_v, 1, keepdims=True)
        )
        own[3][...] = val - rate * ratio * step_v
        own[4][...] = first
        own[5][...] = second
    if direct:
        for copy in copies:
            copy.wait()


def body(
    nrow,
    ncol,
    pair,
    cotangent,
    segments,
    lengths,
    weights,
    moment_one,
    moment_two,
    gain,
    gain_m,
    gain_v,
    chain_bias,
    bias_m,
    bias_v,
):
    crops, rl, cl, width = pair.shape
    heads = chain_bias.shape[0]
    half = nrow // 2
    qn = half * rl
    wr = weights.shape[1] // width
    slots = -(-8 // ncol)
    direct = cl % 16 == 0 and rl % 16 == 0
    pairs = cl // (half // 2)
    light = LIGHT if direct and pairs == 64 else pairs // 2
    heavy = pairs - light
    dims = (nrow, ncol, crops, light, heavy, rl, width, heads, wr, direct)
    wtype = BF if wr % 16 == 0 else F32
    ring = AHEAD + LAG + 1
    hbm = pl.BlockSpec(memory_space=pl.ANY)
    vmem = pl.BlockSpec(memory_space=pltpu.VMEM)
    smem = pl.BlockSpec(memory_space=pltpu.SMEM)
    dma = pltpu.SemaphoreType.DMA
    outs = {
        "red": pltpu.VMEM((slots * ncol, wr * width), F32),
        "nrm": pltpu.VMEM((1, width), F32),
        "cols": pltpu.VMEM((2, crops, cl * rl, width), BF),
    }
    scratch = {
        "zin": pltpu.VMEM((heavy, crops, 2, half, rl, width), BF),
        "y3": pltpu.VMEM((heavy, 3 * qn, width), BF),
        "d3": pltpu.VMEM((heavy, 3 * qn, width), BF),
        "own": pltpu.VMEM((ring, 3 * qn, width), F32),
        "xring": pltpu.VMEM((ring, 2 * qn, width), F32),
        "iring": pltpu.VMEM((ring, 2 * qn, width), F32),
        "yring": pltpu.VMEM((ring, 2 * qn, width), BF),
        "rev": pltpu.VMEM((qn, qn), BF),
        "wtmp": pltpu.VMEM((8, wr, width), F32),
        "wsend": pltpu.VMEM((slots * ncol, wr, width), wtype),
        "wrow": pltpu.VMEM((nrow, slots, wr, width), wtype),
        "wall": pltpu.VMEM((ncol, nrow, slots, wr, width), wtype),
        "gsend": pltpu.VMEM((slots * ncol, width, width), wtype),
        "grecv": pltpu.VMEM((ncol, slots, width, width), wtype),
        "ssend": pltpu.VMEM((nrow, slots, wr, width), wtype),
        "srecv": pltpu.VMEM((nrow, slots, wr, width), wtype),
        "csend": pltpu.VMEM((slots, wr, width), F32),
        "crecv": pltpu.VMEM((ncol, slots, wr, width), F32),
        "vsend": pltpu.VMEM((2, 2, width), F32),
        "vrow": pltpu.VMEM((nrow, 2, width), F32),
        "vcol": pltpu.VMEM((ncol, 2, width), F32),
        "nsend": pltpu.VMEM((1, width), F32),
        "nrecv": pltpu.VMEM((nrow, 1, width), F32),
        "wqg": pltpu.VMEM((width, 2 * width), BF),
        "wkv": pltpu.VMEM((width, 2 * width), BF),
        "wqg_t": pltpu.VMEM((2 * width, width), BF),
        "wkv_t": pltpu.VMEM((2 * width, width), BF),
        "w4": pltpu.VMEM((width, width), BF),
        "augk": pltpu.VMEM((crops, 2 * qn, width), BF),
        "augq": pltpu.VMEM((crops, heads, width, qn), BF),
        "hotk": pltpu.VMEM((crops, 16, 2 * qn), BF),
        "hotq": pltpu.VMEM((crops, 16, qn), BF),
        "dwqg_acc": pltpu.VMEM((2 * width, width), F32),
        "dwkv_acc": pltpu.VMEM((2 * width, width), F32),
        "dw4_acc": pltpu.VMEM((width, width), F32),
        "dg_acc": pltpu.VMEM((8, width), F32),
        "db_acc": pltpu.VMEM((heads, 8, qn), F32),
        "in_sem": dma((heavy,)),
        "y_sem": dma((heavy,)),
        "d_sem": dma((heavy,)),
        "send_sem": dma((1,)),
        "ret_sem": dma((cl // 16 if direct else 1,)),
        "rsend_sem": dma((1,)),
        "x_send": dma((2,)),
        "misc_recv": dma((8,)),
        "misc_send": dma((8,)),
    }
    if direct:
        sources = (pair, cotangent)
        scratch["raw"] = pltpu.VMEM((3, crops, 2, rl, 16, width), BF)
        scratch["sbuf"] = pltpu.VMEM((cl, crops, 2, rl, width), BF)
        scratch["stage"] = pltpu.VMEM((2, rl * 16, width), F32)
        scratch["raw_sem"] = dma((3, crops, 2))
    else:
        sources = (jnp.transpose(jnp.stack([pair, cotangent], 1), (3, 0, 1, 2, 4)), cotangent)
    names = tuple(outs) + tuple(scratch)
    res1 = pl.pallas_call(
        functools.partial(main_kernel, dims, names),
        out_shape=tuple(outs.values()),
        in_specs=[hbm, hbm, vmem, smem, vmem, vmem, vmem, vmem, smem],
        out_specs=(vmem,) * len(outs),
        scratch_shapes=list(scratch.values()),
        compiler_params=pltpu.CompilerParams(
            collective_id=0, has_side_effects=True, vmem_limit_bytes=55 << 20
        ),
        name="column_attention",
    )(
        *(
            pltpu.with_memory_space_constraint(x, pltpu.HBM)
            for x in (
                *sources,
                segments,
                lengths,
                weights,
                moment_one,
                moment_two,
                gain.reshape(1, width),
                chain_bias,
            )
        )
    )
    res1 = dict(zip(outs, res1))
    small = (gain, gain_m, gain_v, chain_bias, bias_m, bias_v)
    ops = [res1["red"], res1["nrm"], weights, moment_one, moment_two] + [a.reshape(1, -1) for a in small]
    fin = jax.ShapeDtypeStruct(pair.shape, BF)
    bigs = [fin, fin] if direct else []
    count = 2 * crops * (cl // 16)
    soon = early_blocks(light, heavy, half, 16) if direct else []
    turned = ()
    if direct:
        turned = (res1["cols"], res1["cols"].reshape(2, crops, cl // 16, rl, 16, width))
    res = pl.pallas_call(
        functools.partial(step_kernel, direct, soon),
        out_shape=bigs
        + [jax.ShapeDtypeStruct(weights.shape, F32)] * 3
        + [jax.ShapeDtypeStruct((1, width), F32)] * 3
        + [jax.ShapeDtypeStruct((1, heads), F32)] * 3,
        in_specs=[vmem] * (len(ops) + len(turned)),
        out_specs=[hbm] * len(bigs) + [vmem] * 9,
        scratch_shapes=[
            pltpu.VMEM((cl // 16 - len(soon), crops, 2, rl, 16, width), BF),
            pltpu.VMEM((2, rl * 16, width), F32),
            dma((count,)),
        ]
        if direct
        else [],
        compiler_params=pltpu.CompilerParams(vmem_limit_bytes=18 << 20),
        name="lamb_step",
    )(*turned, *ops)
    if direct:
        fins, res = res[:2], res[2:]
    else:
        fins = [jnp.swapaxes(res1["cols"][a].reshape(crops, cl, rl, width), 1, 2) for a in range(2)]
    return (*fins, *res[:3], *[a.reshape(-1) for a in res[3:]])


def solution(mesh):
    big = P(None, "row", "col", None)
    shard = P(None, "row")
    return jax.shard_map(
        functools.partial(body, mesh.shape["row"], mesh.shape["col"]),
        mesh=mesh,
        in_specs=(big, big, P(), P(), shard, shard, shard) + (P(),) * 6,
        out_specs=(big, big, shard, shard, shard) + (P(),) * 6,
        check_vma=False,
    )
```

```python
import functools
import math

import jax
import jax.numpy as jnp
from jax import lax
from jax.experimental import pallas as pl
from jax.experimental.pallas import tpu as pltpu
from jax.sharding import PartitionSpec as P

STEP = 10
beta_one = 0.9
beta_two = 0.999
epsilon = 1e-06
decay = 0.01
rate = 0.25

BF = jnp.bfloat16
F32 = jnp.float32
MESH = pl.DeviceIdType.MESH
NT = ((1,), (1,))
TN = ((0,), (0,))
LOG2E = math.log2(math.e)
SEGS = 4
EARLY, LEAD, AHEAD, LAG = 2, 4, 2, 3
LIGHT = 22


def dot(a, b, dims=((1,), (0,))):
    return lax.dot_general(a, b, (dims, ((), ())), preferred_element_type=F32)


def normed(z, gain):
    mean = jnp.mean(z, -1, keepdims=True)
    cen = z - mean
    var = jnp.mean(cen * cen, -1, keepdims=True)
    inv = lax.rsqrt(var + 1e-05)
    xhat = cen * inv
    return xhat, inv, (xhat * gain).astype(BF)


def attend(z, co, yown, yall, wqg_t, wkv, wkv_t, w4, wqg, augk, augq, hotk, hotq, heads):
    qn, width = z[0].shape
    hsize = width // heads
    scale = 1.0 / math.sqrt(hsize)
    head_of = lax.broadcasted_iota(jnp.int32, (width, 1), 0) // hsize
    row16 = lax.broadcasted_iota(jnp.int32, (16, 1), 0)
    packed = slice(2 * qn, 3 * qn)

    def spread(xT, last):
        parts = [jnp.where(head_of == h, xT, jnp.zeros_like(xT)) for h in range(heads)]
        if last is not None:
            parts = [jnp.concatenate([p, x], 0) for p, x in zip(parts, last)]
        return jnp.concatenate(parts, 1)

    kv = dot(yall, wkv).astype(BF)
    kvT = dot(wkv_t, yall, NT).astype(BF)
    ones = [jnp.broadcast_to(jnp.where(row16 == h, 1.0, 0.0).astype(BF), (16, 2 * qn)) for h in range(heads)]
    crops = range(2)
    st = [{} for c in crops]
    for c in crops:
        t = st[c]
        first = slice(c * qn, (c + 1) * qn)
        t["k"] = jnp.concatenate([kv[first, :width], kv[packed, :width]], 0)
        t["v"] = jnp.concatenate([kv[first, width:], kv[packed, width:]], 0)
        bothT = jnp.concatenate([kvT[:, first], kvT[:, packed]], 1)
        t["kT"], t["vT"] = bothT[:width], bothT[width:]
        projT = dot(wqg_t, yown[c], NT)
        t["qT"] = projT[:width].astype(BF)
        t["gT"] = jax.nn.sigmoid(projT[width:])
        t["doT"] = dot(w4, co[c], NT).astype(BF).astype(F32)
    outs, dqgT, dkA, dkP = [], [], [], None
    dw4, db = 0.0, [0.0] * heads
    for c in crops:
        t = st[c]
        kaug = jnp.concatenate([t["k"], augk[c]], 1)
        es = []
        for h in range(heads):
            qaug = jnp.concatenate([jnp.where(head_of == h, t["qT"], jnp.zeros_like(t["qT"])), augq[c][h]], 0)
            s = dot(kaug, qaug) * (scale * LOG2E)
            es.append(jnp.exp2(s - jnp.max(s, 0, keepdims=True)).astype(BF))
        t["es"] = es
        t = st[c]
        a = dot(spread(t["vT"], ones), jnp.concatenate(t["es"], 0))
        r = 1.0 / a[width : width + heads]
        t["rb"] = jnp.concatenate([jnp.broadcast_to(r[h : h + 1], (hsize, qn)) for h in range(heads)], 0)
        t["aT"] = a[:width] * t["rb"]
        t = st[c]
        aT, gT, doT = t["aT"], t["gT"], t["doT"]
        daT = (doT * gT).astype(BF).astype(F32)
        t["dgT"] = (doT * aT * gT * (1.0 - gT)).astype(BF)
        t["dnT"] = (daT * t["rb"] * scale).astype(BF)
        prod = aT * t["dnT"].astype(F32)
        t["shift"] = [jnp.sum(prod[h * hsize : (h + 1) * hsize], 0, keepdims=True) for h in range(heads)]
    for c in crops:
        t = st[c]
        dps = dot(t["v"], spread(t["dnT"], None))
        t["ds"] = [
            (t["es"][h].astype(F32) * (dps[:, h * qn : (h + 1) * qn] - t["shift"][h])).astype(BF) for h in range(heads)
        ]
        t = st[c]
        oT = (t["aT"] * t["gT"]).astype(BF)
        outs.append(z[c] + dot(oT, w4, TN))
        dw4 = dw4 + dot(oT, co[c])
        t = st[c]
        dk, dv = [], []
        for h in range(heads):
            rows = slice(h * hsize, (h + 1) * hsize)
            dk.append(dot(t["qT"][rows], t["ds"][h], NT))
            dv.append(dot(t["dnT"][rows], t["es"][h], NT) * (1.0 / scale))
        t["dkv"] = jnp.concatenate(dk + dv, 0)
    for c in crops:
        t = st[c]
        tile_k = jnp.concatenate([hotk[c][:4].astype(F32)] * 4, 0)
        tile_q = jnp.concatenate([hotq[c][:4].astype(F32)] * 4, 0)
        x = dot(
            spread(t["kT"], [jnp.where(row16 // 4 == h, tile_k, 0.0).astype(BF) for h in range(heads)]),
            jnp.concatenate(t["ds"], 0),
        )
        for h in range(heads):
            part = jnp.where(row16 // 4 == h, x[width : width + 16] * tile_q, 0.0)
            db[h] = db[h] + part[:8] + part[8:]
        dqgT.append(jnp.concatenate([x[:width].astype(BF), t["dgT"]], 0))
        dkv = t["dkv"]
        dkA.append(dkv[:, :qn].astype(BF))
        dkP = dkv[:, qn:] if dkP is None else dkP + dkv[:, qn:]
    dqgT = jnp.concatenate(dqgT, 1)
    dkvT = jnp.concatenate(dkA + [dkP.astype(BF)], 1)
    dwqg = dot(dqgT, jnp.concatenate(yown, 0))
    dwkv = dot(dkvT, yall)
    dy_own = jnp.transpose(dot(wqg, dqgT))
    dy_all = jnp.transpose(dot(wkv, dkvT))
    return outs, dy_own, dy_all, dwqg, dwkv, dw4, db


def moments(value, grad, first, second):
    first_new = beta_one * first + (1.0 - beta_one) * grad
    second_new = beta_two * second + (1.0 - beta_two) * grad * grad
    step_dir = (
        first_new
        / (1.0 - beta_one**STEP)
        / (jnp.sqrt(second_new / (1.0 - beta_two**STEP)) + epsilon)
        + decay * value
    )
    return (first_new, second_new, step_dir)


def blocks_of(rank, units, light, heavy, half, gc):
    far = rank < half // 2
    first = rank * light if far else half // 2 * light + (rank - half // 2) * heavy
    count = light if far else heavy
    return sorted({(first + (count - 1 - u if rank % 2 else u)) // gc for u in units if u < count})


def early_blocks(light, heavy, half, gc):
    late = set()
    for r in range(half):
        count = light if r < half // 2 else heavy
        units = [u for u in range(count) if -(-((u + 1) * heavy) // count) > heavy - 6]
        late |= set(blocks_of(r, units, light, heavy, half, gc))
    return [b for b in range(half // 2 * (light + heavy) // gc) if b not in late]


def main_kernel(dims, names, *refs):
    nrow, ncol, crops, light, heavy, rl, width, heads, wr, direct = dims
    pair_ref, cot_ref, seg_ref, len_ref, w_ref, m1_ref, m2_ref, gain_ref, bias_ref = refs[:9]
    srcs = (pair_ref, cot_ref)
    s = dict(zip(names, refs[9:]))
    zin, y3, d3, own, xring, iring, yring = (s[n] for n in ("zin", "y3", "d3", "own", "xring", "iring", "yring"))
    in_sem, send_sem, ret_sem, rsend_sem = s["in_sem"], s["send_sem"], s["ret_sem"], s["rsend_sem"]
    misc_recv, misc_send, y_sem, d_sem, x_send = (
        s[n] for n in ("misc_recv", "misc_send", "y_sem", "d_sem", "x_send")
    )
    red_ref, nrm_ref = s["red"], s["nrm"]
    half = nrow // 2
    qn = half * rl
    gc = 16 if direct else half // 2 * (light + heavy)
    ring = xring.shape[0]
    cols = s["cols"]
    nblocks = (half // 2 * (light + heavy)) // gc
    hsize = width // heads
    scale = 1.0 / math.sqrt(hsize)
    slots = s["wrow"].shape[1]
    me = lax.axis_index("row")
    mc = lax.axis_index("col")
    side = me // half
    place = lax.rem(me, half)

    def rank_of(at_side, w):
        return lax.rem(w + at_side * (half // 2), half)

    def first_of(rank):
        near_rank = rank - half // 2
        return jnp.where(near_rank < 0, rank * light, (half // 2) * light + near_rank * heavy)

    def column_at(there, u):
        count = jnp.where(there < half // 2, light, heavy)
        return first_of(there) + jnp.where(lax.rem(there, 2) == 1, count - 1 - u, u)

    rank = rank_of(side, place)
    is_heavy = rank >= half // 2
    partner = ((1 - side) * half + rank_of(1 - side, rank), mc)

    def active(heavy_one, n):
        return heavy_one | (((n + 1) * light) // heavy > (n * light) // heavy)

    def unit_of(heavy_one, n):
        return jnp.where(heavy_one, n, (n * light) // heavy)

    def row_peer(d):
        return lax.rem(me + d, nrow)

    def col_peer(d):
        return lax.rem(mc + d, ncol)

    def near(d):
        return lax.rem(place + d, half)

    def device(w):
        return (side * half + w, mc)

    def load_block(b, slot):
        for c in range(crops):
            for a in range(2):
                pltpu.make_async_copy(
                    srcs[a].at[c, :, pl.ds(b * gc, gc), :],
                    s["raw"].at[slot, c, a],
                    s["raw_sem"].at[slot, c, a],
                ).start()

    if direct:
        needs = [blocks_of(r, range(LEAD), light, heavy, half, gc) for r in range(half)]
        order = []
        for need in needs[half // 2 :] + needs[: half // 2]:
            order += [b for b in need if b not in order]
        order += [b for b in range(nblocks) if b not in order]
        done_blocks = 0
        nslot = s["raw"].shape[0]
        for n in range(nslot):
            load_block(order[n], n)

    barrier = pltpu.get_barrier_semaphore()

    def greet_row(d, _):
        pl.semaphore_signal(barrier, inc=1, device_id=(row_peer(d), mc), device_id_type=MESH)
        return 0

    def greet_col(d, _):
        pl.semaphore_signal(barrier, inc=1, device_id=(me, col_peer(d)), device_id_type=MESH)
        return 0

    lax.fori_loop(1, nrow, greet_row, 0)
    lax.fori_loop(1, ncol, greet_col, 0)
    for j in range(wr):
        s["wtmp"][0:5, j, :] = w_ref[:, j * width : (j + 1) * width]
    for k in range(slots * ncol):
        s["wsend"][k] = (s["wtmp"][k] if k < 5 else jnp.zeros((wr, width), F32)).astype(s["wsend"].dtype)
    pl.semaphore_wait(barrier, nrow - 1 + ncol - 1)

    def remote(src, dst, send, recv, peer):
        pltpu.make_async_remote_copy(
            src, dst, send, recv, device_id=peer, device_id_type=MESH
        ).start()

    def exchange_row(src_of, dst, n):
        def push(d, _):
            p = row_peer(d)
            remote(src_of(p), dst.at[me], misc_send.at[n], misc_recv.at[n], (p, mc))
            return 0

        lax.fori_loop(1, nrow, push, 0)
        pltpu.make_async_copy(src_of(me), dst.at[me], misc_recv.at[n]).start()

    def exchange_col(src_of, dst, n):
        def push(d, _):
            p = col_peer(d)
            remote(src_of(p), dst.at[mc], misc_send.at[n], misc_recv.at[n], (me, p))
            return 0

        lax.fori_loop(1, ncol, push, 0)
        pltpu.make_async_copy(src_of(mc), dst.at[mc], misc_recv.at[n]).start()

    def landed(dst, n):
        pltpu.make_async_copy(dst, dst, misc_recv.at[n]).wait()

    def total_of(ref, n):
        return lax.fori_loop(1, n, lambda r, t: t + ref[r].astype(F32), ref[0].astype(F32))

    exchange_row(lambda p: s["wsend"].at[pl.ds(mc * slots, slots)], s["wrow"], 0)

    def column_of(col):
        return s["sbuf"].at[col] if direct else pair_ref.at[col]

    def push_turn(n):
        def to_peer(d, _):
            w = near(d)
            there = rank_of(side, w)
            to_heavy = there >= half // 2
            u = unit_of(to_heavy, n)

            @pl.when(active(to_heavy, n))
            def _():
                src = column_of(column_at(there, u))
                remote(src, zin.at[u, :, :, place], send_sem.at[0], in_sem.at[u], device(w))

            return 0

        lax.fori_loop(1, half, to_peer, 0)
        mine = unit_of(is_heavy, n)

        @pl.when(active(is_heavy, n))
        def _():
            src = column_of(column_at(rank, mine))
            pltpu.make_async_copy(src, zin.at[mine, :, :, place], in_sem.at[mine]).start()

    def push_turns(first, last):
        def at_turn(n, _):
            push_turn(n)
            return 0

        lax.fori_loop(first, last, at_turn, 0)

    def turn_block(n):
        b, slot = order[n], n % nslot
        for c in range(crops):
            for a in range(2):
                here = s["raw"].at[slot, c, a]
                pltpu.make_async_copy(here, here, s["raw_sem"].at[slot, c, a]).wait()
                s["stage"][a] = s["raw"][slot, c, a].astype(F32).reshape(rl * gc, width)
                for j in range(gc):
                    s["sbuf"][b * gc + j, c, a] = s["stage"][a, pl.ds(j, rl, stride=gc), :].astype(BF)
        if n + nslot < len(order):
            load_block(order[n + nslot], slot)

    def push_one(there, n):
        to_heavy = there >= half // 2
        u = unit_of(to_heavy, n)

        @pl.when(active(to_heavy, n) & (there == rank))
        def _():
            src = column_of(column_at(rank, u))
            pltpu.make_async_copy(src, zin.at[u, :, :, place], in_sem.at[u]).start()

        @pl.when(active(to_heavy, n) & (there != rank))
        def _():
            src = column_of(column_at(there, u))
            remote(src, zin.at[u, :, :, place], send_sem.at[0], in_sem.at[u], device(rank_of(side, there)))

    if direct:
        for there in list(range(half // 2, half)) + list(range(half // 2)):
            for b in needs[there]:
                if b in order[:done_blocks]:
                    continue
                turn_block(order.index(b))
                done_blocks += 1
            for n in range(EARLY):
                push_one(there, n)
        push_turns(EARLY, LEAD)
    else:
        push_turns(0, LEAD)

    back = lax.broadcasted_iota(jnp.int32, (qn, qn), 0) + lax.broadcasted_iota(jnp.int32, (qn, qn), 1)
    s["rev"][...] = jnp.where(back == qn - 1, 1.0, 0.0).astype(BF)

    where_t = lax.broadcasted_iota(jnp.int32, (qn, 1), 0)

    def prepare(u, at):
        pltpu.make_async_copy(zin.at[u], zin.at[u], in_sem.at[u]).wait()
        for c in range(crops):
            rows = slice(c * qn, (c + 1) * qn)
            xhat, inv, y = normed(zin[u, c, 0].astype(F32).reshape(qn, width), gain_ref[...])
            xring[at, rows, :] = xhat
            iring[at, rows, :] = jnp.broadcast_to(inv, (qn, width))
            yring[at, rows, :] = y

        @pl.when(side == 0)
        def _():
            y3[u, 0 : 2 * qn, :] = yring[at]
            part = y3.at[u, pl.ds(0, 2 * qn)]
            remote(part, part, x_send.at[0], y_sem.at[u], partner)

        @pl.when(side == 1)
        def _():
            y1 = dot(s["rev"][...], yring[at, qn : 2 * qn, :])
            y0 = yring[at, 0:qn, :].astype(F32)
            y3[u, 2 * qn : 3 * qn, :] = jnp.where(where_t < len_ref[0] - qn, y0, y1).astype(BF)
            part = y3.at[u, pl.ds(2 * qn, qn)]
            remote(part, part, x_send.at[0], y_sem.at[u], partner)

    def at_turn(t, act):
        @pl.when((t >= 0) & (t < heavy) & active(is_heavy, t))
        def _():
            act(unit_of(is_heavy, t), lax.rem(t, ring))

    def early_turn(n, _):
        at_turn(n, prepare)
        return 0

    lax.fori_loop(0, 1, early_turn, 0)
    if direct:
        for n in range(done_blocks, nblocks):
            turn_block(n)
    lax.fori_loop(1, AHEAD, early_turn, 0)

    landed(s["wrow"], 0)
    exchange_col(lambda p: s["wrow"], s["wall"], 1)

    lane = lax.broadcasted_iota(jnp.int32, (1, qn), 1)
    line = lax.broadcasted_iota(jnp.int32, (width, 1), 0)
    for c in range(crops):
        low_seg, high_seg = seg_ref[c : c + 1, :qn], seg_ref[c : c + 1, qn:]
        own_seg = jnp.where(side == 0, low_seg, high_seg)
        same_low = (lax.rem(line, SEGS) == low_seg).astype(F32)
        same_high = (lax.rem(line, SEGS) == high_seg).astype(F32)
        pad = jnp.where(lane + qn >= len_ref[c], -1e30, 0.0)
        if c == 1:
            same_high = dot(same_high.astype(BF), s["rev"][...])
            pad = jnp.where(2 * qn - 1 - lane >= len_ref[c], -1e30, 0.0)
        same = jnp.concatenate([same_low, same_high], 1)
        pad = jnp.concatenate([jnp.zeros((1, qn), F32), pad], 1)
        s["hotk"][c] = jnp.where(line[:16] < SEGS, same[:16], 0.0).astype(BF)
        rowsk = jnp.where(line < 3 * SEGS, same, jnp.where(line == 3 * SEGS, pad, 0.0))
        s["augk"][c] = jnp.transpose(rowsk).astype(BF)
        same = (lax.rem(line, SEGS) == own_seg).astype(F32)
        s["hotq"][c] = jnp.where(line[:16] < SEGS, same[:16], 0.0).astype(BF)
        for h in range(heads):
            full = jnp.full((width, 1), bias_ref[h] * (1.0 / scale), F32)
            high = full.astype(BF).astype(F32)
            mid = (full - high).astype(BF).astype(F32)
            low = full - high - mid
            part = jnp.where(line < SEGS, high, jnp.where(line < 2 * SEGS, mid, low))
            rowsq = jnp.where(line < 3 * SEGS, same * part, jnp.where(line == 3 * SEGS, 1.0, 0.0))
            s["augq"][c, h] = rowsq.astype(BF)

    for name in ("dwqg_acc", "dwkv_acc", "dw4_acc", "dg_acc", "db_acc"):
        s[name][...] = jnp.zeros_like(s[name])

    landed(s["wall"], 1)
    for k in range(5):
        w = s["wall"][k // slots, :, k % slots].astype(F32).reshape(width, width)
        if k == 4:
            s["w4"][...] = w.astype(BF)
        else:
            name, at = {0: ("wqg", 0), 3: ("wqg", 1), 1: ("wkv", 0), 2: ("wkv", 1)}[k]
            s[name][:, at * width : (at + 1) * width] = w.astype(BF)
            s[name + "_t"][at * width : (at + 1) * width, :] = jnp.transpose(w).astype(BF)

    def give(u, a):
        col = column_at(rank, u)
        here = cols.at[a, :, pl.ds(col * rl, rl)]
        landing = ret_sem.at[col // gc]

        def to_peer(d, _):
            w = near(d)
            remote(zin.at[u, :, a, w], here, rsend_sem.at[0], landing, device(w))
            return 0

        lax.fori_loop(1, half, to_peer, 0)
        pltpu.make_async_copy(zin.at[u, :, a, place], here, landing).start()

    def work(u, at):
        @pl.when(side == 0)
        def _():
            part = y3.at[u, pl.ds(2 * qn, qn)]
            pltpu.make_async_copy(part, part, y_sem.at[u]).wait()

        @pl.when(side == 1)
        def _():
            part = y3.at[u, pl.ds(0, 2 * qn)]
            pltpu.make_async_copy(part, part, y_sem.at[u]).wait()

        outs, dy_own, dy_all, dwqg, dwkv, dw4, db = attend(
            [zin[u, c, 0].astype(F32).reshape(qn, width) for c in range(crops)],
            [zin[u, c, 1].astype(F32).reshape(qn, width).astype(BF) for c in range(crops)],
            [yring[at, c * qn : (c + 1) * qn, :] for c in range(crops)],
            y3[u],
            s["wqg_t"][...],
            s["wkv"][...],
            s["wkv_t"][...],
            s["w4"][...],
            s["wqg"][...],
            [s["augk"][c] for c in range(crops)],
            [[s["augq"][c, h] for h in range(heads)] for c in range(crops)],
            [s["hotk"][c] for c in range(crops)],
            [s["hotq"][c] for c in range(crops)],
            heads,
        )
        s["dwqg_acc"][...] += dwqg
        s["dwkv_acc"][...] += dwkv
        s["dw4_acc"][...] += dw4
        for h in range(heads):
            s["db_acc"][h] += db[h]
        @pl.when(side == 0)
        def _():
            own[at, 0 : 2 * qn, :] = dy_own + dy_all[0 : 2 * qn]
            d3[u, 2 * qn : 3 * qn, :] = dy_all[2 * qn :].astype(BF)
            part = d3.at[u, pl.ds(2 * qn, qn)]
            remote(part, part, x_send.at[1], d_sem.at[u], partner)

        @pl.when(side == 1)
        def _():
            own[at, 0 : 2 * qn, :] = dy_own
            own[at, 2 * qn : 3 * qn, :] = dy_all[2 * qn :]
            d3[u, 0 : 2 * qn, :] = dy_all[0 : 2 * qn].astype(BF)
            part = d3.at[u, pl.ds(0, 2 * qn)]
            remote(part, part, x_send.at[1], d_sem.at[u], partner)

        for c in range(crops):
            zin[u, c, 0] = outs[c].reshape(half, rl, width).astype(BF)
        give(u, 0)

    def finish(u, at):

        @pl.when(side == 0)
        def _():
            part = d3.at[u, pl.ds(0, 2 * qn)]
            pltpu.make_async_copy(part, part, d_sem.at[u]).wait()
            own[at, 0 : 2 * qn, :] += d3[u, 0 : 2 * qn, :].astype(F32)

        @pl.when(side == 1)
        def _():
            part = d3.at[u, pl.ds(2 * qn, qn)]
            pltpu.make_async_copy(part, part, d_sem.at[u]).wait()
            both = own[at, 2 * qn : 3 * qn, :] + d3[u, 2 * qn : 3 * qn, :].astype(F32)
            mine = where_t < len_ref[0] - qn
            own[at, 0:qn, :] += jnp.where(mine, both, 0.0)
            own[at, qn : 2 * qn, :] += dot(s["rev"][...], jnp.where(mine, 0.0, both).astype(BF))

        for c in range(crops):
            rows = slice(c * qn, (c + 1) * qn)
            dy, xhat = own[at, rows, :], xring[at, rows, :]
            s["dg_acc"][0:1] += jnp.sum(dy * xhat, 0, keepdims=True)
            dx = dy * gain_ref[...]
            rest = dx - jnp.mean(dx, -1, keepdims=True) - xhat * jnp.mean(dx * xhat, -1, keepdims=True)
            grad = zin[u, c, 1].astype(F32).reshape(qn, width) + iring[at, rows, :] * rest
            zin[u, c, 1] = grad.reshape(half, rl, width).astype(BF)
        give(u, 1)

    def step(it, _):
        at_turn(it + AHEAD, prepare)

        @pl.when(it + LEAD < heavy)
        def _():
            push_turn(it + LEAD)

        at_turn(it, work)
        at_turn(it - LAG, finish)
        return 0

    lax.fori_loop(0, heavy, step, 0)

    def turn_back(b):
        block = cols.at[:, :, pl.ds(b * gc * rl, gc * rl)]
        pltpu.make_async_copy(block, block, ret_sem.at[b]).wait()
        rows = slice(b * gc * rl, (b + 1) * gc * rl)
        for c in range(crops):
            for a in range(2):
                for j in range(gc):
                    at = (b * gc + j) * rl
                    s["stage"][a, pl.ds(j, rl, stride=gc), :] = cols[a, c, at : at + rl, :].astype(F32)
                cols[a, c, rows, :] = s["stage"][a].astype(BF)

    soon = early_blocks(light, heavy, half, gc) if direct else []

    gsend = s["gsend"]
    for k, (name, at) in enumerate((("dwqg_acc", 0), ("dwkv_acc", 0), ("dwkv_acc", 1), ("dwqg_acc", 1))):
        gsend[k] = jnp.transpose(s[name][at * width : (at + 1) * width, :]).astype(gsend.dtype)
    gsend[4] = s["dw4_acc"][...].astype(gsend.dtype)
    spot = lax.broadcasted_iota(jnp.int32, (1, width), 1)
    dbias = jnp.zeros((1, width), F32)
    for h in range(heads):
        total_h = jnp.sum(jnp.sum(s["db_acc"][h], 0, keepdims=True), 1, keepdims=True)
        dbias = jnp.where(spot == h, total_h * (1.0 / scale), dbias)
    for k in range(5, slots * ncol):
        gsend[k] = jnp.zeros((width, width), gsend.dtype)
    exchange_col(lambda p: gsend.at[pl.ds(p * slots, slots)], s["grecv"], 2)

    def last_turn(t, _):
        at_turn(t, finish)
        return 0

    lax.fori_loop(heavy - LAG, heavy, last_turn, 0)
    s["vsend"][0, 0:1, :] = s["dg_acc"][0:1]
    s["vsend"][0, 1:2, :] = dbias
    exchange_row(lambda p: s["vsend"].at[0], s["vrow"], 6)
    landed(s["grecv"], 2)
    share = total_of(s["grecv"], ncol)
    for p in range(nrow):
        s["ssend"][p] = share[:, p * wr : (p + 1) * wr, :].astype(s["ssend"].dtype)
    exchange_row(lambda p: s["ssend"].at[p], s["srecv"], 3)
    for b in soon[0::3]:
        turn_back(b)
    landed(s["vrow"], 6)
    s["vsend"][1] = total_of(s["vrow"], nrow)
    exchange_col(lambda p: s["vsend"].at[1], s["vcol"], 7)
    landed(s["srecv"], 3)
    s["csend"][...] = total_of(s["srecv"], nrow)
    exchange_col(lambda p: s["csend"], s["crecv"], 4)
    for b in soon[1::3]:
        turn_back(b)
    landed(s["crecv"], 4)
    landed(s["vcol"], 7)
    for j in range(wr):
        red_ref[:, j * width : (j + 1) * width] = s["crecv"][:, :, j, :].reshape(slots * ncol, width)
    red_ref[5:7, 0:width] = total_of(s["vcol"], ncol)
    wval = w_ref[...]
    step_w = moments(wval, red_ref[0:5, :], m1_ref[...], m2_ref[...])[2]
    row5 = lax.broadcasted_iota(jnp.int32, (5, 1), 0)
    squares = jnp.where(spot == row5, jnp.sum(wval * wval, 1, keepdims=True), 0.0)
    squares += jnp.where(spot == row5 + 8, jnp.sum(step_w * step_w, 1, keepdims=True), 0.0)
    s["nsend"][...] = jnp.sum(squares, 0, keepdims=True)
    exchange_row(lambda p: s["nsend"], s["nrecv"], 5)
    for b in soon[2::3]:
        turn_back(b)
    landed(s["nrecv"], 5)
    nrm_ref[...] = total_of(s["nrecv"], nrow)

    for b in range(nblocks):
        if b not in soon:
            block = cols.at[:, :, pl.ds(b * gc * rl, gc * rl)]
            pltpu.make_async_copy(block, block, ret_sem.at[b]).wait()

    def ended(count):
        sent = s["sbuf"] if direct else pair_ref
        sent = sent.at[pl.ds(0, half // 2 * (light + heavy) - count)]
        pltpu.make_async_copy(sent, sent, send_sem.at[0]).wait()
        gone = zin.at[pl.ds(0, count), :, :, pl.ds(0, half - 1)]
        pltpu.make_async_copy(gone, gone, rsend_sem.at[0]).wait()
        for at_side, rows_y, rows_d in ((0, 2 * qn, qn), (1, qn, 2 * qn)):

            @pl.when(side == at_side)
            def _():
                part = y3.at[pl.ds(0, count), pl.ds(0, rows_y)]
                pltpu.make_async_copy(part, part, x_send.at[0]).wait()
                part = d3.at[pl.ds(0, count), pl.ds(0, rows_d)]
                pltpu.make_async_copy(part, part, x_send.at[1]).wait()

    for kind, count in ((False, light), (True, heavy)):

        @pl.when(is_heavy == kind)
        def _():
            ended(count)

    for n, name in enumerate(
        ("wrow", "wall", "grecv", "srecv", "crecv", "nrecv", "vrow", "vcol")
    ):
        sent = s[name].at[pl.ds(0, s[name].shape[0] - 1)]
        pltpu.make_async_copy(sent, sent, misc_send.at[n]).wait()


def step_kernel(direct, soon, *refs):
    if direct:
        cols, blocks, refs = refs[0], refs[1], refs[2:]
    red_ref, nrm_ref, w_ref, m1_ref, m2_ref, gain_ref, gm_ref, gv_ref, bias_ref, bm_ref, bv_ref = refs[:11]
    refs = refs[11:]
    if direct:
        bigs, refs = refs[0:2], refs[2:11] + refs[11:]
        refs, (slot, stage, sem) = refs[:9], refs[9:]
        _, crops, _, width = cols.shape
        _, rl, cl, _ = bigs[0].shape
        gc = 16
        copies = []

        def put(src, a, c, b):
            n = len(copies)
            copy = pltpu.make_async_copy(src, bigs[a].at[c, :, pl.ds(b * gc, gc), :], sem.at[n])
            copy.start()
            copies.append(copy)

        for b in soon:
            for c in range(crops):
                for a in range(2):
                    put(blocks.at[a, c, b], a, c, b)
        late = [b for b in range(cl // gc) if b not in soon]
        for n, b in enumerate(late):
            for c in range(crops):
                for a in range(2):
                    for j in range(gc):
                        at = (b * gc + j) * rl
                        stage[a, pl.ds(j, rl, stride=gc), :] = cols[a, c, at : at + rl, :].astype(F32)
                    slot[n, c, a] = stage[a].reshape(rl, gc, width).astype(BF)
                    put(slot.at[n, c, a], a, c, b)
    nw_ref, n1_ref, n2_ref, ng_ref, ngm_ref, ngv_ref, nb_ref, nbm_ref, nbv_ref = refs
    width = gain_ref.shape[1]
    heads = bias_ref.shape[1]
    wval = w_ref[...]
    first, second, step_w = moments(wval, red_ref[0:5, :], m1_ref[...], m2_ref[...])
    spot = lax.broadcasted_iota(jnp.int32, (1, width), 1)
    place = lax.broadcasted_iota(jnp.int32, (5, 1), 0)
    value_sq = jnp.sum(jnp.where(spot == place, nrm_ref[...], 0.0), 1, keepdims=True)
    step_sq = jnp.sum(jnp.where(spot == place + 8, nrm_ref[...], 0.0), 1, keepdims=True)
    nw_ref[...] = wval - rate * (jnp.sqrt(value_sq) / jnp.sqrt(step_sq)) * step_w
    n1_ref[...] = first
    n2_ref[...] = second
    for row, n, own in (
        (5, width, (gain_ref, gm_ref, gv_ref, ng_ref, ngm_ref, ngv_ref)),
        (6, heads, (bias_ref, bm_ref, bv_ref, nb_ref, nbm_ref, nbv_ref)),
    ):
        val = own[0][...]
        first, second, step_v = moments(val, red_ref[row : row + 1, 0:n], own[1][...], own[2][...])
        ratio = jnp.sqrt(jnp.sum(val * val, 1, keepdims=True)) / jnp.sqrt(
            jnp.sum(step_v * step_v, 1, keepdims=True)
        )
        own[3][...] = val - rate * ratio * step_v
        own[4][...] = first
        own[5][...] = second
    if direct:
        for copy in copies:
            copy.wait()


def body(
    nrow,
    ncol,
    pair,
    cotangent,
    segments,
    lengths,
    weights,
    moment_one,
    moment_two,
    gain,
    gain_m,
    gain_v,
    chain_bias,
    bias_m,
    bias_v,
):
    crops, rl, cl, width = pair.shape
    heads = chain_bias.shape[0]
    half = nrow // 2
    qn = half * rl
    wr = weights.shape[1] // width
    slots = -(-8 // ncol)
    direct = cl % 16 == 0 and rl % 16 == 0
    pairs = cl // (half // 2)
    light = LIGHT if direct and pairs == 64 else pairs // 2
    heavy = pairs - light
    dims = (nrow, ncol, crops, light, heavy, rl, width, heads, wr, direct)
    wtype = BF if wr % 16 == 0 else F32
    ring = AHEAD + LAG + 1
    hbm = pl.BlockSpec(memory_space=pl.ANY)
    vmem = pl.BlockSpec(memory_space=pltpu.VMEM)
    smem = pl.BlockSpec(memory_space=pltpu.SMEM)
    dma = pltpu.SemaphoreType.DMA
    outs = {
        "red": pltpu.VMEM((slots * ncol, wr * width), F32),
        "nrm": pltpu.VMEM((1, width), F32),
        "cols": pltpu.VMEM((2, crops, cl * rl, width), BF),
    }
    scratch = {
        "zin": pltpu.VMEM((heavy, crops, 2, half, rl, width), BF),
        "y3": pltpu.VMEM((heavy, 3 * qn, width), BF),
        "d3": pltpu.VMEM((heavy, 3 * qn, width), BF),
        "own": pltpu.VMEM((ring, 3 * qn, width), F32),
        "xring": pltpu.VMEM((ring, 2 * qn, width), F32),
        "iring": pltpu.VMEM((ring, 2 * qn, width), F32),
        "yring": pltpu.VMEM((ring, 2 * qn, width), BF),
        "rev": pltpu.VMEM((qn, qn), BF),
        "wtmp": pltpu.VMEM((8, wr, width), F32),
        "wsend": pltpu.VMEM((slots * ncol, wr, width), wtype),
        "wrow": pltpu.VMEM((nrow, slots, wr, width), wtype),
        "wall": pltpu.VMEM((ncol, nrow, slots, wr, width), wtype),
        "gsend": pltpu.VMEM((slots * ncol, width, width), wtype),
        "grecv": pltpu.VMEM((ncol, slots, width, width), wtype),
        "ssend": pltpu.VMEM((nrow, slots, wr, width), wtype),
        "srecv": pltpu.VMEM((nrow, slots, wr, width), wtype),
        "csend": pltpu.VMEM((slots, wr, width), F32),
        "crecv": pltpu.VMEM((ncol, slots, wr, width), F32),
        "vsend": pltpu.VMEM((2, 2, width), F32),
        "vrow": pltpu.VMEM((nrow, 2, width), F32),
        "vcol": pltpu.VMEM((ncol, 2, width), F32),
        "nsend": pltpu.VMEM((1, width), F32),
        "nrecv": pltpu.VMEM((nrow, 1, width), F32),
        "wqg": pltpu.VMEM((width, 2 * width), BF),
        "wkv": pltpu.VMEM((width, 2 * width), BF),
        "wqg_t": pltpu.VMEM((2 * width, width), BF),
        "wkv_t": pltpu.VMEM((2 * width, width), BF),
        "w4": pltpu.VMEM((width, width), BF),
        "augk": pltpu.VMEM((crops, 2 * qn, width), BF),
        "augq": pltpu.VMEM((crops, heads, width, qn), BF),
        "hotk": pltpu.VMEM((crops, 16, 2 * qn), BF),
        "hotq": pltpu.VMEM((crops, 16, qn), BF),
        "dwqg_acc": pltpu.VMEM((2 * width, width), F32),
        "dwkv_acc": pltpu.VMEM((2 * width, width), F32),
        "dw4_acc": pltpu.VMEM((width, width), F32),
        "dg_acc": pltpu.VMEM((8, width), F32),
        "db_acc": pltpu.VMEM((heads, 8, qn), F32),
        "in_sem": dma((heavy,)),
        "y_sem": dma((heavy,)),
        "d_sem": dma((heavy,)),
        "send_sem": dma((1,)),
        "ret_sem": dma((cl // 16 if direct else 1,)),
        "rsend_sem": dma((1,)),
        "x_send": dma((2,)),
        "misc_recv": dma((8,)),
        "misc_send": dma((8,)),
    }
    if direct:
        sources = (pair, cotangent)
        scratch["raw"] = pltpu.VMEM((3, crops, 2, rl, 16, width), BF)
        scratch["sbuf"] = pltpu.VMEM((cl, crops, 2, rl, width), BF)
        scratch["stage"] = pltpu.VMEM((2, rl * 16, width), F32)
        scratch["raw_sem"] = dma((3, crops, 2))
    else:
        sources = (jnp.transpose(jnp.stack([pair, cotangent], 1), (3, 0, 1, 2, 4)), cotangent)
    names = tuple(outs) + tuple(scratch)
    res1 = pl.pallas_call(
        functools.partial(main_kernel, dims, names),
        out_shape=tuple(outs.values()),
        in_specs=[hbm, hbm, vmem, smem, vmem, vmem, vmem, vmem, smem],
        out_specs=(vmem,) * len(outs),
        scratch_shapes=list(scratch.values()),
        compiler_params=pltpu.CompilerParams(
            collective_id=0, has_side_effects=True, vmem_limit_bytes=55 << 20
        ),
        name="column_attention",
    )(
        *(
            pltpu.with_memory_space_constraint(x, pltpu.HBM)
            for x in (
                *sources,
                segments,
                lengths,
                weights,
                moment_one,
                moment_two,
                gain.reshape(1, width),
                chain_bias,
            )
        )
    )
    res1 = dict(zip(outs, res1))
    small = (gain, gain_m, gain_v, chain_bias, bias_m, bias_v)
    ops = [res1["red"], res1["nrm"], weights, moment_one, moment_two] + [a.reshape(1, -1) for a in small]
    fin = jax.ShapeDtypeStruct(pair.shape, BF)
    bigs = [fin, fin] if direct else []
    count = 2 * crops * (cl // 16)
    soon = early_blocks(light, heavy, half, 16) if direct else []
    turned = ()
    if direct:
        turned = (res1["cols"], res1["cols"].reshape(2, crops, cl // 16, rl, 16, width))
    res = pl.pallas_call(
        functools.partial(step_kernel, direct, soon),
        out_shape=bigs
        + [jax.ShapeDtypeStruct(weights.shape, F32)] * 3
        + [jax.ShapeDtypeStruct((1, width), F32)] * 3
        + [jax.ShapeDtypeStruct((1, heads), F32)] * 3,
        in_specs=[vmem] * (len(ops) + len(turned)),
        out_specs=[hbm] * len(bigs) + [vmem] * 9,
        scratch_shapes=[
            pltpu.VMEM((cl // 16 - len(soon), crops, 2, rl, 16, width), BF),
            pltpu.VMEM((2, rl * 16, width), F32),
            dma((count,)),
        ]
        if direct
        else [],
        compiler_params=pltpu.CompilerParams(vmem_limit_bytes=18 << 20),
        name="lamb_step",
    )(*turned, *ops)
    if direct:
        fins, res = res[:2], res[2:]
    else:
        fins = [jnp.swapaxes(res1["cols"][a].reshape(crops, cl, rl, width), 1, 2) for a in range(2)]
    return (*fins, *res[:3], *[a.reshape(-1) for a in res[3:]])


def solution(mesh):
    big = P(None, "row", "col", None)
    shard = P(None, "row")
    return jax.shard_map(
        functools.partial(body, mesh.shape["row"], mesh.shape["col"]),
        mesh=mesh,
        in_specs=(big, big, P(), P(), shard, shard, shard) + (P(),) * 6,
        out_specs=(big, big, shard, shard, shard) + (P(),) * 6,
        check_vma=False,
    )
```

```python
import functools
import math

import jax
import jax.numpy as jnp
from jax import lax
from jax.experimental import pallas as pl
from jax.experimental.pallas import tpu as pltpu
from jax.sharding import PartitionSpec as P

STEP = 10
beta_one = 0.9
beta_two = 0.999
epsilon = 1e-06
decay = 0.01
rate = 0.25

BF = jnp.bfloat16
F32 = jnp.float32
MESH = pl.DeviceIdType.MESH
NT = ((1,), (1,))
TN = ((0,), (0,))
LOG2E = math.log2(math.e)
SEGS = 4
EARLY, LEAD, AHEAD, LAG = 3, 4, 2, 3
LIGHT = 22


def dot(a, b, dims=((1,), (0,))):
    return lax.dot_general(a, b, (dims, ((), ())), preferred_element_type=F32)


def normed(z, gain):
    mean = jnp.mean(z, -1, keepdims=True)
    cen = z - mean
    var = jnp.mean(cen * cen, -1, keepdims=True)
    inv = lax.rsqrt(var + 1e-05)
    xhat = cen * inv
    return xhat, inv, (xhat * gain).astype(BF)


def attend(z, co, yown, yall, wqg_t, wkv, wkv_t, w4, wqg, augk, augq, hotk, hotq, heads):
    qn, width = z[0].shape
    hsize = width // heads
    scale = 1.0 / math.sqrt(hsize)
    head_of = lax.broadcasted_iota(jnp.int32, (width, 1), 0) // hsize
    row16 = lax.broadcasted_iota(jnp.int32, (16, 1), 0)
    packed = slice(2 * qn, 3 * qn)

    def spread(xT, last):
        parts = [jnp.where(head_of == h, xT, jnp.zeros_like(xT)) for h in range(heads)]
        if last is not None:
            parts = [jnp.concatenate([p, x], 0) for p, x in zip(parts, last)]
        return jnp.concatenate(parts, 1)

    kv = dot(yall, wkv).astype(BF)
    kvT = dot(wkv_t, yall, NT).astype(BF)
    ones = [jnp.broadcast_to(jnp.where(row16 == h, 1.0, 0.0).astype(BF), (16, 2 * qn)) for h in range(heads)]
    crops = range(2)
    st = [{} for c in crops]
    for c in crops:
        t = st[c]
        first = slice(c * qn, (c + 1) * qn)
        t["k"] = jnp.concatenate([kv[first, :width], kv[packed, :width]], 0)
        t["v"] = jnp.concatenate([kv[first, width:], kv[packed, width:]], 0)
        bothT = jnp.concatenate([kvT[:, first], kvT[:, packed]], 1)
        t["kT"], t["vT"] = bothT[:width], bothT[width:]
        projT = dot(wqg_t, yown[c], NT)
        t["qT"] = projT[:width].astype(BF)
        t["gT"] = jax.nn.sigmoid(projT[width:])
        t["doT"] = dot(w4, co[c], NT).astype(BF).astype(F32)
    outs, dqgT, dkA, dkP = [], [], [], None
    dw4, db = 0.0, [0.0] * heads
    for c in crops:
        t = st[c]
        kaug = jnp.concatenate([t["k"], augk[c]], 1)
        es = []
        for h in range(heads):
            qaug = jnp.concatenate([jnp.where(head_of == h, t["qT"], jnp.zeros_like(t["qT"])), augq[c][h]], 0)
            s = dot(kaug, qaug) * (scale * LOG2E)
            es.append(jnp.exp2(s - jnp.max(s, 0, keepdims=True)).astype(BF))
        t["es"] = es
        t = st[c]
        a = dot(spread(t["vT"], ones), jnp.concatenate(t["es"], 0))
        r = 1.0 / a[width : width + heads]
        t["rb"] = jnp.concatenate([jnp.broadcast_to(r[h : h + 1], (hsize, qn)) for h in range(heads)], 0)
        t["aT"] = a[:width] * t["rb"]
        t = st[c]
        aT, gT, doT = t["aT"], t["gT"], t["doT"]
        daT = (doT * gT).astype(BF).astype(F32)
        t["dgT"] = (doT * aT * gT * (1.0 - gT)).astype(BF)
        t["dnT"] = (daT * t["rb"] * scale).astype(BF)
        prod = aT * t["dnT"].astype(F32)
        t["shift"] = [jnp.sum(prod[h * hsize : (h + 1) * hsize], 0, keepdims=True) for h in range(heads)]
    for c in crops:
        t = st[c]
        dps = dot(t["v"], spread(t["dnT"], None))
        t["ds"] = [
            (t["es"][h].astype(F32) * (dps[:, h * qn : (h + 1) * qn] - t["shift"][h])).astype(BF) for h in range(heads)
        ]
        t = st[c]
        oT = (t["aT"] * t["gT"]).astype(BF)
        outs.append(z[c] + dot(oT, w4, TN))
        dw4 = dw4 + dot(oT, co[c])
        t = st[c]
        dk, dv = [], []
        for h in range(heads):
            rows = slice(h * hsize, (h + 1) * hsize)
            dk.append(dot(t["qT"][rows], t["ds"][h], NT))
            dv.append(dot(t["dnT"][rows], t["es"][h], NT) * (1.0 / scale))
        t["dkv"] = jnp.concatenate(dk + dv, 0)
    for c in crops:
        t = st[c]
        tile_k = jnp.concatenate([hotk[c][:4].astype(F32)] * 4, 0)
        tile_q = jnp.concatenate([hotq[c][:4].astype(F32)] * 4, 0)
        x = dot(
            spread(t["kT"], [jnp.where(row16 // 4 == h, tile_k, 0.0).astype(BF) for h in range(heads)]),
            jnp.concatenate(t["ds"], 0),
        )
        for h in range(heads):
            part = jnp.where(row16 // 4 == h, x[width : width + 16] * tile_q, 0.0)
            db[h] = db[h] + part[:8] + part[8:]
        dqgT.append(jnp.concatenate([x[:width].astype(BF), t["dgT"]], 0))
        dkv = t["dkv"]
        dkA.append(dkv[:, :qn].astype(BF))
        dkP = dkv[:, qn:] if dkP is None else dkP + dkv[:, qn:]
    dqgT = jnp.concatenate(dqgT, 1)
    dkvT = jnp.concatenate(dkA + [dkP.astype(BF)], 1)
    dwqg = dot(dqgT, jnp.concatenate(yown, 0))
    dwkv = dot(dkvT, yall)
    dy_own = jnp.transpose(dot(wqg, dqgT))
    dy_all = jnp.transpose(dot(wkv, dkvT))
    return outs, dy_own, dy_all, dwqg, dwkv, dw4, db


def moments(value, grad, first, second):
    first_new = beta_one * first + (1.0 - beta_one) * grad
    second_new = beta_two * second + (1.0 - beta_two) * grad * grad
    step_dir = (
        first_new
        / (1.0 - beta_one**STEP)
        / (jnp.sqrt(second_new / (1.0 - beta_two**STEP)) + epsilon)
        + decay * value
    )
    return (first_new, second_new, step_dir)


def blocks_of(rank, units, light, heavy, half, gc):
    far = rank < half // 2
    first = rank * light if far else half // 2 * light + (rank - half // 2) * heavy
    count = light if far else heavy
    return sorted({(first + (count - 1 - u if rank % 2 else u)) // gc for u in units if u < count})


def early_blocks(light, heavy, half, gc):
    late = set()
    for r in range(half):
        count = light if r < half // 2 else heavy
        units = [u for u in range(count) if -(-((u + 1) * heavy) // count) > heavy - 6]
        late |= set(blocks_of(r, units, light, heavy, half, gc))
    return [b for b in range(half // 2 * (light + heavy) // gc) if b not in late]


def main_kernel(dims, names, *refs):
    nrow, ncol, crops, light, heavy, rl, width, heads, wr, direct = dims
    pair_ref, cot_ref, seg_ref, len_ref, w_ref, m1_ref, m2_ref, gain_ref, bias_ref = refs[:9]
    srcs = (pair_ref, cot_ref)
    s = dict(zip(names, refs[9:]))
    zin, y3, d3, own, xring, iring, yring = (s[n] for n in ("zin", "y3", "d3", "own", "xring", "iring", "yring"))
    in_sem, send_sem, ret_sem, rsend_sem = s["in_sem"], s["send_sem"], s["ret_sem"], s["rsend_sem"]
    misc_recv, misc_send, y_sem, d_sem, x_send = (
        s[n] for n in ("misc_recv", "misc_send", "y_sem", "d_sem", "x_send")
    )
    red_ref, nrm_ref = s["red"], s["nrm"]
    half = nrow // 2
    qn = half * rl
    gc = 16 if direct else half // 2 * (light + heavy)
    ring = xring.shape[0]
    cols = s["cols"]
    nblocks = (half // 2 * (light + heavy)) // gc
    hsize = width // heads
    scale = 1.0 / math.sqrt(hsize)
    slots = s["wrow"].shape[1]
    me = lax.axis_index("row")
    mc = lax.axis_index("col")
    side = me // half
    place = lax.rem(me, half)

    def rank_of(at_side, w):
        return lax.rem(w + at_side * (half // 2), half)

    def first_of(rank):
        near_rank = rank - half // 2
        return jnp.where(near_rank < 0, rank * light, (half // 2) * light + near_rank * heavy)

    def column_at(there, u):
        count = jnp.where(there < half // 2, light, heavy)
        return first_of(there) + jnp.where(lax.rem(there, 2) == 1, count - 1 - u, u)

    rank = rank_of(side, place)
    is_heavy = rank >= half // 2
    partner = ((1 - side) * half + rank_of(1 - side, rank), mc)

    def active(heavy_one, n):
        return heavy_one | (((n + 1) * light) // heavy > (n * light) // heavy)

    def unit_of(heavy_one, n):
        return jnp.where(heavy_one, n, (n * light) // heavy)

    def row_peer(d):
        return lax.rem(me + d, nrow)

    def col_peer(d):
        return lax.rem(mc + d, ncol)

    def near(d):
        return lax.rem(place + d, half)

    def device(w):
        return (side * half + w, mc)

    def load_block(b, slot):
        for c in range(crops):
            for a in range(2):
                pltpu.make_async_copy(
                    srcs[a].at[c, :, pl.ds(b * gc, gc), :],
                    s["raw"].at[slot, c, a],
                    s["raw_sem"].at[slot, c, a],
                ).start()

    if direct:
        needs = [blocks_of(r, range(LEAD), light, heavy, half, gc) for r in range(half)]
        order = []
        for need in needs[half // 2 :] + needs[: half // 2]:
            order += [b for b in need if b not in order]
        order += [b for b in range(nblocks) if b not in order]
        done_blocks = 0
        nslot = s["raw"].shape[0]
        for n in range(nslot):
            load_block(order[n], n)

    barrier = pltpu.get_barrier_semaphore()

    def greet_row(d, _):
        pl.semaphore_signal(barrier, inc=1, device_id=(row_peer(d), mc), device_id_type=MESH)
        return 0

    def greet_col(d, _):
        pl.semaphore_signal(barrier, inc=1, device_id=(me, col_peer(d)), device_id_type=MESH)
        return 0

    lax.fori_loop(1, nrow, greet_row, 0)
    lax.fori_loop(1, ncol, greet_col, 0)
    for j in range(wr):
        s["wtmp"][0:5, j, :] = w_ref[:, j * width : (j + 1) * width]
    for k in range(slots * ncol):
        s["wsend"][k] = (s["wtmp"][k] if k < 5 else jnp.zeros((wr, width), F32)).astype(s["wsend"].dtype)
    pl.semaphore_wait(barrier, nrow - 1 + ncol - 1)

    def remote(src, dst, send, recv, peer):
        pltpu.make_async_remote_copy(
            src, dst, send, recv, device_id=peer, device_id_type=MESH
        ).start()

    def exchange_row(src_of, dst, n):
        def push(d, _):
            p = row_peer(d)
            remote(src_of(p), dst.at[me], misc_send.at[n], misc_recv.at[n], (p, mc))
            return 0

        lax.fori_loop(1, nrow, push, 0)
        pltpu.make_async_copy(src_of(me), dst.at[me], misc_recv.at[n]).start()

    def exchange_col(src_of, dst, n):
        def push(d, _):
            p = col_peer(d)
            remote(src_of(p), dst.at[mc], misc_send.at[n], misc_recv.at[n], (me, p))
            return 0

        lax.fori_loop(1, ncol, push, 0)
        pltpu.make_async_copy(src_of(mc), dst.at[mc], misc_recv.at[n]).start()

    def landed(dst, n):
        pltpu.make_async_copy(dst, dst, misc_recv.at[n]).wait()

    def total_of(ref, n):
        return lax.fori_loop(1, n, lambda r, t: t + ref[r].astype(F32), ref[0].astype(F32))

    exchange_row(lambda p: s["wsend"].at[pl.ds(mc * slots, slots)], s["wrow"], 0)

    def column_of(col):
        return s["sbuf"].at[col] if direct else pair_ref.at[col]

    def push_turn(n):
        def to_peer(d, _):
            w = near(d)
            there = rank_of(side, w)
            to_heavy = there >= half // 2
            u = unit_of(to_heavy, n)

            @pl.when(active(to_heavy, n))
            def _():
                src = column_of(column_at(there, u))
                remote(src, zin.at[u, :, :, place], send_sem.at[0], in_sem.at[u], device(w))

            return 0

        lax.fori_loop(1, half, to_peer, 0)
        mine = unit_of(is_heavy, n)

        @pl.when(active(is_heavy, n))
        def _():
            src = column_of(column_at(rank, mine))
            pltpu.make_async_copy(src, zin.at[mine, :, :, place], in_sem.at[mine]).start()

    def push_turns(first, last):
        def at_turn(n, _):
            push_turn(n)
            return 0

        lax.fori_loop(first, last, at_turn, 0)

    def turn_block(n):
        b, slot = order[n], n % nslot
        for c in range(crops):
            for a in range(2):
                here = s["raw"].at[slot, c, a]
                pltpu.make_async_copy(here, here, s["raw_sem"].at[slot, c, a]).wait()
                s["stage"][a] = s["raw"][slot, c, a].astype(F32).reshape(rl * gc, width)
                for j in range(gc):
                    s["sbuf"][b * gc + j, c, a] = s["stage"][a, pl.ds(j, rl, stride=gc), :].astype(BF)
        if n + nslot < len(order):
            load_block(order[n + nslot], slot)

    def push_one(there, n):
        to_heavy = there >= half // 2
        u = unit_of(to_heavy, n)

        @pl.when(active(to_heavy, n) & (there == rank))
        def _():
            src = column_of(column_at(rank, u))
            pltpu.make_async_copy(src, zin.at[u, :, :, place], in_sem.at[u]).start()

        @pl.when(active(to_heavy, n) & (there != rank))
        def _():
            src = column_of(column_at(there, u))
            remote(src, zin.at[u, :, :, place], send_sem.at[0], in_sem.at[u], device(rank_of(side, there)))

    if direct:
        for there in list(range(half // 2, half)) + list(range(half // 2)):
            for b in needs[there]:
                if b in order[:done_blocks]:
                    continue
                turn_block(order.index(b))
                done_blocks += 1
            for n in range(EARLY):
                push_one(there, n)
        push_turns(EARLY, LEAD)
    else:
        push_turns(0, LEAD)

    back = lax.broadcasted_iota(jnp.int32, (qn, qn), 0) + lax.broadcasted_iota(jnp.int32, (qn, qn), 1)
    s["rev"][...] = jnp.where(back == qn - 1, 1.0, 0.0).astype(BF)

    where_t = lax.broadcasted_iota(jnp.int32, (qn, 1), 0)

    def prepare(u, at):
        pltpu.make_async_copy(zin.at[u], zin.at[u], in_sem.at[u]).wait()
        for c in range(crops):
            rows = slice(c * qn, (c + 1) * qn)
            xhat, inv, y = normed(zin[u, c, 0].astype(F32).reshape(qn, width), gain_ref[...])
            xring[at, rows, :] = xhat
            iring[at, rows, :] = jnp.broadcast_to(inv, (qn, width))
            yring[at, rows, :] = y

        @pl.when(side == 0)
        def _():
            y3[u, 0 : 2 * qn, :] = yring[at]
            part = y3.at[u, pl.ds(0, 2 * qn)]
            remote(part, part, x_send.at[0], y_sem.at[u], partner)

        @pl.when(side == 1)
        def _():
            y1 = dot(s["rev"][...], yring[at, qn : 2 * qn, :])
            y0 = yring[at, 0:qn, :].astype(F32)
            y3[u, 2 * qn : 3 * qn, :] = jnp.where(where_t < len_ref[0] - qn, y0, y1).astype(BF)
            part = y3.at[u, pl.ds(2 * qn, qn)]
            remote(part, part, x_send.at[0], y_sem.at[u], partner)

    def at_turn(t, act):
        @pl.when((t >= 0) & (t < heavy) & active(is_heavy, t))
        def _():
            act(unit_of(is_heavy, t), lax.rem(t, ring))

    def early_turn(n, _):
        at_turn(n, prepare)
        return 0

    lax.fori_loop(0, 1, early_turn, 0)
    if direct:
        for n in range(done_blocks, nblocks):
            turn_block(n)
    lax.fori_loop(1, AHEAD, early_turn, 0)

    landed(s["wrow"], 0)
    exchange_col(lambda p: s["wrow"], s["wall"], 1)

    lane = lax.broadcasted_iota(jnp.int32, (1, qn), 1)
    line = lax.broadcasted_iota(jnp.int32, (width, 1), 0)
    for c in range(crops):
        low_seg, high_seg = seg_ref[c : c + 1, :qn], seg_ref[c : c + 1, qn:]
        own_seg = jnp.where(side == 0, low_seg, high_seg)
        same_low = (lax.rem(line, SEGS) == low_seg).astype(F32)
        same_high = (lax.rem(line, SEGS) == high_seg).astype(F32)
        pad = jnp.where(lane + qn >= len_ref[c], -1e30, 0.0)
        if c == 1:
            same_high = dot(same_high.astype(BF), s["rev"][...])
            pad = jnp.where(2 * qn - 1 - lane >= len_ref[c], -1e30, 0.0)
        same = jnp.concatenate([same_low, same_high], 1)
        pad = jnp.concatenate([jnp.zeros((1, qn), F32), pad], 1)
        s["hotk"][c] = jnp.where(line[:16] < SEGS, same[:16], 0.0).astype(BF)
        rowsk = jnp.where(line < 3 * SEGS, same, jnp.where(line == 3 * SEGS, pad, 0.0))
        s["augk"][c] = jnp.transpose(rowsk).astype(BF)
        same = (lax.rem(line, SEGS) == own_seg).astype(F32)
        s["hotq"][c] = jnp.where(line[:16] < SEGS, same[:16], 0.0).astype(BF)
        for h in range(heads):
            full = jnp.full((width, 1), bias_ref[h] * (1.0 / scale), F32)
            high = full.astype(BF).astype(F32)
            mid = (full - high).astype(BF).astype(F32)
            low = full - high - mid
            part = jnp.where(line < SEGS, high, jnp.where(line < 2 * SEGS, mid, low))
            rowsq = jnp.where(line < 3 * SEGS, same * part, jnp.where(line == 3 * SEGS, 1.0, 0.0))
            s["augq"][c, h] = rowsq.astype(BF)

    for name in ("dwqg_acc", "dwkv_acc", "dw4_acc", "dg_acc", "db_acc"):
        s[name][...] = jnp.zeros_like(s[name])

    landed(s["wall"], 1)
    for k in range(5):
        w = s["wall"][k // slots, :, k % slots].astype(F32).reshape(width, width)
        if k == 4:
            s["w4"][...] = w.astype(BF)
        else:
            name, at = {0: ("wqg", 0), 3: ("wqg", 1), 1: ("wkv", 0), 2: ("wkv", 1)}[k]
            s[name][:, at * width : (at + 1) * width] = w.astype(BF)
            s[name + "_t"][at * width : (at + 1) * width, :] = jnp.transpose(w).astype(BF)

    def give(u, a):
        col = column_at(rank, u)
        here = cols.at[a, :, pl.ds(col * rl, rl)]
        landing = ret_sem.at[col // gc]

        def to_peer(d, _):
            w = near(d)
            remote(zin.at[u, :, a, w], here, rsend_sem.at[0], landing, device(w))
            return 0

        lax.fori_loop(1, half, to_peer, 0)
        pltpu.make_async_copy(zin.at[u, :, a, place], here, landing).start()

    def work(u, at):
        @pl.when(side == 0)
        def _():
            part = y3.at[u, pl.ds(2 * qn, qn)]
            pltpu.make_async_copy(part, part, y_sem.at[u]).wait()

        @pl.when(side == 1)
        def _():
            part = y3.at[u, pl.ds(0, 2 * qn)]
            pltpu.make_async_copy(part, part, y_sem.at[u]).wait()

        outs, dy_own, dy_all, dwqg, dwkv, dw4, db = attend(
            [zin[u, c, 0].astype(F32).reshape(qn, width) for c in range(crops)],
            [zin[u, c, 1].astype(F32).reshape(qn, width).astype(BF) for c in range(crops)],
            [yring[at, c * qn : (c + 1) * qn, :] for c in range(crops)],
            y3[u],
            s["wqg_t"][...],
            s["wkv"][...],
            s["wkv_t"][...],
            s["w4"][...],
            s["wqg"][...],
            [s["augk"][c] for c in range(crops)],
            [[s["augq"][c, h] for h in range(heads)] for c in range(crops)],
            [s["hotk"][c] for c in range(crops)],
            [s["hotq"][c] for c in range(crops)],
            heads,
        )
        s["dwqg_acc"][...] += dwqg
        s["dwkv_acc"][...] += dwkv
        s["dw4_acc"][...] += dw4
        for h in range(heads):
            s["db_acc"][h] += db[h]
        @pl.when(side == 0)
        def _():
            own[at, 0 : 2 * qn, :] = dy_own + dy_all[0 : 2 * qn]
            d3[u, 2 * qn : 3 * qn, :] = dy_all[2 * qn :].astype(BF)
            part = d3.at[u, pl.ds(2 * qn, qn)]
            remote(part, part, x_send.at[1], d_sem.at[u], partner)

        @pl.when(side == 1)
        def _():
            own[at, 0 : 2 * qn, :] = dy_own
            own[at, 2 * qn : 3 * qn, :] = dy_all[2 * qn :]
            d3[u, 0 : 2 * qn, :] = dy_all[0 : 2 * qn].astype(BF)
            part = d3.at[u, pl.ds(0, 2 * qn)]
            remote(part, part, x_send.at[1], d_sem.at[u], partner)

        for c in range(crops):
            zin[u, c, 0] = outs[c].reshape(half, rl, width).astype(BF)
        give(u, 0)

    def finish(u, at):

        @pl.when(side == 0)
        def _():
            part = d3.at[u, pl.ds(0, 2 * qn)]
            pltpu.make_async_copy(part, part, d_sem.at[u]).wait()
            own[at, 0 : 2 * qn, :] += d3[u, 0 : 2 * qn, :].astype(F32)

        @pl.when(side == 1)
        def _():
            part = d3.at[u, pl.ds(2 * qn, qn)]
            pltpu.make_async_copy(part, part, d_sem.at[u]).wait()
            both = own[at, 2 * qn : 3 * qn, :] + d3[u, 2 * qn : 3 * qn, :].astype(F32)
            mine = where_t < len_ref[0] - qn
            own[at, 0:qn, :] += jnp.where(mine, both, 0.0)
            own[at, qn : 2 * qn, :] += dot(s["rev"][...], jnp.where(mine, 0.0, both).astype(BF))

        for c in range(crops):
            rows = slice(c * qn, (c + 1) * qn)
            dy, xhat = own[at, rows, :], xring[at, rows, :]
            s["dg_acc"][0:1] += jnp.sum(dy * xhat, 0, keepdims=True)
            dx = dy * gain_ref[...]
            rest = dx - jnp.mean(dx, -1, keepdims=True) - xhat * jnp.mean(dx * xhat, -1, keepdims=True)
            grad = zin[u, c, 1].astype(F32).reshape(qn, width) + iring[at, rows, :] * rest
            zin[u, c, 1] = grad.reshape(half, rl, width).astype(BF)
        give(u, 1)

    def step(it, _):
        at_turn(it + AHEAD, prepare)

        @pl.when(it + LEAD < heavy)
        def _():
            push_turn(it + LEAD)

        at_turn(it, work)
        at_turn(it - LAG, finish)
        return 0

    lax.fori_loop(0, heavy, step, 0)

    def turn_back(b):
        block = cols.at[:, :, pl.ds(b * gc * rl, gc * rl)]
        pltpu.make_async_copy(block, block, ret_sem.at[b]).wait()
        rows = slice(b * gc * rl, (b + 1) * gc * rl)
        for c in range(crops):
            for a in range(2):
                for j in range(gc):
                    at = (b * gc + j) * rl
                    s["stage"][a, pl.ds(j, rl, stride=gc), :] = cols[a, c, at : at + rl, :].astype(F32)
                cols[a, c, rows, :] = s["stage"][a].astype(BF)

    soon = early_blocks(light, heavy, half, gc) if direct else []

    gsend = s["gsend"]
    for k, (name, at) in enumerate((("dwqg_acc", 0), ("dwkv_acc", 0), ("dwkv_acc", 1), ("dwqg_acc", 1))):
        gsend[k] = jnp.transpose(s[name][at * width : (at + 1) * width, :]).astype(gsend.dtype)
    gsend[4] = s["dw4_acc"][...].astype(gsend.dtype)
    spot = lax.broadcasted_iota(jnp.int32, (1, width), 1)
    dbias = jnp.zeros((1, width), F32)
    for h in range(heads):
        total_h = jnp.sum(jnp.sum(s["db_acc"][h], 0, keepdims=True), 1, keepdims=True)
        dbias = jnp.where(spot == h, total_h * (1.0 / scale), dbias)
    for k in range(5, slots * ncol):
        gsend[k] = jnp.zeros((width, width), gsend.dtype)
    exchange_col(lambda p: gsend.at[pl.ds(p * slots, slots)], s["grecv"], 2)

    def last_turn(t, _):
        at_turn(t, finish)
        return 0

    lax.fori_loop(heavy - LAG, heavy, last_turn, 0)
    s["vsend"][0, 0:1, :] = s["dg_acc"][0:1]
    s["vsend"][0, 1:2, :] = dbias
    exchange_row(lambda p: s["vsend"].at[0], s["vrow"], 6)
    landed(s["grecv"], 2)
    share = total_of(s["grecv"], ncol)
    for p in range(nrow):
        s["ssend"][p] = share[:, p * wr : (p + 1) * wr, :].astype(s["ssend"].dtype)
    exchange_row(lambda p: s["ssend"].at[p], s["srecv"], 3)
    for b in soon[0::3]:
        turn_back(b)
    landed(s["vrow"], 6)
    s["vsend"][1] = total_of(s["vrow"], nrow)
    exchange_col(lambda p: s["vsend"].at[1], s["vcol"], 7)
    landed(s["srecv"], 3)
    s["csend"][...] = total_of(s["srecv"], nrow)
    exchange_col(lambda p: s["csend"], s["crecv"], 4)
    for b in soon[1::3]:
        turn_back(b)
    landed(s["crecv"], 4)
    landed(s["vcol"], 7)
    for j in range(wr):
        red_ref[:, j * width : (j + 1) * width] = s["crecv"][:, :, j, :].reshape(slots * ncol, width)
    red_ref[5:7, 0:width] = total_of(s["vcol"], ncol)
    wval = w_ref[...]
    step_w = moments(wval, red_ref[0:5, :], m1_ref[...], m2_ref[...])[2]
    row5 = lax.broadcasted_iota(jnp.int32, (5, 1), 0)
    squares = jnp.where(spot == row5, jnp.sum(wval * wval, 1, keepdims=True), 0.0)
    squares += jnp.where(spot == row5 + 8, jnp.sum(step_w * step_w, 1, keepdims=True), 0.0)
    s["nsend"][...] = jnp.sum(squares, 0, keepdims=True)
    exchange_row(lambda p: s["nsend"], s["nrecv"], 5)
    for b in soon[2::3]:
        turn_back(b)
    landed(s["nrecv"], 5)
    nrm_ref[...] = total_of(s["nrecv"], nrow)

    for b in range(nblocks):
        if b not in soon:
            block = cols.at[:, :, pl.ds(b * gc * rl, gc * rl)]
            pltpu.make_async_copy(block, block, ret_sem.at[b]).wait()

    def ended(count):
        sent = s["sbuf"] if direct else pair_ref
        sent = sent.at[pl.ds(0, half // 2 * (light + heavy) - count)]
        pltpu.make_async_copy(sent, sent, send_sem.at[0]).wait()
        gone = zin.at[pl.ds(0, count), :, :, pl.ds(0, half - 1)]
        pltpu.make_async_copy(gone, gone, rsend_sem.at[0]).wait()
        for at_side, rows_y, rows_d in ((0, 2 * qn, qn), (1, qn, 2 * qn)):

            @pl.when(side == at_side)
            def _():
                part = y3.at[pl.ds(0, count), pl.ds(0, rows_y)]
                pltpu.make_async_copy(part, part, x_send.at[0]).wait()
                part = d3.at[pl.ds(0, count), pl.ds(0, rows_d)]
                pltpu.make_async_copy(part, part, x_send.at[1]).wait()

    for kind, count in ((False, light), (True, heavy)):

        @pl.when(is_heavy == kind)
        def _():
            ended(count)

    for n, name in enumerate(
        ("wrow", "wall", "grecv", "srecv", "crecv", "nrecv", "vrow", "vcol")
    ):
        sent = s[name].at[pl.ds(0, s[name].shape[0] - 1)]
        pltpu.make_async_copy(sent, sent, misc_send.at[n]).wait()


def step_kernel(direct, soon, *refs):
    if direct:
        cols, blocks, refs = refs[0], refs[1], refs[2:]
    red_ref, nrm_ref, w_ref, m1_ref, m2_ref, gain_ref, gm_ref, gv_ref, bias_ref, bm_ref, bv_ref = refs[:11]
    refs = refs[11:]
    if direct:
        bigs, refs = refs[0:2], refs[2:11] + refs[11:]
        refs, (slot, stage, sem) = refs[:9], refs[9:]
        _, crops, _, width = cols.shape
        _, rl, cl, _ = bigs[0].shape
        gc = 16
        copies = []

        def put(src, a, c, b):
            n = len(copies)
            copy = pltpu.make_async_copy(src, bigs[a].at[c, :, pl.ds(b * gc, gc), :], sem.at[n])
            copy.start()
            copies.append(copy)

        for b in soon:
            for c in range(crops):
                for a in range(2):
                    put(blocks.at[a, c, b], a, c, b)
        late = [b for b in range(cl // gc) if b not in soon]
        for n, b in enumerate(late):
            for c in range(crops):
                for a in range(2):
                    for j in range(gc):
                        at = (b * gc + j) * rl
                        stage[a, pl.ds(j, rl, stride=gc), :] = cols[a, c, at : at + rl, :].astype(F32)
                    slot[n, c, a] = stage[a].reshape(rl, gc, width).astype(BF)
                    put(slot.at[n, c, a], a, c, b)
    nw_ref, n1_ref, n2_ref, ng_ref, ngm_ref, ngv_ref, nb_ref, nbm_ref, nbv_ref = refs
    width = gain_ref.shape[1]
    heads = bias_ref.shape[1]
    wval = w_ref[...]
    first, second, step_w = moments(wval, red_ref[0:5, :], m1_ref[...], m2_ref[...])
    spot = lax.broadcasted_iota(jnp.int32, (1, width), 1)
    place = lax.broadcasted_iota(jnp.int32, (5, 1), 0)
    value_sq = jnp.sum(jnp.where(spot == place, nrm_ref[...], 0.0), 1, keepdims=True)
    step_sq = jnp.sum(jnp.where(spot == place + 8, nrm_ref[...], 0.0), 1, keepdims=True)
    nw_ref[...] = wval - rate * (jnp.sqrt(value_sq) / jnp.sqrt(step_sq)) * step_w
    n1_ref[...] = first
    n2_ref[...] = second
    for row, n, own in (
        (5, width, (gain_ref, gm_ref, gv_ref, ng_ref, ngm_ref, ngv_ref)),
        (6, heads, (bias_ref, bm_ref, bv_ref, nb_ref, nbm_ref, nbv_ref)),
    ):
        val = own[0][...]
        first, second, step_v = moments(val, red_ref[row : row + 1, 0:n], own[1][...], own[2][...])
        ratio = jnp.sqrt(jnp.sum(val * val, 1, keepdims=True)) / jnp.sqrt(
            jnp.sum(step_v * step_v, 1, keepdims=True)
        )
        own[3][...] = val - rate * ratio * step_v
        own[4][...] = first
        own[5][...] = second
    if direct:
        for copy in copies:
            copy.wait()


def body(
    nrow,
    ncol,
    pair,
    cotangent,
    segments,
    lengths,
    weights,
    moment_one,
    moment_two,
    gain,
    gain_m,
    gain_v,
    chain_bias,
    bias_m,
    bias_v,
):
    crops, rl, cl, width = pair.shape
    heads = chain_bias.shape[0]
    half = nrow // 2
    qn = half * rl
    wr = weights.shape[1] // width
    slots = -(-8 // ncol)
    direct = cl % 16 == 0 and rl % 16 == 0
    pairs = cl // (half // 2)
    light = LIGHT if direct and pairs == 64 else pairs // 2
    heavy = pairs - light
    dims = (nrow, ncol, crops, light, heavy, rl, width, heads, wr, direct)
    wtype = BF if wr % 16 == 0 else F32
    ring = AHEAD + LAG + 1
    hbm = pl.BlockSpec(memory_space=pl.ANY)
    vmem = pl.BlockSpec(memory_space=pltpu.VMEM)
    smem = pl.BlockSpec(memory_space=pltpu.SMEM)
    dma = pltpu.SemaphoreType.DMA
    outs = {
        "red": pltpu.VMEM((slots * ncol, wr * width), F32),
        "nrm": pltpu.VMEM((1, width), F32),
        "cols": pltpu.VMEM((2, crops, cl * rl, width), BF),
    }
    scratch = {
        "zin": pltpu.VMEM((heavy, crops, 2, half, rl, width), BF),
        "y3": pltpu.VMEM((heavy, 3 * qn, width), BF),
        "d3": pltpu.VMEM((heavy, 3 * qn, width), BF),
        "own": pltpu.VMEM((ring, 3 * qn, width), F32),
        "xring": pltpu.VMEM((ring, 2 * qn, width), F32),
        "iring": pltpu.VMEM((ring, 2 * qn, width), F32),
        "yring": pltpu.VMEM((ring, 2 * qn, width), BF),
        "rev": pltpu.VMEM((qn, qn), BF),
        "wtmp": pltpu.VMEM((8, wr, width), F32),
        "wsend": pltpu.VMEM((slots * ncol, wr, width), wtype),
        "wrow": pltpu.VMEM((nrow, slots, wr, width), wtype),
        "wall": pltpu.VMEM((ncol, nrow, slots, wr, width), wtype),
        "gsend": pltpu.VMEM((slots * ncol, width, width), wtype),
        "grecv": pltpu.VMEM((ncol, slots, width, width), wtype),
        "ssend": pltpu.VMEM((nrow, slots, wr, width), wtype),
        "srecv": pltpu.VMEM((nrow, slots, wr, width), wtype),
        "csend": pltpu.VMEM((slots, wr, width), F32),
        "crecv": pltpu.VMEM((ncol, slots, wr, width), F32),
        "vsend": pltpu.VMEM((2, 2, width), F32),
        "vrow": pltpu.VMEM((nrow, 2, width), F32),
        "vcol": pltpu.VMEM((ncol, 2, width), F32),
        "nsend": pltpu.VMEM((1, width), F32),
        "nrecv": pltpu.VMEM((nrow, 1, width), F32),
        "wqg": pltpu.VMEM((width, 2 * width), BF),
        "wkv": pltpu.VMEM((width, 2 * width), BF),
        "wqg_t": pltpu.VMEM((2 * width, width), BF),
        "wkv_t": pltpu.VMEM((2 * width, width), BF),
        "w4": pltpu.VMEM((width, width), BF),
        "augk": pltpu.VMEM((crops, 2 * qn, width), BF),
        "augq": pltpu.VMEM((crops, heads, width, qn), BF),
        "hotk": pltpu.VMEM((crops, 16, 2 * qn), BF),
        "hotq": pltpu.VMEM((crops, 16, qn), BF),
        "dwqg_acc": pltpu.VMEM((2 * width, width), F32),
        "dwkv_acc": pltpu.VMEM((2 * width, width), F32),
        "dw4_acc": pltpu.VMEM((width, width), F32),
        "dg_acc": pltpu.VMEM((8, width), F32),
        "db_acc": pltpu.VMEM((heads, 8, qn), F32),
        "in_sem": dma((heavy,)),
        "y_sem": dma((heavy,)),
        "d_sem": dma((heavy,)),
        "send_sem": dma((1,)),
        "ret_sem": dma((cl // 16 if direct else 1,)),
        "rsend_sem": dma((1,)),
        "x_send": dma((2,)),
        "misc_recv": dma((8,)),
        "misc_send": dma((8,)),
    }
    if direct:
        sources = (pair, cotangent)
        scratch["raw"] = pltpu.VMEM((3, crops, 2, rl, 16, width), BF)
        scratch["sbuf"] = pltpu.VMEM((cl, crops, 2, rl, width), BF)
        scratch["stage"] = pltpu.VMEM((2, rl * 16, width), F32)
        scratch["raw_sem"] = dma((3, crops, 2))
    else:
        sources = (jnp.transpose(jnp.stack([pair, cotangent], 1), (3, 0, 1, 2, 4)), cotangent)
    names = tuple(outs) + tuple(scratch)
    res1 = pl.pallas_call(
        functools.partial(main_kernel, dims, names),
        out_shape=tuple(outs.values()),
        in_specs=[hbm, hbm, vmem, smem, vmem, vmem, vmem, vmem, smem],
        out_specs=(vmem,) * len(outs),
        scratch_shapes=list(scratch.values()),
        compiler_params=pltpu.CompilerParams(
            collective_id=0, has_side_effects=True, vmem_limit_bytes=55 << 20
        ),
        name="column_attention",
    )(
        *(
            pltpu.with_memory_space_constraint(x, pltpu.HBM)
            for x in (
                *sources,
                segments,
                lengths,
                weights,
                moment_one,
                moment_two,
                gain.reshape(1, width),
                chain_bias,
            )
        )
    )
    res1 = dict(zip(outs, res1))
    small = (gain, gain_m, gain_v, chain_bias, bias_m, bias_v)
    ops = [res1["red"], res1["nrm"], weights, moment_one, moment_two] + [a.reshape(1, -1) for a in small]
    fin = jax.ShapeDtypeStruct(pair.shape, BF)
    bigs = [fin, fin] if direct else []
    count = 2 * crops * (cl // 16)
    soon = early_blocks(light, heavy, half, 16) if direct else []
    turned = ()
    if direct:
        turned = (res1["cols"], res1["cols"].reshape(2, crops, cl // 16, rl, 16, width))
    res = pl.pallas_call(
        functools.partial(step_kernel, direct, soon),
        out_shape=bigs
        + [jax.ShapeDtypeStruct(weights.shape, F32)] * 3
        + [jax.ShapeDtypeStruct((1, width), F32)] * 3
        + [jax.ShapeDtypeStruct((1, heads), F32)] * 3,
        in_specs=[vmem] * (len(ops) + len(turned)),
        out_specs=[hbm] * len(bigs) + [vmem] * 9,
        scratch_shapes=[
            pltpu.VMEM((cl // 16 - len(soon), crops, 2, rl, 16, width), BF),
            pltpu.VMEM((2, rl * 16, width), F32),
            dma((count,)),
        ]
        if direct
        else [],
        compiler_params=pltpu.CompilerParams(vmem_limit_bytes=18 << 20),
        name="lamb_step",
    )(*turned, *ops)
    if direct:
        fins, res = res[:2], res[2:]
    else:
        fins = [jnp.swapaxes(res1["cols"][a].reshape(crops, cl, rl, width), 1, 2) for a in range(2)]
    return (*fins, *res[:3], *[a.reshape(-1) for a in res[3:]])


def solution(mesh):
    big = P(None, "row", "col", None)
    shard = P(None, "row")
    return jax.shard_map(
        functools.partial(body, mesh.shape["row"], mesh.shape["col"]),
        mesh=mesh,
        in_specs=(big, big, P(), P(), shard, shard, shard) + (P(),) * 6,
        out_specs=(big, big, shard, shard, shard) + (P(),) * 6,
        check_vma=False,
    )
```
